32 devices in a mesh: row: 4 (over z), col: 4 (over y, x), ch: 2 (over core).
Axes of the slice: x: 2, y: 2, z: 4, core: 2. Of those that a mesh axis runs over, the one named last changes fastest.
Arguments:
- field: float32 [32, 512, 2048], P(None, 'row', 'col'), may hold values from -6 to 6
- spec_weight: float32 [2, 32, 32, 512], replicated, may hold values from -0.75 to 0.75
- point_weight: float32 [32, 32], replicated, may hold values from -1 to 1
- bias: float32 [32], P('ch'), may hold values from -1 to 1
- kept_modes: int32 [32], replicated, may hold values from 8 to 16, as said below
- residual: float32 [32, 16384], P('ch', ('row', 'col')), may hold values from -6 to 6
- trace_dest: int32 [16384, 1], P(('row', 'col')), may hold values from 0 to 15; in each aligned block of 1024 rows (0 to 1023, 1024 to 2047, ...) at most 128 rows name the same one
- trace_cell: int32 [16384], P(('row', 'col')), may hold values from 0 to 65535
Outputs:
- grad_field: float32 [32, 512, 2048], P('ch', 'row', 'col')
- grad_spec: float32 [2, 32, 32, 512], P(None, None, 'ch')
- grad_point: float32 [32, 32], P(None, 'ch')
- grad_bias: float32 [32], P('ch')
The draws below stay inside these ranges and needn't reach their ends.
Inputs may be any that keep to these rules, and one draw needn't show every extreme that they name: `trace_dest`: of the 1024 points of one device, at most 128 go to one tile. `kept_modes`: some channel keeps 16 and some keeps 16 // 2.
All inputs are finite; a program needn't handle non-finite values.
Results may differ from the reference program's by a relative error of at most 0.00012.
Values sent between devices are 32-bit elements; how exact they have to be, the bound alone decides.
A program may use at most 192 MiB of HBM per device.

```python
import math
import jax
import jax.numpy as jnp
import numpy as np
from jax import lax

C = 32
M = 16
RD = 128
CD = 512
P_DEV = 1024
NR = 512
NC = 2048
TILES = 16
NPTS = 16384
MODES = 512
CAP = 128
N_COL = 4


def draw_kept_modes(key, part):
    values = jax.random.randint(key, (C,), M // 2, M + 1)
    first_spot = jax.random.randint(jax.random.fold_in(key, 11), (), 0, C)
    shift_by = jax.random.randint(jax.random.fold_in(key, 13), (), 1, C)
    second_spot = (first_spot + shift_by) % C
    places = jnp.arange(C)
    values = jnp.where(places == first_spot, M, values)
    values = jnp.where(places == second_spot, M // 2, values)
    return values.astype(jnp.int32)


def set_ends(drawn, stream_key, low, top_value):
    place = [jax.random.randint(jax.random.fold_in(stream_key, axis), (), 0, length) for axis, length in enumerate(drawn.shape)]
    main_axis = drawn.shape.index(max(drawn.shape))
    next_to = place[:main_axis] + [(place[main_axis] + 1) % drawn.shape[main_axis]] + place[main_axis + 1:]
    return drawn.at[tuple(place)].set(low).at[tuple(next_to)].set(top_value)


def shard_levels(stream_key, shape, pieces, least, top_value):
    level = 1.0
    for position, blocks in pieces:
        heights = jax.random.uniform(jax.random.fold_in(jax.random.fold_in(stream_key, 6), position), (blocks,), jnp.float32, least / len(pieces), top_value / len(pieces))
        level = level * jnp.repeat(jnp.exp(heights), shape[position] // blocks).reshape((-1,) + (1,) * (len(shape) - 1 - position))
    return level


def assign_block(stream_key, own, number, rows, count, top, bound, skew):
    sequence = jax.random.permutation(stream_key, count)
    packed, usual = portions_of(count, rows * top, bound, skew, True), portions_of(count, rows * top, bound, skew, False)
    places = jnp.arange(count)

    def named(tallies, turn):
        used = int((tallies > 0).sum())
        fixed = max(1, used // 4)
        shifted = fixed + (places - fixed + turn * (used - fixed)) % max(1, count - fixed)
        return jnp.zeros((count,), jnp.int32).at[sequence[jnp.where(places < fixed, places, shifted)]].set(jnp.asarray(tallies, jnp.int32))

    tallies = jnp.where(number % 4 == 0, named(packed, number // 4), named(usual, number - number // 4 - 1))
    mixed = jax.random.permutation(jax.random.fold_in(own, 3), count)
    giver, taker = mixed[0:count // 2 * 2:2], mixed[1:count // 2 * 2:2]
    room = jnp.minimum(tallies[giver] - 1, bound - tallies[taker]) // 2
    room = jnp.where((giver == sequence[0]) | (taker == sequence[0]) | (tallies[taker] == 0), 0, jnp.maximum(room, 0))
    shifted = jax.random.randint(jax.random.fold_in(own, 4), (count // 2,), 0, 1 << 20) % (room + 1)
    tallies = tallies.at[giver].add(-shifted).at[taker].add(shifted)
    labels = jnp.searchsorted(jnp.cumsum(tallies), jnp.arange(rows * top), side="right").astype(jnp.int32)
    table = labels.reshape(top, rows).T
    table = table[jax.random.permutation(jax.random.fold_in(own, 1), rows)]
    turn = jax.random.randint(jax.random.fold_in(own, 2), (rows, 1), 0, top)
    return jnp.take_along_axis(table, (jnp.arange(top)[None, :] + turn) % top, axis=1)


def portions_of(amount, total, bound, skew, full):
    portions = [(1 << 20) // math.isqrt(rank ** skew) + 1 for rank in range(1, amount + 1)]
    largest = bound if full else min(bound, max(-(-total // amount), total * portions[0] // sum(portions)))
    least = 1 if total - largest >= amount - 1 else 0
    given, spare = [largest] + [least] * (amount - 1), total - largest - least * (amount - 1)
    while spare > 0:
        free = [i for i in range(1, amount) if given[i] < largest] or [i for i in range(1, amount) if given[i] < bound]
        pool, budget = sum([portions[i] for i in free]), spare
        for i in free:
            more = min(bound - given[i], max(1, budget * portions[i] // pool), spare)
            given[i] = given[i] + more
            spare = spare - more
    return np.array(given)


def scatter_about(rng, dims, spread, limit, split=(), kind=jnp.bfloat16):
    values = spread * jax.random.normal(rng, dims, jnp.float32)
    if split:
        values = values * shard_levels(rng, dims, split, -0.22, 0.18)
    return jnp.clip(values, -limit, limit).astype(kind)


def setup_inputs(seed: int = 0) -> dict:
    splits = jax.random.split(jax.random.key(seed), 9)
    field = scatter_about(splits[0], (C, NR, NC), 1.0, 6.0, ((1, 4), (2, 4)), jnp.float32)
    spec_weight = scatter_about(splits[1], (2, C, C, MODES), (2 * C) ** -0.5, 0.75, (), jnp.float32)
    point_weight = scatter_about(splits[2], (C, C), C ** -0.5, 1.0, (), jnp.float32)
    bias = jnp.clip(jax.random.uniform(splits[3], (C,), jnp.float32, -1.0, 1.0) * shard_levels(splits[3], (C,), ((0, 2),), -0.4, 0.0), -1.0, 1.0)
    kept_modes = draw_kept_modes(jax.random.fold_in(splits[8], 71), 0)
    residual = scatter_about(splits[5], (C, NPTS), 1.0, 6.0, ((0, 2), (1, 16)), jnp.float32)
    trace_dest_keys = jax.random.split(jax.random.fold_in(splits[6], 1), NPTS // P_DEV)
    trace_dest_turns = jax.random.permutation(jax.random.fold_in(splits[6], 3), NPTS // P_DEV)
    trace_dest = jax.vmap(lambda own, number: assign_block(jax.random.fold_in(splits[6], 2), own, number, P_DEV, TILES, 1, CAP, 2))(trace_dest_keys, trace_dest_turns).reshape((NPTS, 1))
    trace_cell = set_ends(jax.random.randint(splits[7], (NPTS,), 0, RD * CD), jax.random.fold_in(splits[7], 1), 0, (RD * CD) - 1).astype(jnp.int32)
    return dict(field=field, spec_weight=spec_weight, point_weight=point_weight, bias=bias, kept_modes=kept_modes, residual=residual, trace_dest=trace_dest, trace_cell=trace_cell)


full_turn = 6.283185307179586
exact_mode = lax.Precision.HIGHEST

def row_angles(start_at, extent, period):
    frequency = jnp.arange(2 * M, dtype=jnp.int32)
    frequency = jnp.where(frequency < M, frequency, frequency - 2 * M)
    places = start_at + jnp.arange(extent, dtype=jnp.int32)
    phases = frequency[:, None] * places[None, :] % period
    angles = phases.astype(jnp.float32) * (full_turn / period)
    return (jnp.cos(angles), jnp.sin(angles))

def col_angles(start_at, extent, period):
    frequency = jnp.arange(M, dtype=jnp.int32)
    places = start_at + jnp.arange(extent, dtype=jnp.int32)
    phases = places[:, None] * frequency[None, :] % period
    angles = phases.astype(jnp.float32) * (full_turn / period)
    return (jnp.cos(angles), jnp.sin(angles))

def mode_mask(kept_modes):
    indices = jnp.arange(MODES, dtype=jnp.int32)
    row_mode = indices // M
    col_mode = indices % M
    row_rank = jnp.where(row_mode < M, row_mode, 2 * M - 1 - row_mode)
    allowed = (row_rank[None, :] < kept_modes[:, None]) & (col_mode[None, :] < kept_modes[:, None])
    return allowed.astype(jnp.float32)

def full_modes(values, scale_by):
    cos_rows, sin_rows = row_angles(0, NR, NR)
    real_rows = jnp.einsum('ar,crs->cas', cos_rows, values, precision=exact_mode)
    imag_rows = -jnp.einsum('ar,crs->cas', sin_rows, values, precision=exact_mode)
    cos_cols, sin_cols = col_angles(0, NC, NC)
    mode_re = jnp.einsum('cas,sb->cab', real_rows, cos_cols, precision=exact_mode) + jnp.einsum('cas,sb->cab', imag_rows, sin_cols, precision=exact_mode)
    mode_im = jnp.einsum('cas,sb->cab', imag_rows, cos_cols, precision=exact_mode) - jnp.einsum('cas,sb->cab', real_rows, sin_cols, precision=exact_mode)
    count = values.shape[0]
    return (mode_re.reshape(count, MODES) * scale_by, mode_im.reshape(count, MODES) * scale_by)

def full_field(mode_re, mode_im, scale_by):
    count = mode_re.shape[0]
    grid_re = mode_re.reshape(count, 2 * M, M)
    grid_im = mode_im.reshape(count, 2 * M, M)
    cos_cols, sin_cols = col_angles(0, NC, NC)
    half_re = jnp.einsum('cab,sb->cas', grid_re, cos_cols, precision=exact_mode) - jnp.einsum('cab,sb->cas', grid_im, sin_cols, precision=exact_mode)
    half_im = jnp.einsum('cab,sb->cas', grid_re, sin_cols, precision=exact_mode) + jnp.einsum('cab,sb->cas', grid_im, cos_cols, precision=exact_mode)
    cos_rows, sin_rows = row_angles(0, NR, NR)
    result = jnp.einsum('ar,cas->crs', cos_rows, half_re, precision=exact_mode) - jnp.einsum('ar,cas->crs', sin_rows, half_im, precision=exact_mode)
    return result * scale_by

def reference(field, spec_weight, point_weight, bias, kept_modes, residual, trace_dest, trace_cell):
    forward_scale = 1.0 / math.sqrt(NR * NC)
    mix_scale = 1.0 / math.sqrt(MODES)
    spec_re, spec_im = full_modes(field, forward_scale)
    allowed = mode_mask(kept_modes)
    weight_re = spec_weight[0] * allowed[None, :, :]
    weight_im = spec_weight[1] * allowed[None, :, :]
    mixed_re = lax.optimization_barrier(jnp.sum(weight_re * spec_re[:, None, :] - weight_im * spec_im[:, None, :], axis=0))
    mixed_im = lax.optimization_barrier(jnp.sum(weight_re * spec_im[:, None, :] + weight_im * spec_re[:, None, :], axis=0))
    pre_act = full_field(mixed_re, mixed_im, mix_scale) + jnp.einsum('co,crs->ors', point_weight, field, precision=exact_mode) + bias[:, None, None]
    targets = trace_dest[:, 0]
    rows_at = targets // N_COL * RD + trace_cell // CD
    cols_at = targets % N_COL * CD + trace_cell % CD
    flat_cells = (rows_at * NC + cols_at).astype(jnp.int32)
    cotangent = jnp.zeros((C, NR * NC), jnp.float32).at[:, flat_cells].add(residual).reshape(C, NR, NC)
    slope = jax.vjp(jax.nn.gelu, pre_act)[1](cotangent)[0]
    grad_re, grad_im = full_modes(slope, mix_scale)
    grad_scale = math.sqrt(MODES / NPTS)
    spec_grad_re = allowed[None] * (grad_re[None] * spec_re[:, None] + grad_im[None] * spec_im[:, None]) * grad_scale
    spec_grad_im = allowed[None] * (grad_im[None] * spec_re[:, None] - grad_re[None] * spec_im[:, None]) * grad_scale
    grad_spec = jnp.stack((spec_grad_re, spec_grad_im), axis=0)
    adjoint_re = lax.optimization_barrier(jnp.sum(weight_re * grad_re[None] + weight_im * grad_im[None], axis=1))
    adjoint_im = lax.optimization_barrier(jnp.sum(weight_re * grad_im[None] - weight_im * grad_re[None], axis=1))
    grad_field = jnp.einsum('co,ors->crs', point_weight, slope, precision=exact_mode) + full_field(adjoint_re, adjoint_im, forward_scale)
    norm_points = 1.0 / math.sqrt(NPTS)
    grad_point = jnp.einsum('crs,ors->co', field, slope, precision=exact_mode) * norm_points
    grad_bias = lax.optimization_barrier(jnp.sum(slope, axis=(1, 2))) * norm_points
    return (grad_field, grad_spec, grad_point, grad_bias)
```

```python
import functools
import math

import jax
import jax.numpy as jnp
import ml_dtypes
import numpy as np
from jax import lax
from jax.experimental import pallas as pl
from jax.experimental.pallas import tpu as pltpu
from jax.sharding import PartitionSpec as P

M = 16
A = 2 * M
MODES = A * M
RB = 8
FOLD = 32
F32 = jnp.float32
BF16 = jnp.bfloat16
FULL_TURN = 6.283185307179586
NN = (((1,), (0,)), ((), ()))
NT = (((1,), (1,)), ((), ()))
MIB = 1 << 20
MESH = pl.DeviceIdType.MESH


def trig(frequency, period):
    phases = frequency[:, None] * np.arange(period)[None, :] % period
    angles = phases.astype(np.float32) * np.float32(FULL_TURN / period)
    angles = angles.astype(np.float64)
    return np.cos(angles).astype(np.float32), np.sin(angles).astype(np.float32)


def np_split(x):
    hi = x.astype(ml_dtypes.bfloat16)
    return hi, (x - hi.astype(np.float32)).astype(ml_dtypes.bfloat16)


@functools.lru_cache(maxsize=None)
def tables(n_rows, n_cols):
    frequency = np.arange(A)
    frequency = np.where(frequency < M, frequency, frequency - A)
    rows = np.concatenate(trig(frequency, n_rows), axis=0)
    cos, sin = trig(np.arange(M), n_cols)
    hi, low = np_split(rows)
    rows2 = np.concatenate((hi, low), axis=0)
    rows3 = np.concatenate((hi.T, low.T, hi.T), axis=1)
    hi, low = np_split(np.concatenate((cos, sin), axis=0))
    cols2 = np.concatenate((hi.T, low.T), axis=1)
    hi, low = np_split(np.concatenate((cos, -sin), axis=0))
    wide3 = np.concatenate((hi, hi, low), axis=0)
    return rows2, rows3, cols2, wide3


def split2(x):
    hi = x.astype(BF16)
    return hi, (x - hi.astype(F32)).astype(BF16)


def mm(a, b, dims=NN):
    return lax.dot_general(a, b, dims, preferred_element_type=F32)


def stacked(x, axis):
    hi, low = split2(x)
    return jnp.concatenate((hi.astype(F32), low.astype(F32)), axis=axis).astype(BF16)


def deep_left(x):
    hi = x.astype(BF16).astype(F32)
    return jnp.concatenate((hi, x - hi, hi), axis=1)


def deep_right(x):
    hi = x.astype(BF16).astype(F32)
    return jnp.concatenate((hi, hi, x - hi), axis=0).astype(BF16)


def exact(a, b, dims=NN):
    return lax.dot_general(
        a, b, dims, precision=lax.Precision.HIGHEST, preferred_element_type=F32
    )


def iota(shape, axis):
    return lax.broadcasted_iota(jnp.int32, shape, axis)


def sel(mask):
    return mask.astype(F32)


def pack(dest, vals, out_ref, tiles, cap):
    n = dest.shape[1]
    named = dest == iota((tiles, n), 0)
    before = iota((n, n), 0) < iota((n, n), 1)
    earlier = mm(sel(named).astype(BF16), sel(before).astype(BF16))
    rank = jnp.sum(jnp.where(named, earlier, 0.0), axis=0, keepdims=True)
    position = dest * cap + rank.astype(jnp.int32)
    rows = vals.shape[0]
    hi = vals.astype(BF16)
    left = vals - hi.astype(F32)
    mid = left.astype(BF16)
    low = (left - mid.astype(F32)).astype(BF16)
    parts = jnp.concatenate((hi.astype(F32), mid.astype(F32), low.astype(F32)), axis=0).astype(BF16)
    step = 512
    for first in range(0, tiles * cap, step):
        place = sel(position == iota((step, n), 0) + first).astype(BF16)
        got = mm(parts, place, NT)
        got = got[:rows] + got[rows : 2 * rows] + got[2 * rows : 3 * rows]
        for at in range(0, step, cap):
            out_ref[(first + at) // cap] = got[:, at : at + cap]


def mode_lines(rows2, tall, scale):
    side = tall.shape[1] // 2
    both = mm(rows2, stacked(tall, 1))
    grid = both[: 2 * A, : 2 * side] + both[2 * A :, : 2 * side] + both[: 2 * A, 2 * side :]
    re = (grid[:A, :side] - grid[A:, side:]) * scale
    im = (grid[A:, :side] + grid[:A, side:]) * (-scale)
    return [part[:, at : at + 128] for part in (re, im) for at in range(0, side, 128)]


def as_column(line, first=0, count=None):
    width = line.shape[1]
    shape = (count or width, width)
    picked = jnp.where(iota(shape, 1) == iota(shape, 0) + first, line.astype(F32), 0.0)
    return jnp.sum(picked, axis=1, keepdims=True).astype(jnp.int32)


def same_place():
    return sel(iota((128, 128), 0) % M == iota((128, 128), 1) % M)


def spread8(s8):
    z = jnp.broadcast_to(s8[:, None, :], (8, 8, 128)).reshape(64, 128)
    z = jnp.where(iota((64, 128), 1) // M == iota((64, 128), 0) % 8, z, 0.0)
    z = exact(z, same_place())
    re = jnp.concatenate((z[0:16], z[32:48]), axis=0)
    im = jnp.concatenate((z[16:32], z[48:64]), axis=0)
    return re, im


def compact8(re, im, a):
    y = jnp.concatenate((re, im), axis=0)
    group = iota(y.shape, 1) // M
    y = jnp.where(group == lax.rem(a, 8), y, 0.0)
    y = exact(y, same_place())
    y = jnp.where(group == iota(y.shape, 0) % 8, y, 0.0)
    return jnp.sum(y.reshape(8, 8, 128), axis=1)


def mode_half(re, im, rows3, half_ref):
    grid = jnp.concatenate(
        (jnp.concatenate((re, im), axis=1), jnp.concatenate((-im, re), axis=1)), axis=0
    )
    half = mm(rows3, deep_right(grid))
    side = half.shape[1] // 2
    for o in range(side // M):
        at = o * M
        pair = jnp.concatenate((half[:, at : at + M], half[:, side + at : side + at + M]), axis=1)
        half_ref[o] = deep_left(pair)


def put_tall(tall_ref, first, tall, own):
    for c in range(own):
        for part in range(2):
            at = (part * own + c) * M
            tall_ref[pl.ds(first, RB), at : at + M] = tall[
                c * RB : (c + 1) * RB, part * M : (part + 1) * M
            ]


def col_modes(parts, cols2):
    half = parts.shape[0] // 2
    got = mm(parts, cols2)
    return got[:half, : 2 * M] + got[:half, 2 * M :] + got[half:, : 2 * M]


def main_kernel(
    n_row, n_col, scales,
    dest_ref, cell_ref, res_ref, kept_ref, bias_ref, point_ref, field_ref, w_ref,
    rows2_hbm, rows3_hbm, cols2_hbm, wide3_hbm,
    partial_ref, spec_ref, back_ref, gp_ref,
    rows2_ref, rows3_ref, cols2_ref, wide3_ref, table_sem,
    fbuf, load_sem, wbuf, w_sem, f2_ref, pre_ref, kron2_ref, kronb_ref, tall_ref,
    x1, landed1, send1, gat1, x2, landed2, send2, gat2, rs_send, rs_recv, ag_send, ag_recv,
    grouped, came, trade_send, trade_recv, pts, ids_ref, vm_ref, hot_ref, cot_ref, half_ref,
    sl_ref, other_ref, swap_send, swap_recv, acc_ref, gpx, gpl, gp_send, gp_recv, out_sem,
):
    forward_scale, mix_scale = scales
    n = n_row * n_col
    count = 2 * n
    stride = count // A
    ch = lax.axis_index("ch")
    me = lax.axis_index("row") * n_col + lax.axis_index("col")
    flat = me * 2 + ch
    a = flat // stride
    is_reducer = lax.rem(flat, stride) == 0
    steps, inputs, block, width = fbuf.shape
    own = inputs // 2
    rows = own * RB
    height = steps * block
    subs = block // RB
    points = pts.shape[1]

    def device_of(f):
        p = f // 2
        return (p // n_col, lax.rem(p, n_col), lax.rem(f, 2))

    def remote(src, dst, send, recv, f):
        return pltpu.make_async_remote_copy(
            src_ref=src, dst_ref=dst, send_sem=send, recv_sem=recv,
            device_id=device_of(f), device_id_type=MESH,
        )

    def each(low, high, body):
        def go(k, carry):
            body(k)
            return carry

        lax.fori_loop(low, high, go, 0)

    def on_reducer(body):
        if stride == 1:
            body()
        else:
            pl.when(is_reducer)(body)

    def off_reducer(body):
        if stride > 1:
            pl.when(jnp.logical_not(is_reducer))(body)

    row_at = pl.multiple_of(lax.axis_index("row") * height, 128)
    col_at = pl.multiple_of(lax.axis_index("col") * width, 128)
    table_loads = [
        pltpu.make_async_copy(src, dst, table_sem.at[i])
        for i, (src, dst) in enumerate((
            (rows2_hbm.at[:, pl.ds(row_at, height)], rows2_ref),
            (rows3_hbm.at[pl.ds(row_at, height), :], rows3_ref),
            (cols2_hbm.at[pl.ds(col_at, width), :], cols2_ref),
            (wide3_hbm.at[:, pl.ds(col_at, width)], wide3_ref),
        ))
    ]

    def load(i):
        return pltpu.make_async_copy(
            field_ref.at[:, pl.ds(pl.multiple_of(i * block, block), block), :],
            fbuf.at[i], load_sem.at[i],
        )

    w_load = pltpu.make_async_copy(
        w_ref.at[:, :, :, pl.ds(pl.multiple_of(a // 8 * 128, 128), 128)], wbuf, w_sem
    )
    for one in table_loads:
        one.start()
    each(0, steps, lambda i: load(i).start())
    w_load.start()

    barrier = pltpu.get_barrier_semaphore()
    each(1, count, lambda k: pl.semaphore_signal(
        barrier, inc=1, device_id=device_of(lax.rem(flat + k, count)), device_id_type=MESH
    ))

    shape = (rows, inputs)
    pick = sel(iota(shape, 1) == ch * own + iota(shape, 0) // RB)
    wide_shape = (inputs, inputs * RB)
    spread = sel(iota(wide_shape, 0) == iota(wide_shape, 1) // RB)
    turned = sel(iota(wide_shape, 0) == (iota(wide_shape, 1) // RB + ch * own) % inputs)
    kron_shape = (rows, inputs * RB)
    same = iota(kron_shape, 0) % RB == iota(kron_shape, 1) % RB
    forward_point = exact(exact(pick, point_ref[...], NT), spread)
    kron2_ref[...] = stacked(jnp.where(same, forward_point, 0.0), 0)
    backward_point = exact(exact(pick, point_ref[...]), turned)
    kronb_ref[...] = stacked(jnp.where(same, backward_point, 0.0), 0)
    acc_ref[...] = jnp.zeros_like(acc_ref)
    for one in table_loads:
        one.wait()

    def front(i):
        load(i).wait()
        for u in range(subs):
            b = i * subs + u
            hi, low = split2(fbuf[i, :, u * RB : (u + 1) * RB, :].reshape(inputs * RB, width))
            f2_ref[b, : inputs * RB, :] = hi
            f2_ref[b, inputs * RB :, :] = low
            both = mm(kron2_ref[...], hi)
            pre_ref[b] = both[:rows] + both[rows:] + mm(kron2_ref[:rows, :], low)
            at = pl.multiple_of(ch * rows, rows)
            mine = jnp.concatenate(
                (f2_ref[b, pl.ds(at, rows), :], f2_ref[b, pl.ds(at + inputs * RB, rows), :]), axis=0
            )
            put_tall(tall_ref, pl.multiple_of(b * RB, RB), col_modes(mine, cols2_ref[...]), own)

    each(0, steps, front)

    def scatter(x, landed, stage):
        def copy(k):
            to = lax.rem(a + k, A)
            target = to * stride
            slot = lax.rem(flat - target + count, count)
            return remote(
                x.at[to], landed.at[slot], rs_send.at[stage, k], rs_recv.at[stage], target
            )

        return copy

    def scatter_start(x, landed, stage, scale):
        lines = mode_lines(rows2_ref[...], tall_ref[...], scale)
        for j, line in enumerate(lines):
            x[:, j, :] = line
        copy = scatter(x, landed, stage)
        if stage == 0:
            pl.semaphore_wait(barrier, count - 1)
        each(1, A, lambda k: copy(k).start())
        off_reducer(lambda: copy(0).start())

    def scatter_end(x, landed, stage):
        copy = scatter(x, landed, stage)
        each(1, A, lambda k: copy(k).wait_send())
        off_reducer(lambda: copy(0).wait_send())

    def reduced(x, landed, stage):
        got = landed.at[pl.ds(1, count - 1)]
        remote(got, got, rs_send.at[stage, 0], rs_recv.at[stage], flat).wait_recv()
        pairs = landed[pl.ds(2, count - 2)].reshape(n - 1, 2, 4, 128)
        pairs = jnp.sum(pairs, axis=0)
        mine = x[a] + pairs[0]
        theirs = landed[1] + pairs[1]
        first = jnp.where(ch == 0, mine, theirs)
        second = jnp.where(ch == 0, theirs, mine)
        return jnp.concatenate((first, second), axis=0)

    def gather(source, gat, stage):
        def copy(k):
            f = lax.rem(flat + k, count)
            return remote(
                source.at[lax.rem(ch + k, 2)], gat.at[a], ag_send.at[stage, k],
                ag_recv.at[stage], f,
            )

        return copy

    def gather_wait(gat, stage):
        def take(slots):
            got = gat.at[pl.ds(0, slots)]
            remote(got, got, ag_send.at[stage, 0], ag_recv.at[stage], flat).wait_recv()

        on_reducer(lambda: take(A - 1))
        off_reducer(lambda: take(A))

    def gather_end(source, gat, stage):
        copy = gather(source, gat, stage)
        on_reducer(lambda: each(1, count, lambda k: copy(k).wait_send()))

    rank = jnp.where(a < M, a, A - 1 - a)
    kept = as_column(kept_ref[...])
    allowed = sel((rank < kept) & (iota((inputs, 128), 1) % M < kept))

    scatter_start(x1, landed1, 0, forward_scale)

    cells = (cell_ref[...] + 1).astype(F32)
    vals = jnp.concatenate(
        (res_ref[...], jnp.broadcast_to(cells, (8, cells.shape[1]))), axis=0
    )
    cap = grouped.shape[2]
    pack(dest_ref[...], vals, grouped, n, cap)

    def trade(k):
        p = lax.rem(me + k, n)
        return remote(grouped.at[p], came.at[k], trade_send.at[k], trade_recv, p * 2 + ch)

    each(1, n, lambda k: trade(k).start())
    came[0] = grouped[me]

    def mix():
        s8 = reduced(x1, landed1, 0)
        spec_re, spec_im = spread8(s8)
        w_load.wait()
        re = jnp.zeros((inputs, 128), F32)
        im = jnp.zeros((inputs, 128), F32)
        for c in range(inputs):
            one_re, one_im = spec_re[c : c + 1], spec_im[c : c + 1]
            re = re + (wbuf[0, c] * one_re - wbuf[1, c] * one_im)
            im = im + (wbuf[0, c] * one_im + wbuf[1, c] * one_re)
        keep = allowed * mix_scale
        mixed = compact8(re * keep, im * keep, a)
        for d in range(2):
            send1[d, :8] = s8
            send1[d, 8:10] = mixed[2 * d : 2 * d + 2]
            send1[d, 10:12] = mixed[4 + 2 * d : 6 + 2 * d]
        copy = gather(send1, gat1, 0)
        each(1, count, lambda k: copy(k).start())
        gat1[a] = send1[ch]

    on_reducer(mix)
    if stride > 1:
        off_reducer(lambda: w_load.wait())

    came_all = came.at[pl.ds(1, n - 1)]
    remote(came_all, came_all, trade_send.at[0], trade_recv, flat).wait_recv()
    for p in range(n):
        pts[:, p * cap : (p + 1) * cap] = came[p]
    cell = pts[own : own + 1, :].astype(jnp.int32) - 1
    row = cell // width
    fold = jnp.where(cell < 0, -1, row % FOLD)
    code = jnp.where(cell < 0, -1, row // FOLD * width + cell % width).astype(F32)
    for first in range(0, points, 128):
        ids_ref[first : first + 128, :] = jnp.broadcast_to(
            code[:, first : first + 128], (128, 128)
        ).T
    here = fold == iota((FOLD, points), 0)
    half_own = own // 2

    def fill(o):
        value = pts[pl.ds(o, 1), :]
        hi = value.astype(BF16).astype(F32)
        group = o // half_own
        at = pl.multiple_of(lax.rem(o, half_own) * FOLD, FOLD)
        vm_ref[group, pl.ds(at, FOLD), :] = jnp.where(here, hi, 0.0).astype(BF16)
        vm_ref[group, pl.ds(at + half_own * FOLD, FOLD), :] = jnp.where(
            here, value - hi, 0.0
        ).astype(BF16)

    each(0, own, fill)
    span = half_own * FOLD

    def place(q):
        for at in range(0, width, 128):
            names = (iota((points, 128), 1) + (q * width + at)).astype(F32)
            hot_ref[:, at : at + 128] = sel(ids_ref[...] == names).astype(BF16)
        for group in range(2):
            got = mm(vm_ref[group], hot_ref[...])
            got = (got[:span] + got[span:]).reshape(half_own, FOLD, width)
            cot_ref[
                group * half_own : (group + 1) * half_own,
                pl.ds(pl.multiple_of(q * FOLD, FOLD), FOLD), :,
            ] = got

    each(0, height // FOLD, place)

    gather_wait(gat1, 0)
    re = jnp.concatenate((gat1[:, 8, :], gat1[:, 9, :]), axis=1)
    im = jnp.concatenate((gat1[:, 10, :], gat1[:, 11, :]), axis=1)
    bias_shape = (own, own * M)
    bias_at = sel(iota(bias_shape, 1) == iota(bias_shape, 0) * M)
    bias_line = exact(jnp.broadcast_to(bias_ref[...], (8, own)), bias_at)[:1]
    re = re + jnp.where(iota(re.shape, 0) == 0, bias_line, 0.0)
    mode_half(re, im, rows3_ref[...], half_ref)

    def swap(i):
        at = pl.ds(i * subs, subs)
        return remote(
            pre_ref.at[at], other_ref.at[at], swap_send.at[i], swap_recv.at[i], me * 2 + 1 - ch
        )

    k0 = math.sqrt(2.0 / math.pi)

    def slopes(i):
        for u in range(subs):
            b = i * subs + u
            first = pl.multiple_of(b * RB, RB)
            half = half_ref[:, pl.ds(first, RB), :].reshape(rows, 6 * M).astype(BF16)
            pre = pre_ref[b] + mm(half, wide3_ref[...])
            cot = cot_ref[:, pl.ds(first, RB), :].reshape(rows, width)
            square = pre * pre
            t = jnp.tanh(k0 * pre * (1.0 + 0.044715 * square))
            rate = 0.5 * (1.0 + t) + 0.5 * k0 * pre * (1.0 - t * t) * (1.0 + 3 * 0.044715 * square)
            slope = cot * rate
            pre_ref[b] = slope
            hi, low = split2(slope)
            sl_ref[b, :rows, :] = hi
            sl_ref[b, rows:, :] = low
            put_tall(tall_ref, first, col_modes(sl_ref[b], cols2_ref[...]), own)
        swap(i).start()

    each(0, steps, slopes)
    scatter_start(x2, landed2, 1, mix_scale)

    def point_sums(i):
        fields = jnp.concatenate([f2_ref[i * 2 + u] for u in range(2)], axis=1)
        found = jnp.concatenate([sl_ref[i * 2 + u] for u in range(2)], axis=1)
        acc_ref[...] += mm(fields, found, NT)

    each(0, steps * subs // 2, point_sums)
    total = acc_ref[: inputs * RB, :] + acc_ref[inputs * RB :, :]
    total = total[:, :rows] + total[:, rows:]
    matched = iota(total.shape, 0) % RB == iota(total.shape, 1) % RB
    total = jnp.sum(jnp.where(matched, total, 0.0).reshape(inputs, RB, rows), axis=1)
    into = 128 // own
    group = sel(iota((rows, 128), 0) // RB == iota((rows, 128), 1) % own)
    total = exact(total, group)
    mine = iota(total.shape, 1) // own == iota(total.shape, 0) % into
    gpx[...] = jnp.sum(jnp.where(mine, total, 0.0).reshape(inputs // into, into, 128), axis=1)

    def point_send(k):
        p = lax.rem(me + k, n)
        return remote(gpx, gpl.at[k], gp_send.at[k], gp_recv, p * 2 + ch)

    each(1, n, lambda k: point_send(k).start())

    def adjoint():
        s8 = reduced(x2, landed2, 1)
        grad_re, grad_im = spread8(s8)
        grad_re = grad_re * allowed
        grad_im = grad_im * allowed
        lines_re, lines_im = [], []
        for c in range(inputs):
            w_re, w_im = wbuf[0, c], wbuf[1, c]
            lines_re.append(jnp.sum(w_re * grad_re + w_im * grad_im, axis=0, keepdims=True))
            lines_im.append(jnp.sum(w_re * grad_im - w_im * grad_re, axis=0, keepdims=True))
        re = jnp.concatenate(lines_re, axis=0) * forward_scale
        im = jnp.concatenate(lines_im, axis=0) * forward_scale
        turned_modes = compact8(re, im, a)
        for d in range(2):
            send2[d, :2] = turned_modes[2 * d : 2 * d + 2]
            send2[d, 2:4] = turned_modes[4 + 2 * d : 6 + 2 * d]
            send2[d, 4:8] = s8[4 * d : 4 * d + 4]
        copy = gather(send2, gat2, 1)
        each(1, count, lambda k: copy(k).start())
        gat2[a] = send2[ch]

    on_reducer(adjoint)

    def store(i):
        at = pl.ds(pl.multiple_of(i * block, block), block)
        return pltpu.make_async_copy(cot_ref.at[:, at, :], partial_ref.at[:, at, :], out_sem.at[i])

    def backs(i):
        swap(i).wait_recv()
        for u in range(subs):
            b = i * subs + u
            first = pl.multiple_of(b * RB, RB)
            other_hi, other_low = split2(other_ref[b])
            hi = jnp.concatenate((sl_ref[b, :rows, :], other_hi), axis=0)
            low = jnp.concatenate((sl_ref[b, rows:, :], other_low), axis=0)
            both = mm(kronb_ref[...], hi)
            result = both[:rows] + both[rows:] + mm(kronb_ref[:rows, :], low)
            cot_ref[:, pl.ds(first, RB), :] = result.reshape(own, RB, width)
        store(i).start()

    each(0, steps, backs)

    gp_all = gpl.at[pl.ds(1, n - 1)]
    remote(gp_all, gp_all, gp_send.at[0], gp_recv, flat).wait_recv()
    gp_ref[...] = gpx[...] + jnp.sum(gpl[pl.ds(1, n - 1)], axis=0)
    gather_wait(gat2, 1)
    spec_ref[...] = gat1[...]
    back_ref[...] = gat2[...]

    scatter_end(x1, landed1, 0)
    scatter_end(x2, landed2, 1)
    gather_end(send1, gat1, 0)
    gather_end(send2, gat2, 1)
    each(1, n, lambda k: trade(k).wait_send())
    each(1, n, lambda k: point_send(k).wait_send())
    each(0, steps, lambda i: swap(i).wait_send())
    each(0, steps, lambda i: store(i).wait())


def main_pass(args, constants, scales, cap, n_row, n_col):
    field = args[6]
    n = n_row * n_col
    count = 2 * n
    inputs, height, width = field.shape
    own = inputs // 2
    block = 2 * RB
    steps = height // block
    blocks = height // RB
    rows = own * RB
    kept = own + 8
    points = n * cap
    vmem = pl.BlockSpec(memory_space=pltpu.VMEM)
    hbm = pl.BlockSpec(memory_space=pl.ANY)
    dma = pltpu.SemaphoreType.DMA
    rows2, rows3, cols2, wide3 = constants
    return pl.pallas_call(
        functools.partial(main_kernel, n_row, n_col, scales),
        out_shape=[
            jax.ShapeDtypeStruct((own, height, width), F32),
            jax.ShapeDtypeStruct((A, 12, 128), F32),
            jax.ShapeDtypeStruct((A, 8, 128), F32),
            jax.ShapeDtypeStruct((4, 128), F32),
        ],
        in_specs=[vmem] * 6 + [hbm] * 6,
        out_specs=[hbm, vmem, vmem, vmem],
        scratch_shapes=[
            pltpu.VMEM((rows2.shape[0], height), BF16),
            pltpu.VMEM((height, rows3.shape[1]), BF16),
            pltpu.VMEM((width, cols2.shape[1]), BF16),
            pltpu.VMEM((wide3.shape[0], width), BF16),
            dma((4,)),
            pltpu.VMEM((steps, inputs, block, width), F32),
            dma((steps,)),
            pltpu.VMEM((2, inputs, inputs, 128), F32),
            dma,
            pltpu.VMEM((blocks, 2 * inputs * RB, width), BF16),
            pltpu.VMEM((blocks, rows, width), F32),
            pltpu.VMEM((2 * rows, inputs * RB), BF16),
            pltpu.VMEM((2 * rows, inputs * RB), BF16),
            pltpu.VMEM((height, 2 * own * M), F32),
            pltpu.VMEM((A, 4, 128), F32),
            pltpu.VMEM((count, 4, 128), F32),
            pltpu.VMEM((2, 12, 128), F32),
            pltpu.VMEM((A, 12, 128), F32),
            pltpu.VMEM((A, 4, 128), F32),
            pltpu.VMEM((count, 4, 128), F32),
            pltpu.VMEM((2, 8, 128), F32),
            pltpu.VMEM((A, 8, 128), F32),
            dma((2, A)),
            dma((2,)),
            dma((2, count)),
            dma((2,)),
            pltpu.VMEM((n, kept, cap), F32),
            pltpu.VMEM((n, kept, cap), F32),
            dma((n,)),
            dma,
            pltpu.VMEM((kept, points), F32),
            pltpu.VMEM((points, 128), F32),
            pltpu.VMEM((2, own * FOLD, points), BF16),
            pltpu.VMEM((points, width), BF16),
            pltpu.VMEM((own, height, width), F32),
            pltpu.VMEM((own, height, 6 * M), F32),
            pltpu.VMEM((blocks, 2 * rows, width), BF16),
            pltpu.VMEM((blocks, rows, width), F32),
            dma((steps,)),
            dma((steps,)),
            pltpu.VMEM((2 * inputs * RB, 2 * rows), F32),
            pltpu.VMEM((4, 128), F32),
            pltpu.VMEM((n, 4, 128), F32),
            dma((n,)),
            dma,
            dma((steps,)),
        ],
        compiler_params=pltpu.CompilerParams(
            collective_id=0, has_side_effects=True, vmem_limit_bytes=58 * MIB
        ),
    )(*args, *constants)


def turn_blocks(x):
    group = iota((8, 128), 1) // M
    line = iota((8, 128), 0)
    out = jnp.where(group == line, x, 0.0)
    for d in range(1, 8):
        y = pltpu.roll(pltpu.roll(x, d * M, 1), 8 - d, 0)
        out = jnp.where((group - line + 8) % 8 == d, y, out)
    return out


def back_kernel(
    scales, partial_ref, spec_ref, back_ref, gp_ref, kept_ref, rows3_hbm, wide3_hbm,
    out_ref, gs_ref, point_ref, bias_ref,
    half_ref, spec_t, grad_t, point_t, rows3_ref, wide3_ref, table_sem,
):
    grad_scale, norm_points, bias_scale = scales
    step = pl.program_id(0)
    own, block, width = out_ref.shape
    rows = own * RB
    height = half_ref.shape[1]
    each = gs_ref.shape[1]
    inputs = 2 * own

    @pl.when(step == 0)
    def _():
        row_at = pl.multiple_of(lax.axis_index("row") * height, 128)
        col_at = pl.multiple_of(lax.axis_index("col") * width, 128)
        loads = [
            pltpu.make_async_copy(
                rows3_hbm.at[pl.ds(row_at, height), :], rows3_ref, table_sem.at[0]
            ),
            pltpu.make_async_copy(
                wide3_hbm.at[:, pl.ds(col_at, width)], wide3_ref, table_sem.at[1]
            ),
        ]
        for one in loads:
            one.start()
        kept = as_column(kept_ref[...], lax.axis_index("ch") * own, own)
        mode = iota((own, MODES), 1)
        row_mode = mode // M
        rank = jnp.where(row_mode < M, row_mode, A - 1 - row_mode)
        keep = jnp.where((rank < kept) & (mode % M < kept), grad_scale, 0.0)
        biases = jnp.zeros((1, own), F32)
        for part in range(2):
            for octet in range(own // 8):
                j = part * (own // 8) + octet
                for t in range(A // 8):
                    lanes = slice(t * 128, (t + 1) * 128)
                    lines = slice(octet * 8, octet * 8 + 8)
                    got = turn_blocks(back_ref[t * 8 : t * 8 + 8, 4 + j, :])
                    if part == 0 and t == 0:
                        shape = (8, own)
                        named = iota(shape, 1) == iota(shape, 0) + octet * 8
                        named = jnp.where(named, got[:, :1] * bias_scale, 0.0)
                        biases = biases + jnp.sum(named, axis=0, keepdims=True)
                    grad_t[part, lines, lanes] = got * keep[lines, lanes]
                    for side in range(2):
                        at = side * own + octet * 8
                        spec_t[part, at : at + 8, lanes] = turn_blocks(
                            spec_ref[t * 8 : t * 8 + 8, side * 4 + j, :]
                        )
        bias_ref[...] = biases
        gp = gp_ref[...] * norm_points
        into = 128 // own
        for k in range(into):
            for i in range(inputs // into):
                at = i * into + k
                point_t[at : at + 1, :] = gp[i : i + 1, k * own : (k + 1) * own]
        eye = sel(iota((own, own), 0) == iota((own, own), 1))
        point_ref[...] = exact(eye, point_t[...], NT)
        for one in loads:
            one.wait()
        re = jnp.concatenate((back_ref[:, 0, :], back_ref[:, 1, :]), axis=1)
        im = jnp.concatenate((back_ref[:, 2, :], back_ref[:, 3, :]), axis=1)
        mode_half(re, im, rows3_ref[...], half_ref)

    for u in range(block // RB):
        at = slice(u * RB, (u + 1) * RB)
        first = pl.multiple_of(step * block + u * RB, RB)
        half = half_ref[:, pl.ds(first, RB), :].reshape(rows, 6 * M).astype(BF16)
        result = mm(half, wide3_ref[...]).reshape(own, RB, width)
        out_ref[:, at, :] = partial_ref[:, at, :] + result
    for i in range(each):
        c = step * each + i
        spec_re = spec_t[0, pl.ds(c, 1), :]
        spec_im = spec_t[1, pl.ds(c, 1), :]
        gs_ref[0, i] = grad_t[0] * spec_re + grad_t[1] * spec_im
        gs_ref[1, i] = grad_t[1] * spec_re - grad_t[0] * spec_im


def whole(shape):
    return pl.BlockSpec(shape, lambda i: (0,) * len(shape))


def back_pass(partial, spec, back, gp, kept, rows3, wide3, scales):
    own, height, width = partial.shape
    block = 4 * RB
    steps = height // block
    each = 2 * own // steps
    hbm = pl.BlockSpec(memory_space=pl.ANY)
    tile = pl.BlockSpec((own, block, width), lambda i: (0, i, 0))
    return pl.pallas_call(
        functools.partial(back_kernel, scales),
        grid=(steps,),
        in_specs=[tile, whole(spec.shape), whole(back.shape), whole(gp.shape), whole(kept.shape)]
        + [hbm, hbm],
        out_specs=[
            tile,
            pl.BlockSpec((2, each, own, MODES), lambda i: (0, i, 0, 0)),
            whole((own, 2 * own)),
            whole((1, own)),
        ],
        out_shape=[
            jax.ShapeDtypeStruct((own, height, width), F32),
            jax.ShapeDtypeStruct((2, 2 * own, own, MODES), F32),
            jax.ShapeDtypeStruct((own, 2 * own), F32),
            jax.ShapeDtypeStruct((1, own), F32),
        ],
        scratch_shapes=[
            pltpu.VMEM((own, height, 6 * M), F32),
            pltpu.VMEM((2, 2 * own, MODES), F32),
            pltpu.VMEM((2, own, MODES), F32),
            pltpu.VMEM((2 * own, own), F32),
            pltpu.VMEM((height, rows3.shape[1]), BF16),
            pltpu.VMEM((wide3.shape[0], width), BF16),
            pltpu.SemaphoreType.DMA((2,)),
        ],
        compiler_params=pltpu.CompilerParams(vmem_limit_bytes=58 * MIB),
    )(partial, spec, back, gp, kept, rows3, wide3)


def per_device(
    field, spec_weight, point_weight, bias, kept_modes, residual, trace_dest, trace_cell
):
    n_row = lax.axis_size("row")
    n_col = lax.axis_size("col")
    inputs, height, width = field.shape
    own = inputs // lax.axis_size("ch")
    points = trace_dest.shape[0]
    tiles = n_row * n_col
    points_all = points * tiles
    cap = max(2, 2 * points // tiles)
    forward_scale = 1.0 / math.sqrt(height * n_row * width * n_col)
    mix_scale = 1.0 / math.sqrt(MODES)
    norm_points = 1.0 / math.sqrt(points_all)
    constants = [jnp.asarray(t) for t in tables(height * n_row, width * n_col)]
    kept = kept_modes.reshape(1, inputs)
    args = (
        trace_dest.reshape(1, points), trace_cell.reshape(1, points), residual, kept,
        bias.reshape(1, own), point_weight, field, spec_weight,
    )
    partial, spec, back, gp = main_pass(
        args, constants, (forward_scale, mix_scale), cap, n_row, n_col
    )
    grad_field, grad_spec, grad_point, grad_bias = back_pass(
        partial, spec, back, gp, kept, constants[1], constants[3],
        (math.sqrt(MODES / points_all), norm_points, norm_points / mix_scale),
    )
    return (grad_field, grad_spec, grad_point.T, grad_bias.reshape(own))


def solution(mesh):
    return jax.shard_map(
        per_device,
        mesh=mesh,
        in_specs=(
            P(None, "row", "col"),
            P(),
            P(),
            P("ch"),
            P(),
            P("ch", ("row", "col")),
            P(("row", "col"), None),
            P(("row", "col")),
        ),
        out_specs=(P("ch", "row", "col"), P(None, None, "ch", None), P(None, "ch"), P("ch")),
        check_vma=False,
    )
```

```python
import functools
import math

import jax
import jax.numpy as jnp
import ml_dtypes
import numpy as np
from jax import lax
from jax.experimental import pallas as pl
from jax.experimental.pallas import tpu as pltpu
from jax.sharding import PartitionSpec as P

M = 16
A = 2 * M
MODES = A * M
RB = 8
FOLD = 32
F32 = jnp.float32
BF16 = jnp.bfloat16
FULL_TURN = 6.283185307179586
NN = (((1,), (0,)), ((), ()))
NT = (((1,), (1,)), ((), ()))
MIB = 1 << 20
MESH = pl.DeviceIdType.MESH


def trig(frequency, period):
    phases = frequency[:, None] * np.arange(period)[None, :] % period
    angles = phases.astype(np.float32) * np.float32(FULL_TURN / period)
    angles = angles.astype(np.float64)
    return np.cos(angles).astype(np.float32), np.sin(angles).astype(np.float32)


def np_split(x):
    hi = x.astype(ml_dtypes.bfloat16)
    return hi, (x - hi.astype(np.float32)).astype(ml_dtypes.bfloat16)


@functools.lru_cache(maxsize=None)
def tables(n_rows, n_cols):
    frequency = np.arange(A)
    frequency = np.where(frequency < M, frequency, frequency - A)
    rows = np.concatenate(trig(frequency, n_rows), axis=0)
    cos, sin = trig(np.arange(M), n_cols)
    hi, low = np_split(rows)
    rows2 = np.concatenate((hi, low), axis=0)
    rows3 = np.concatenate((hi.T, low.T, hi.T), axis=1)
    hi, low = np_split(np.concatenate((cos, sin), axis=0))
    cols2 = np.concatenate((hi.T, low.T), axis=1)
    hi, low = np_split(np.concatenate((cos, -sin), axis=0))
    wide3 = np.concatenate((hi, hi, low), axis=0)
    return rows2, rows3, cols2, wide3


def split2(x):
    hi = x.astype(BF16)
    return hi, (x - hi.astype(F32)).astype(BF16)


def mm(a, b, dims=NN):
    return lax.dot_general(a, b, dims, preferred_element_type=F32)


def stacked(x, axis):
    hi, low = split2(x)
    return jnp.concatenate((hi.astype(F32), low.astype(F32)), axis=axis).astype(BF16)


def deep_left(x):
    hi = x.astype(BF16).astype(F32)
    return jnp.concatenate((hi, x - hi, hi), axis=1)


def deep_right(x):
    hi = x.astype(BF16).astype(F32)
    return jnp.concatenate((hi, hi, x - hi), axis=0).astype(BF16)


def exact(a, b, dims=NN):
    return lax.dot_general(
        a, b, dims, precision=lax.Precision.HIGHEST, preferred_element_type=F32
    )


def iota(shape, axis):
    return lax.broadcasted_iota(jnp.int32, shape, axis)


def sel(mask):
    return mask.astype(F32)


def pack(dest, vals, out_ref, tiles, cap):
    n = dest.shape[1]
    named = dest == iota((tiles, n), 0)
    before = iota((n, n), 0) < iota((n, n), 1)
    earlier = mm(sel(named).astype(BF16), sel(before).astype(BF16))
    rank = jnp.sum(jnp.where(named, earlier, 0.0), axis=0, keepdims=True)
    position = dest * cap + rank.astype(jnp.int32)
    rows = vals.shape[0]
    hi = vals.astype(BF16)
    left = vals - hi.astype(F32)
    mid = left.astype(BF16)
    low = (left - mid.astype(F32)).astype(BF16)
    parts = jnp.concatenate((hi.astype(F32), mid.astype(F32), low.astype(F32)), axis=0).astype(BF16)
    step = 512
    for first in range(0, tiles * cap, step):
        place = sel(position == iota((step, n), 0) + first).astype(BF16)
        got = mm(parts, place, NT)
        got = got[:rows] + got[rows : 2 * rows] + got[2 * rows : 3 * rows]
        for at in range(0, step, cap):
            out_ref[(first + at) // cap] = got[:, at : at + cap]


def mode_lines(rows2, tall, scale):
    side = tall.shape[1] // 2
    both = mm(rows2, stacked(tall, 1))
    grid = both[: 2 * A, : 2 * side] + both[2 * A :, : 2 * side] + both[: 2 * A, 2 * side :]
    re = (grid[:A, :side] - grid[A:, side:]) * scale
    im = (grid[A:, :side] + grid[:A, side:]) * (-scale)
    return [part[:, at : at + 128] for part in (re, im) for at in range(0, side, 128)]


def part_of(x, size):
    if size & (size - 1) == 0:
        return lax.shift_right_logical(x, size.bit_length() - 1)
    return lax.div(x, size)


def rest_of(x, size):
    if size & (size - 1) == 0:
        return x & (size - 1)
    return lax.rem(x, size)


def as_column(line, first=0, count=None):
    width = line.shape[1]
    shape = (count or width, width)
    picked = jnp.where(iota(shape, 1) == iota(shape, 0) + first, line.astype(F32), 0.0)
    return jnp.sum(picked, axis=1, keepdims=True).astype(jnp.int32)


def same_place():
    return sel(iota((128, 128), 0) % M == iota((128, 128), 1) % M)


def spread8(s8):
    z = jnp.broadcast_to(s8[:, None, :], (8, 8, 128)).reshape(64, 128)
    z = jnp.where(iota((64, 128), 1) // M == iota((64, 128), 0) % 8, z, 0.0)
    z = exact(z, same_place())
    re = jnp.concatenate((z[0:16], z[32:48]), axis=0)
    im = jnp.concatenate((z[16:32], z[48:64]), axis=0)
    return re, im


def compact8(re, im, a):
    y = jnp.concatenate((re, im), axis=0)
    group = iota(y.shape, 1) // M
    y = jnp.where(group == lax.rem(a, 8), y, 0.0)
    y = exact(y, same_place())
    y = jnp.where(group == iota(y.shape, 0) % 8, y, 0.0)
    return jnp.sum(y.reshape(8, 8, 128), axis=1)


def mode_half(re, im, rows3, half_ref):
    grid = jnp.concatenate(
        (jnp.concatenate((re, im), axis=1), jnp.concatenate((-im, re), axis=1)), axis=0
    )
    half = mm(rows3, deep_right(grid))
    side = half.shape[1] // 2
    for o in range(side // M):
        at = o * M
        pair = jnp.concatenate((half[:, at : at + M], half[:, side + at : side + at + M]), axis=1)
        half_ref[o] = deep_left(pair)


def put_tall(tall_ref, first, tall, own):
    for c in range(own):
        for part in range(2):
            at = (part * own + c) * M
            tall_ref[pl.ds(first, RB), at : at + M] = tall[
                c * RB : (c + 1) * RB, part * M : (part + 1) * M
            ]


def col_modes(parts, cols2):
    half = parts.shape[0] // 2
    got = mm(parts, cols2)
    return got[:half, : 2 * M] + got[:half, 2 * M :] + got[half:, : 2 * M]


def main_kernel(
    n_row, n_col, scales,
    dest_ref, cell_ref, res_ref, kept_ref, bias_ref, point_ref, field_ref, w_ref,
    rows2_hbm, rows3_hbm, cols2_hbm, wide3_hbm,
    partial_ref, spec_ref, back_ref, gp_ref,
    rows2_ref, rows3_ref, cols2_ref, wide3_ref, table_sem,
    fbuf, load_sem, wbuf, w_sem, f2_ref, pre_ref, kron2_ref, kronb_ref, tall_ref,
    x1, landed1, send1, gat1, x2, landed2, send2, gat2, rs_send, rs_recv, ag_send, ag_recv,
    grouped, came, trade_send, trade_recv, pts, ids_ref, vm_ref, hot_ref, cot_ref, half_ref,
    sl_ref, other_ref, swap_send, swap_recv, acc_ref, gpx, gpl, gp_send, gp_recv, out_sem,
):
    forward_scale, mix_scale = scales
    n = n_row * n_col
    count = 2 * n
    stride = count // A
    ch = lax.axis_index("ch")
    me = lax.axis_index("row") * n_col + lax.axis_index("col")
    flat = me * 2 + ch
    a = part_of(flat, stride)
    is_reducer = rest_of(flat, stride) == 0
    small = stride == 1
    steps, inputs, block, width = fbuf.shape
    own = inputs // 2
    rows = own * RB
    height = steps * block
    subs = block // RB
    points = pts.shape[1]

    def device_of(f):
        f = jnp.int32(f)
        p = part_of(f, 2)
        return (part_of(p, n_col), rest_of(p, n_col), rest_of(f, 2))

    def remote(src, dst, send, recv, f):
        return pltpu.make_async_remote_copy(
            src_ref=src, dst_ref=dst, send_sem=send, recv_sem=recv,
            device_id=device_of(f), device_id_type=MESH,
        )

    def some(low, high, body):
        if small:
            for k in range(low, high):
                body(k)
        else:
            each(low, high, body)

    def each(low, high, body):
        def go(k, carry):
            body(k)
            return carry

        lax.fori_loop(low, high, go, 0)

    def on_reducer(body):
        if stride == 1:
            body()
        else:
            pl.when(is_reducer)(body)

    def off_reducer(body):
        if stride > 1:
            pl.when(jnp.logical_not(is_reducer))(body)

    row_at = pl.multiple_of(lax.axis_index("row") * height, 128)
    col_at = pl.multiple_of(lax.axis_index("col") * width, 128)
    table_loads = [
        pltpu.make_async_copy(src, dst, table_sem.at[i])
        for i, (src, dst) in enumerate((
            (rows2_hbm.at[:, pl.ds(row_at, height)], rows2_ref),
            (rows3_hbm.at[pl.ds(row_at, height), :], rows3_ref),
            (cols2_hbm.at[pl.ds(col_at, width), :], cols2_ref),
            (wide3_hbm.at[:, pl.ds(col_at, width)], wide3_ref),
        ))
    ]

    def load(i):
        return pltpu.make_async_copy(
            field_ref.at[:, pl.ds(pl.multiple_of(i * block, block), block), :],
            fbuf.at[i], load_sem.at[i],
        )

    w_load = pltpu.make_async_copy(
        w_ref.at[:, :, :, pl.ds(pl.multiple_of(part_of(a, 8) * 128, 128), 128)], wbuf, w_sem
    )
    for one in table_loads:
        one.start()
    each(0, steps, lambda i: load(i).start())
    w_load.start()

    barrier = pltpu.get_barrier_semaphore()
    some(1, count, lambda k: pl.semaphore_signal(
        barrier, inc=1, device_id=device_of(rest_of(flat + k, count)), device_id_type=MESH
    ))

    shape = (rows, inputs)
    pick = sel(iota(shape, 1) == ch * own + iota(shape, 0) // RB)
    wide_shape = (inputs, inputs * RB)
    spread = sel(iota(wide_shape, 0) == iota(wide_shape, 1) // RB)
    turned = sel(iota(wide_shape, 0) == (iota(wide_shape, 1) // RB + ch * own) % inputs)
    kron_shape = (rows, inputs * RB)
    same = iota(kron_shape, 0) % RB == iota(kron_shape, 1) % RB
    forward_point = exact(exact(pick, point_ref[...], NT), spread)
    kron2_ref[...] = stacked(jnp.where(same, forward_point, 0.0), 0)
    backward_point = exact(exact(pick, point_ref[...]), turned)
    kronb_ref[...] = stacked(jnp.where(same, backward_point, 0.0), 0)
    acc_ref[...] = jnp.zeros_like(acc_ref)
    for one in table_loads:
        one.wait()

    def front(i):
        load(i).wait()
        for u in range(subs):
            b = i * subs + u
            hi, low = split2(fbuf[i, :, u * RB : (u + 1) * RB, :].reshape(inputs * RB, width))
            f2_ref[b, : inputs * RB, :] = hi
            f2_ref[b, inputs * RB :, :] = low
            both = mm(kron2_ref[...], hi)
            pre_ref[b] = both[:rows] + both[rows:] + mm(kron2_ref[:rows, :], low)
            at = pl.multiple_of(ch * rows, rows)
            mine = jnp.concatenate(
                (f2_ref[b, pl.ds(at, rows), :], f2_ref[b, pl.ds(at + inputs * RB, rows), :]), axis=0
            )
            put_tall(tall_ref, pl.multiple_of(b * RB, RB), col_modes(mine, cols2_ref[...]), own)

    each(0, steps, front)

    def scatter(x, landed, stage):
        def copy(k):
            to = rest_of(a + k, A)
            target = to * stride
            slot = count - k if small else rest_of(flat - target + count, count)
            return remote(
                x.at[to], landed.at[slot], rs_send.at[stage], rs_recv.at[stage], target
            )

        return copy

    def scatter_start(x, landed, stage, scale):
        lines = mode_lines(rows2_ref[...], tall_ref[...], scale)
        for j, line in enumerate(lines):
            x[:, j, :] = line
        copy = scatter(x, landed, stage)
        if stage == 0:
            pl.semaphore_wait(barrier, count - 1)
        some(1, A, lambda k: copy(k).start())
        off_reducer(lambda: copy(0).start())

    def scatter_end(x, landed, stage):
        def take(slots):
            sent = x.at[pl.ds(0, slots)]
            remote(sent, sent, rs_send.at[stage], rs_recv.at[stage], flat).wait_send()

        on_reducer(lambda: take(A - 1))
        off_reducer(lambda: take(A))

    def reduced(x, landed, stage):
        got = landed.at[pl.ds(1, count - 1)]
        remote(got, got, rs_send.at[stage], rs_recv.at[stage], flat).wait_recv()
        pairs = landed[pl.ds(2, count - 2)].reshape(n - 1, 2, 4, 128)
        pairs = jnp.sum(pairs, axis=0)
        mine = x[a] + pairs[0]
        theirs = landed[1] + pairs[1]
        first = jnp.where(ch == 0, mine, theirs)
        second = jnp.where(ch == 0, theirs, mine)
        return jnp.concatenate((first, second), axis=0)

    def gather(source, gat, stage):
        def copy(k):
            f = rest_of(flat + k, count)
            send = ag_send.at[stage, 0 if small else k]
            return remote(
                source.at[rest_of(ch + k, 2)], gat.at[a], send, ag_recv.at[stage], f
            )

        return copy

    def gather_wait(gat, stage):
        def take(slots):
            got = gat.at[pl.ds(0, slots)]
            remote(got, got, ag_send.at[stage, 0], ag_recv.at[stage], flat).wait_recv()

        on_reducer(lambda: take(A - 1))
        off_reducer(lambda: take(A))

    def gather_end(source, gat, stage):
        if small:
            sent = gat.at[pl.ds(0, A - 1)]
            remote(sent, sent, ag_send.at[stage, 0], ag_recv.at[stage], flat).wait_send()
        else:
            copy = gather(source, gat, stage)
            on_reducer(lambda: each(1, count, lambda k: copy(k).wait_send()))

    rank = jnp.where(a < M, a, A - 1 - a)
    kept = as_column(kept_ref[...])
    allowed = sel((rank < kept) & (iota((inputs, 128), 1) % M < kept))

    scatter_start(x1, landed1, 0, forward_scale)

    cells = (cell_ref[...] + 1).astype(F32)
    vals = jnp.concatenate(
        (res_ref[...], jnp.broadcast_to(cells, (8, cells.shape[1]))), axis=0
    )
    cap = grouped.shape[2]
    pack(dest_ref[...], vals, grouped, n, cap)

    def trade(k):
        p = rest_of(me + k, n)
        return remote(grouped.at[p], came.at[k], trade_send, trade_recv, p * 2 + ch)

    some(1, n, lambda k: trade(k).start())
    came[0] = grouped[me]

    def mix():
        s8 = reduced(x1, landed1, 0)
        spec_re, spec_im = spread8(s8)
        w_load.wait()
        re = jnp.zeros((inputs, 128), F32)
        im = jnp.zeros((inputs, 128), F32)
        for c in range(inputs):
            one_re, one_im = spec_re[c : c + 1], spec_im[c : c + 1]
            re = re + (wbuf[0, c] * one_re - wbuf[1, c] * one_im)
            im = im + (wbuf[0, c] * one_im + wbuf[1, c] * one_re)
        keep = allowed * mix_scale
        mixed = compact8(re * keep, im * keep, a)
        for d in range(2):
            send1[d, :8] = s8
            send1[d, 8:10] = mixed[2 * d : 2 * d + 2]
            send1[d, 10:12] = mixed[4 + 2 * d : 6 + 2 * d]
        copy = gather(send1, gat1, 0)
        some(1, count, lambda k: copy(k).start())
        gat1[a] = send1[ch]

    on_reducer(mix)
    if stride > 1:
        off_reducer(lambda: w_load.wait())

    came_all = came.at[pl.ds(1, n - 1)]
    remote(came_all, came_all, trade_send, trade_recv, flat).wait_recv()
    for p in range(n):
        pts[:, p * cap : (p + 1) * cap] = came[p]
    cell = pts[own : own + 1, :].astype(jnp.int32) - 1
    row = cell // width
    fold = jnp.where(cell < 0, -1, row % FOLD)
    code = jnp.where(cell < 0, -1, row // FOLD * width + cell % width).astype(F32)
    for first in range(0, points, 128):
        ids_ref[first : first + 128, :] = jnp.broadcast_to(
            code[:, first : first + 128], (128, 128)
        ).T
    here = fold == iota((FOLD, points), 0)
    half_own = own // 2

    def fill(o):
        value = pts[pl.ds(o, 1), :]
        hi = value.astype(BF16).astype(F32)
        group = o // half_own
        at = pl.multiple_of(lax.rem(o, half_own) * FOLD, FOLD)
        vm_ref[group, pl.ds(at, FOLD), :] = jnp.where(here, hi, 0.0).astype(BF16)
        vm_ref[group, pl.ds(at + half_own * FOLD, FOLD), :] = jnp.where(
            here, value - hi, 0.0
        ).astype(BF16)

    each(0, own, fill)
    span = half_own * FOLD

    def place(q):
        for at in range(0, width, 128):
            names = (iota((points, 128), 1) + (q * width + at)).astype(F32)
            hot_ref[:, at : at + 128] = sel(ids_ref[...] == names).astype(BF16)
        for group in range(2):
            got = mm(vm_ref[group], hot_ref[...])
            got = (got[:span] + got[span:]).reshape(half_own, FOLD, width)
            cot_ref[
                group * half_own : (group + 1) * half_own,
                pl.ds(pl.multiple_of(q * FOLD, FOLD), FOLD), :,
            ] = got

    each(0, height // FOLD, place)

    gather_wait(gat1, 0)
    re = jnp.concatenate((gat1[:, 8, :], gat1[:, 9, :]), axis=1)
    im = jnp.concatenate((gat1[:, 10, :], gat1[:, 11, :]), axis=1)
    bias_shape = (own, own * M)
    bias_at = sel(iota(bias_shape, 1) == iota(bias_shape, 0) * M)
    bias_line = exact(jnp.broadcast_to(bias_ref[...], (8, own)), bias_at)[:1]
    re = re + jnp.where(iota(re.shape, 0) == 0, bias_line, 0.0)
    mode_half(re, im, rows3_ref[...], half_ref)

    def swap(i):
        at = pl.ds(i * subs, subs)
        return remote(
            pre_ref.at[at], other_ref.at[at], swap_send, swap_recv.at[i], me * 2 + 1 - ch
        )

    k0 = math.sqrt(2.0 / math.pi)

    def slopes(i):
        for u in range(subs):
            b = i * subs + u
            first = pl.multiple_of(b * RB, RB)
            half = half_ref[:, pl.ds(first, RB), :].reshape(rows, 6 * M).astype(BF16)
            pre = pre_ref[b] + mm(half, wide3_ref[...])
            cot = cot_ref[:, pl.ds(first, RB), :].reshape(rows, width)
            square = pre * pre
            t = jnp.tanh(k0 * pre * (1.0 + 0.044715 * square))
            rate = 0.5 * (1.0 + t) + 0.5 * k0 * pre * (1.0 - t * t) * (1.0 + 3 * 0.044715 * square)
            slope = cot * rate
            pre_ref[b] = slope
            hi, low = split2(slope)
            sl_ref[b, :rows, :] = hi
            sl_ref[b, rows:, :] = low
            put_tall(tall_ref, first, col_modes(sl_ref[b], cols2_ref[...]), own)
        swap(i).start()

    each(0, steps, slopes)
    scatter_start(x2, landed2, 1, mix_scale)

    def point_sums(i):
        fields = jnp.concatenate([f2_ref[i * 2 + u] for u in range(2)], axis=1)
        found = jnp.concatenate([sl_ref[i * 2 + u] for u in range(2)], axis=1)
        acc_ref[...] += mm(fields, found, NT)

    each(0, steps * subs // 2, point_sums)
    total = acc_ref[: inputs * RB, :] + acc_ref[inputs * RB :, :]
    total = total[:, :rows] + total[:, rows:]
    matched = iota(total.shape, 0) % RB == iota(total.shape, 1) % RB
    total = jnp.sum(jnp.where(matched, total, 0.0).reshape(inputs, RB, rows), axis=1)
    into = 128 // own
    group = sel(iota((rows, 128), 0) // RB == iota((rows, 128), 1) % own)
    total = exact(total, group)
    mine = iota(total.shape, 1) // own == iota(total.shape, 0) % into
    gpx[...] = jnp.sum(jnp.where(mine, total, 0.0).reshape(inputs // into, into, 128), axis=1)

    def point_send(k):
        p = rest_of(me + k, n)
        return remote(gpx, gpl.at[k], gp_send, gp_recv, p * 2 + ch)

    some(1, n, lambda k: point_send(k).start())

    def adjoint():
        s8 = reduced(x2, landed2, 1)
        grad_re, grad_im = spread8(s8)
        grad_re = grad_re * allowed
        grad_im = grad_im * allowed
        lines_re, lines_im = [], []
        for c in range(inputs):
            w_re, w_im = wbuf[0, c], wbuf[1, c]
            lines_re.append(jnp.sum(w_re * grad_re + w_im * grad_im, axis=0, keepdims=True))
            lines_im.append(jnp.sum(w_re * grad_im - w_im * grad_re, axis=0, keepdims=True))
        re = jnp.concatenate(lines_re, axis=0) * forward_scale
        im = jnp.concatenate(lines_im, axis=0) * forward_scale
        turned_modes = compact8(re, im, a)
        for d in range(2):
            send2[d, :2] = turned_modes[2 * d : 2 * d + 2]
            send2[d, 2:4] = turned_modes[4 + 2 * d : 6 + 2 * d]
            send2[d, 4:8] = s8[4 * d : 4 * d + 4]
        copy = gather(send2, gat2, 1)
        some(1, count, lambda k: copy(k).start())
        gat2[a] = send2[ch]

    on_reducer(adjoint)

    def store(i):
        at = pl.ds(pl.multiple_of(i * block, block), block)
        return pltpu.make_async_copy(cot_ref.at[:, at, :], partial_ref.at[:, at, :], out_sem)

    def backs(i):
        swap(i).wait_recv()
        for u in range(subs):
            b = i * subs + u
            first = pl.multiple_of(b * RB, RB)
            other_hi, other_low = split2(other_ref[b])
            hi = jnp.concatenate((sl_ref[b, :rows, :], other_hi), axis=0)
            low = jnp.concatenate((sl_ref[b, rows:, :], other_low), axis=0)
            both = mm(kronb_ref[...], hi)
            result = both[:rows] + both[rows:] + mm(kronb_ref[:rows, :], low)
            cot_ref[:, pl.ds(first, RB), :] = result.reshape(own, RB, width)
        store(i).start()

    each(0, steps, backs)

    gp_all = gpl.at[pl.ds(1, n - 1)]
    remote(gp_all, gp_all, gp_send, gp_recv, flat).wait_recv()
    gp_ref[...] = gpx[...] + jnp.sum(gpl[pl.ds(1, n - 1)], axis=0)
    gather_wait(gat2, 1)
    spec_ref[...] = gat1[...]
    back_ref[...] = gat2[...]

    scatter_end(x1, landed1, 0)
    scatter_end(x2, landed2, 1)
    gather_end(send1, gat1, 0)
    gather_end(send2, gat2, 1)
    remote(came_all, came_all, trade_send, trade_recv, flat).wait_send()
    remote(gp_all, gp_all, gp_send, gp_recv, flat).wait_send()
    sent = pre_ref.at[pl.ds(0, steps * subs)]
    remote(sent, sent, swap_send, swap_recv.at[0], flat).wait_send()
    pltpu.make_async_copy(cot_ref, partial_ref, out_sem).wait()


def main_pass(args, constants, scales, cap, n_row, n_col):
    field = args[6]
    n = n_row * n_col
    count = 2 * n
    inputs, height, width = field.shape
    own = inputs // 2
    block = 2 * RB
    steps = height // block
    blocks = height // RB
    rows = own * RB
    kept = own + 8
    points = n * cap
    vmem = pl.BlockSpec(memory_space=pltpu.VMEM)
    hbm = pl.BlockSpec(memory_space=pl.ANY)
    dma = pltpu.SemaphoreType.DMA
    rows2, rows3, cols2, wide3 = constants
    return pl.pallas_call(
        functools.partial(main_kernel, n_row, n_col, scales),
        out_shape=[
            jax.ShapeDtypeStruct((own, height, width), F32),
            jax.ShapeDtypeStruct((A, 12, 128), F32),
            jax.ShapeDtypeStruct((A, 8, 128), F32),
            jax.ShapeDtypeStruct((4, 128), F32),
        ],
        in_specs=[vmem] * 6 + [hbm] * 6,
        out_specs=[hbm, vmem, vmem, vmem],
        scratch_shapes=[
            pltpu.VMEM((rows2.shape[0], height), BF16),
            pltpu.VMEM((height, rows3.shape[1]), BF16),
            pltpu.VMEM((width, cols2.shape[1]), BF16),
            pltpu.VMEM((wide3.shape[0], width), BF16),
            dma((4,)),
            pltpu.VMEM((steps, inputs, block, width), F32),
            dma((steps,)),
            pltpu.VMEM((2, inputs, inputs, 128), F32),
            dma,
            pltpu.VMEM((blocks, 2 * inputs * RB, width), BF16),
            pltpu.VMEM((blocks, rows, width), F32),
            pltpu.VMEM((2 * rows, inputs * RB), BF16),
            pltpu.VMEM((2 * rows, inputs * RB), BF16),
            pltpu.VMEM((height, 2 * own * M), F32),
            pltpu.VMEM((A, 4, 128), F32),
            pltpu.VMEM((count, 4, 128), F32),
            pltpu.VMEM((2, 12, 128), F32),
            pltpu.VMEM((A, 12, 128), F32),
            pltpu.VMEM((A, 4, 128), F32),
            pltpu.VMEM((count, 4, 128), F32),
            pltpu.VMEM((2, 8, 128), F32),
            pltpu.VMEM((A, 8, 128), F32),
            dma((2,)),
            dma((2,)),
            dma((2, count)),
            dma((2,)),
            pltpu.VMEM((n, kept, cap), F32),
            pltpu.VMEM((n, kept, cap), F32),
            dma,
            dma,
            pltpu.VMEM((kept, points), F32),
            pltpu.VMEM((points, 128), F32),
            pltpu.VMEM((2, own * FOLD, points), BF16),
            pltpu.VMEM((points, width), BF16),
            pltpu.VMEM((own, height, width), F32),
            pltpu.VMEM((own, height, 6 * M), F32),
            pltpu.VMEM((blocks, 2 * rows, width), BF16),
            pltpu.VMEM((blocks, rows, width), F32),
            dma,
            dma((steps,)),
            pltpu.VMEM((2 * inputs * RB, 2 * rows), F32),
            pltpu.VMEM((4, 128), F32),
            pltpu.VMEM((n, 4, 128), F32),
            dma,
            dma,
            dma,
        ],
        compiler_params=pltpu.CompilerParams(
            collective_id=0, has_side_effects=True, vmem_limit_bytes=58 * MIB
        ),
    )(*args, *constants)


def turn_blocks(x):
    group = iota((8, 128), 1) // M
    line = iota((8, 128), 0)
    out = jnp.where(group == line, x, 0.0)
    for d in range(1, 8):
        y = pltpu.roll(pltpu.roll(x, d * M, 1), 8 - d, 0)
        out = jnp.where((group - line + 8) % 8 == d, y, out)
    return out


def back_kernel(
    scales, partial_ref, spec_ref, back_ref, gp_ref, kept_ref, rows3_hbm, wide3_hbm,
    out_ref, gs_ref, point_ref, bias_ref,
    half_ref, spec_t, grad_t, point_t, rows3_ref, wide3_ref, table_sem,
):
    grad_scale, norm_points, bias_scale = scales
    step = pl.program_id(0)
    own, block, width = out_ref.shape
    rows = own * RB
    height = half_ref.shape[1]
    each = gs_ref.shape[1]
    inputs = 2 * own

    @pl.when(step == 0)
    def _():
        row_at = pl.multiple_of(lax.axis_index("row") * height, 128)
        col_at = pl.multiple_of(lax.axis_index("col") * width, 128)
        loads = [
            pltpu.make_async_copy(
                rows3_hbm.at[pl.ds(row_at, height), :], rows3_ref, table_sem.at[0]
            ),
            pltpu.make_async_copy(
                wide3_hbm.at[:, pl.ds(col_at, width)], wide3_ref, table_sem.at[1]
            ),
        ]
        for one in loads:
            one.start()
        kept = as_column(kept_ref[...], lax.axis_index("ch") * own, own)
        mode = iota((own, MODES), 1)
        row_mode = mode // M
        rank = jnp.where(row_mode < M, row_mode, A - 1 - row_mode)
        keep = jnp.where((rank < kept) & (mode % M < kept), grad_scale, 0.0)
        biases = jnp.zeros((1, own), F32)
        for part in range(2):
            for octet in range(own // 8):
                j = part * (own // 8) + octet
                for t in range(A // 8):
                    lanes = slice(t * 128, (t + 1) * 128)
                    lines = slice(octet * 8, octet * 8 + 8)
                    got = turn_blocks(back_ref[t * 8 : t * 8 + 8, 4 + j, :])
                    if part == 0 and t == 0:
                        shape = (8, own)
                        named = iota(shape, 1) == iota(shape, 0) + octet * 8
                        named = jnp.where(named, got[:, :1] * bias_scale, 0.0)
                        biases = biases + jnp.sum(named, axis=0, keepdims=True)
                    grad_t[part, lines, lanes] = got * keep[lines, lanes]
                    for side in range(2):
                        at = side * own + octet * 8
                        spec_t[part, at : at + 8, lanes] = turn_blocks(
                            spec_ref[t * 8 : t * 8 + 8, side * 4 + j, :]
                        )
        bias_ref[...] = biases
        gp = gp_ref[...] * norm_points
        into = 128 // own
        for k in range(into):
            for i in range(inputs // into):
                at = i * into + k
                point_t[at : at + 1, :] = gp[i : i + 1, k * own : (k + 1) * own]
        eye = sel(iota((own, own), 0) == iota((own, own), 1))
        point_ref[...] = exact(eye, point_t[...], NT)
        for one in loads:
            one.wait()
        re = jnp.concatenate((back_ref[:, 0, :], back_ref[:, 1, :]), axis=1)
        im = jnp.concatenate((back_ref[:, 2, :], back_ref[:, 3, :]), axis=1)
        mode_half(re, im, rows3_ref[...], half_ref)

    for u in range(block // RB):
        at = slice(u * RB, (u + 1) * RB)
        first = pl.multiple_of(step * block + u * RB, RB)
        half = half_ref[:, pl.ds(first, RB), :].reshape(rows, 6 * M).astype(BF16)
        result = mm(half, wide3_ref[...]).reshape(own, RB, width)
        out_ref[:, at, :] = partial_ref[:, at, :] + result
    for i in range(each):
        c = step * each + i
        spec_re = spec_t[0, pl.ds(c, 1), :]
        spec_im = spec_t[1, pl.ds(c, 1), :]
        gs_ref[0, i] = grad_t[0] * spec_re + grad_t[1] * spec_im
        gs_ref[1, i] = grad_t[1] * spec_re - grad_t[0] * spec_im


def whole(shape):
    return pl.BlockSpec(shape, lambda i: (0,) * len(shape))


def back_pass(partial, spec, back, gp, kept, rows3, wide3, scales):
    own, height, width = partial.shape
    block = 4 * RB
    steps = height // block
    each = 2 * own // steps
    hbm = pl.BlockSpec(memory_space=pl.ANY)
    tile = pl.BlockSpec((own, block, width), lambda i: (0, i, 0))
    return pl.pallas_call(
        functools.partial(back_kernel, scales),
        grid=(steps,),
        in_specs=[tile, whole(spec.shape), whole(back.shape), whole(gp.shape), whole(kept.shape)]
        + [hbm, hbm],
        out_specs=[
            tile,
            pl.BlockSpec((2, each, own, MODES), lambda i: (0, i, 0, 0)),
            whole((own, 2 * own)),
            whole((1, own)),
        ],
        out_shape=[
            jax.ShapeDtypeStruct((own, height, width), F32),
            jax.ShapeDtypeStruct((2, 2 * own, own, MODES), F32),
            jax.ShapeDtypeStruct((own, 2 * own), F32),
            jax.ShapeDtypeStruct((1, own), F32),
        ],
        scratch_shapes=[
            pltpu.VMEM((own, height, 6 * M), F32),
            pltpu.VMEM((2, 2 * own, MODES), F32),
            pltpu.VMEM((2, own, MODES), F32),
            pltpu.VMEM((2 * own, own), F32),
            pltpu.VMEM((height, rows3.shape[1]), BF16),
            pltpu.VMEM((wide3.shape[0], width), BF16),
            pltpu.SemaphoreType.DMA((2,)),
        ],
        compiler_params=pltpu.CompilerParams(vmem_limit_bytes=58 * MIB),
    )(partial, spec, back, gp, kept, rows3, wide3)


def per_device(
    field, spec_weight, point_weight, bias, kept_modes, residual, trace_dest, trace_cell
):
    n_row = lax.axis_size("row")
    n_col = lax.axis_size("col")
    inputs, height, width = field.shape
    own = inputs // lax.axis_size("ch")
    points = trace_dest.shape[0]
    tiles = n_row * n_col
    points_all = points * tiles
    cap = max(2, 2 * points // tiles)
    forward_scale = 1.0 / math.sqrt(height * n_row * width * n_col)
    mix_scale = 1.0 / math.sqrt(MODES)
    norm_points = 1.0 / math.sqrt(points_all)
    constants = [jnp.asarray(t) for t in tables(height * n_row, width * n_col)]
    kept = kept_modes.reshape(1, inputs)
    args = (
        trace_dest.reshape(1, points), trace_cell.reshape(1, points), residual, kept,
        bias.reshape(1, own), point_weight, field, spec_weight,
    )
    partial, spec, back, gp = main_pass(
        args, constants, (forward_scale, mix_scale), cap, n_row, n_col
    )
    grad_field, grad_spec, grad_point, grad_bias = back_pass(
        partial, spec, back, gp, kept, constants[1], constants[3],
        (math.sqrt(MODES / points_all), norm_points, norm_points / mix_scale),
    )
    return (grad_field, grad_spec, grad_point.T, grad_bias.reshape(own))


def solution(mesh):
    return jax.shard_map(
        per_device,
        mesh=mesh,
        in_specs=(
            P(None, "row", "col"),
            P(),
            P(),
            P("ch"),
            P(),
            P("ch", ("row", "col")),
            P(("row", "col"), None),
            P(("row", "col")),
        ),
        out_specs=(P("ch", "row", "col"), P(None, None, "ch", None), P(None, "ch"), P("ch")),
        check_vma=False,
    )
```

```python
import functools
import math

import jax
import jax.numpy as jnp
import ml_dtypes
import numpy as np
from jax import lax
from jax.experimental import pallas as pl
from jax.experimental.pallas import tpu as pltpu
from jax.sharding import PartitionSpec as P

M = 16
A = 2 * M
MODES = A * M
RB = 8
FOLD = 32
GROUP = 1
F32 = jnp.float32
BF16 = jnp.bfloat16
FULL_TURN = 6.283185307179586
NN = (((1,), (0,)), ((), ()))
NT = (((1,), (1,)), ((), ()))
MIB = 1 << 20
MESH = pl.DeviceIdType.MESH


def trig(frequency, period):
    phases = frequency[:, None] * np.arange(period)[None, :] % period
    angles = phases.astype(np.float32) * np.float32(FULL_TURN / period)
    angles = angles.astype(np.float64)
    return np.cos(angles).astype(np.float32), np.sin(angles).astype(np.float32)


def np_split(x):
    hi = x.astype(ml_dtypes.bfloat16)
    return hi, (x - hi.astype(np.float32)).astype(ml_dtypes.bfloat16)


@functools.lru_cache(maxsize=None)
def tables(n_rows, n_cols):
    frequency = np.arange(A)
    frequency = np.where(frequency < M, frequency, frequency - A)
    rows = np.concatenate(trig(frequency, n_rows), axis=0)
    cos, sin = trig(np.arange(M), n_cols)
    hi, low = np_split(rows)
    rows2 = np.concatenate((hi, low), axis=0)
    rows3 = np.concatenate((hi.T, low.T, hi.T), axis=1)
    hi, low = np_split(np.concatenate((cos, sin), axis=0))
    cols2 = np.concatenate((hi.T, low.T), axis=1)
    hi, low = np_split(np.concatenate((cos, -sin), axis=0))
    wide3 = np.concatenate((hi, hi, low), axis=0)
    return rows2, rows3, cols2, wide3


def split2(x):
    hi = x.astype(BF16)
    return hi, (x - hi.astype(F32)).astype(BF16)


def mm(a, b, dims=NN):
    return lax.dot_general(a, b, dims, preferred_element_type=F32)


def stacked(x, axis):
    hi, low = split2(x)
    return jnp.concatenate((hi.astype(F32), low.astype(F32)), axis=axis).astype(BF16)


def deep_left(x):
    hi = x.astype(BF16).astype(F32)
    return jnp.concatenate((hi, x - hi, hi), axis=1)


def deep_right(x):
    hi = x.astype(BF16).astype(F32)
    return jnp.concatenate((hi, hi, x - hi), axis=0).astype(BF16)


def exact(a, b, dims=NN):
    return lax.dot_general(
        a, b, dims, precision=lax.Precision.HIGHEST, preferred_element_type=F32
    )


def iota(shape, axis):
    return lax.broadcasted_iota(jnp.int32, shape, axis)


def sel(mask):
    return mask.astype(F32)


def pack(dest, vals, out_ref, tiles, cap):
    n = dest.shape[1]
    named = dest == iota((tiles, n), 0)
    before = iota((n, n), 0) < iota((n, n), 1)
    earlier = mm(sel(named).astype(BF16), sel(before).astype(BF16))
    rank = jnp.sum(jnp.where(named, earlier, 0.0), axis=0, keepdims=True)
    position = dest * cap + rank.astype(jnp.int32)
    rows = vals.shape[0]
    hi = vals.astype(BF16)
    left = vals - hi.astype(F32)
    mid = left.astype(BF16)
    low = (left - mid.astype(F32)).astype(BF16)
    parts = jnp.concatenate((hi.astype(F32), mid.astype(F32), low.astype(F32)), axis=0).astype(BF16)
    step = 512
    for first in range(0, tiles * cap, step):
        place = sel(position == iota((step, n), 0) + first).astype(BF16)
        got = mm(parts, place, NT)
        got = got[:rows] + got[rows : 2 * rows] + got[2 * rows : 3 * rows]
        for at in range(0, step, cap):
            out_ref[(first + at) // cap] = got[:, at : at + cap]


def mode_lines(rows2, tall, scale):
    side = tall.shape[1] // 2
    both = mm(rows2, stacked(tall, 1))
    grid = both[: 2 * A, : 2 * side] + both[2 * A :, : 2 * side] + both[: 2 * A, 2 * side :]
    re = (grid[:A, :side] - grid[A:, side:]) * scale
    im = (grid[A:, :side] + grid[:A, side:]) * (-scale)
    return [part[:, at : at + 128] for part in (re, im) for at in range(0, side, 128)]


def part_of(x, size):
    if size & (size - 1) == 0:
        return lax.shift_right_logical(x, size.bit_length() - 1)
    return lax.div(x, size)


def rest_of(x, size):
    if size & (size - 1) == 0:
        return x & (size - 1)
    return lax.rem(x, size)


def as_column(line, first=0, count=None):
    width = line.shape[1]
    shape = (count or width, width)
    picked = jnp.where(iota(shape, 1) == iota(shape, 0) + first, line.astype(F32), 0.0)
    return jnp.sum(picked, axis=1, keepdims=True).astype(jnp.int32)


def same_place():
    return sel(iota((128, 128), 0) % M == iota((128, 128), 1) % M)


def spread8(s8):
    z = jnp.broadcast_to(s8[:, None, :], (8, 8, 128)).reshape(64, 128)
    z = jnp.where(iota((64, 128), 1) // M == iota((64, 128), 0) % 8, z, 0.0)
    z = exact(z, same_place())
    re = jnp.concatenate((z[0:16], z[32:48]), axis=0)
    im = jnp.concatenate((z[16:32], z[48:64]), axis=0)
    return re, im


def compact8(re, im, a):
    y = jnp.concatenate((re, im), axis=0)
    group = iota(y.shape, 1) // M
    y = jnp.where(group == lax.rem(a, 8), y, 0.0)
    y = exact(y, same_place())
    y = jnp.where(group == iota(y.shape, 0) % 8, y, 0.0)
    return jnp.sum(y.reshape(8, 8, 128), axis=1)


def mode_half(re, im, rows3, half_ref):
    grid = jnp.concatenate(
        (jnp.concatenate((re, im), axis=1), jnp.concatenate((-im, re), axis=1)), axis=0
    )
    half = mm(rows3, deep_right(grid))
    side = half.shape[1] // 2
    for o in range(side // M):
        at = o * M
        pair = jnp.concatenate((half[:, at : at + M], half[:, side + at : side + at + M]), axis=1)
        half_ref[o] = deep_left(pair)


def put_tall(tall_ref, first, tall, own):
    for c in range(own):
        for part in range(2):
            at = (part * own + c) * M
            tall_ref[pl.ds(first, RB), at : at + M] = tall[
                c * RB : (c + 1) * RB, part * M : (part + 1) * M
            ]


def col_modes(parts, cols2):
    half = parts.shape[0] // 2
    got = mm(parts, cols2)
    return got[:half, : 2 * M] + got[:half, 2 * M :] + got[half:, : 2 * M]


def main_kernel(
    n_row, n_col, scales,
    dest_ref, cell_ref, res_ref, kept_ref, bias_ref, point_ref, field_ref, w_ref,
    rows2_hbm, rows3_hbm, cols2_hbm, wide3_hbm,
    partial_ref, spec_ref, back_ref, gp_ref,
    rows2_ref, rows3_ref, cols2_ref, wide3_ref, table_sem,
    fbuf, load_sem, wbuf, w_sem, f2_ref, pre_ref, kron2_ref, kronb_ref, tall_ref,
    x1, landed1, send1, gat1, x2, landed2, send2, gat2, rs_send, rs_recv, ag_send, ag_recv,
    grouped, came, trade_send, trade_recv, pts, ids_ref, vm_ref, hot_a, hot_b, cot_ref, half_ref,
    sl_ref, other_ref, swap_send, swap_recv, acc_ref, gpx, gpl, gp_send, gp_recv, out_sem,
):
    forward_scale, mix_scale = scales
    n = n_row * n_col
    count = 2 * n
    stride = count // A
    ch = lax.axis_index("ch")
    me = lax.axis_index("row") * n_col + lax.axis_index("col")
    flat = me * 2 + ch
    a = part_of(flat, stride)
    is_reducer = rest_of(flat, stride) == 0
    small = stride == 1
    steps, inputs, block, width = fbuf.shape
    own = inputs // 2
    rows = own * RB
    height = steps * block
    subs = block // RB
    points = pts.shape[1]

    def device_of(f):
        f = jnp.int32(f)
        p = part_of(f, 2)
        return (part_of(p, n_col), rest_of(p, n_col), rest_of(f, 2))

    def remote(src, dst, send, recv, f):
        return pltpu.make_async_remote_copy(
            src_ref=src, dst_ref=dst, send_sem=send, recv_sem=recv,
            device_id=device_of(f), device_id_type=MESH,
        )

    def some(low, high, body):
        if small:
            for k in range(low, high):
                body(k)
        else:
            each(low, high, body)

    def each(low, high, body):
        def go(k, carry):
            body(k)
            return carry

        lax.fori_loop(low, high, go, 0)

    def on_reducer(body):
        if stride == 1:
            body()
        else:
            pl.when(is_reducer)(body)

    def off_reducer(body):
        if stride > 1:
            pl.when(jnp.logical_not(is_reducer))(body)

    row_at = pl.multiple_of(lax.axis_index("row") * height, 128)
    col_at = pl.multiple_of(lax.axis_index("col") * width, 128)
    table_loads = [
        pltpu.make_async_copy(src, dst, table_sem.at[i])
        for i, (src, dst) in enumerate((
            (rows2_hbm.at[:, pl.ds(row_at, height)], rows2_ref),
            (rows3_hbm.at[pl.ds(row_at, height), :], rows3_ref),
            (cols2_hbm.at[pl.ds(col_at, width), :], cols2_ref),
            (wide3_hbm.at[:, pl.ds(col_at, width)], wide3_ref),
        ))
    ]

    def load(i):
        return pltpu.make_async_copy(
            field_ref.at[:, pl.ds(pl.multiple_of(i * block, block), block), :],
            fbuf.at[i], load_sem.at[i],
        )

    w_load = pltpu.make_async_copy(
        w_ref.at[:, :, :, pl.ds(pl.multiple_of(part_of(a, 8) * 128, 128), 128)], wbuf, w_sem
    )
    for one in table_loads:
        one.start()
    each(0, steps, lambda i: load(i).start())
    w_load.start()

    barrier = pltpu.get_barrier_semaphore()
    some(1, count, lambda k: pl.semaphore_signal(
        barrier, inc=1, device_id=device_of(rest_of(flat + k, count)), device_id_type=MESH
    ))

    shape = (rows, inputs)
    pick = sel(iota(shape, 1) == ch * own + iota(shape, 0) // RB)
    wide_shape = (inputs, inputs * RB)
    spread = sel(iota(wide_shape, 0) == iota(wide_shape, 1) // RB)
    turned = sel(iota(wide_shape, 0) == (iota(wide_shape, 1) // RB + ch * own) % inputs)
    kron_shape = (rows, inputs * RB)
    same = iota(kron_shape, 0) % RB == iota(kron_shape, 1) % RB
    forward_point = exact(exact(pick, point_ref[...], NT), spread)
    kron2_ref[...] = stacked(jnp.where(same, forward_point, 0.0), 0)
    backward_point = exact(exact(pick, point_ref[...]), turned)
    kronb_ref[...] = stacked(jnp.where(same, backward_point, 0.0), 0)
    acc_ref[...] = jnp.zeros_like(acc_ref)
    cells = (cell_ref[...] + 1).astype(F32)
    vals = jnp.concatenate(
        (res_ref[...], jnp.broadcast_to(cells, (8, cells.shape[1]))), axis=0
    )
    cap = grouped.shape[2]
    pack(dest_ref[...], vals, grouped, n, cap)

    for one in table_loads:
        one.wait()

    def front(i):
        load(i).wait()
        for u in range(subs):
            b = i * subs + u
            hi, low = split2(fbuf[i, :, u * RB : (u + 1) * RB, :].reshape(inputs * RB, width))
            f2_ref[b, : inputs * RB, :] = hi
            f2_ref[b, inputs * RB :, :] = low
            at = pl.multiple_of(ch * rows, rows)
            mine = jnp.concatenate(
                (f2_ref[b, pl.ds(at, rows), :], f2_ref[b, pl.ds(at + inputs * RB, rows), :]), axis=0
            )
            put_tall(tall_ref, pl.multiple_of(b * RB, RB), col_modes(mine, cols2_ref[...]), own)

    each(0, steps, front)

    def scatter(x, landed, stage):
        def copy(k):
            to = rest_of(a + k, A)
            target = to * stride
            slot = count - k if small else rest_of(flat - target + count, count)
            return remote(
                x.at[to], landed.at[slot], rs_send.at[stage], rs_recv.at[stage], target
            )

        return copy

    def scatter_start(x, landed, stage, scale):
        lines = mode_lines(rows2_ref[...], tall_ref[...], scale)
        for j, line in enumerate(lines):
            x[:, j, :] = line
        copy = scatter(x, landed, stage)
        if stage == 0:
            pl.semaphore_wait(barrier, count - 1)
        some(1, A, lambda k: copy(k).start())
        off_reducer(lambda: copy(0).start())

    def scatter_end(x, landed, stage):
        def take(slots):
            sent = x.at[pl.ds(0, slots)]
            remote(sent, sent, rs_send.at[stage], rs_recv.at[stage], flat).wait_send()

        on_reducer(lambda: take(A - 1))
        off_reducer(lambda: take(A))

    def reduced(x, landed, stage):
        got = landed.at[pl.ds(1, count - 1)]
        remote(got, got, rs_send.at[stage], rs_recv.at[stage], flat).wait_recv()
        pairs = landed[pl.ds(2, count - 2)].reshape(n - 1, 2, 4, 128)
        pairs = jnp.sum(pairs, axis=0)
        mine = x[a] + pairs[0]
        theirs = landed[1] + pairs[1]
        first = jnp.where(ch == 0, mine, theirs)
        second = jnp.where(ch == 0, theirs, mine)
        return jnp.concatenate((first, second), axis=0)

    def gather(source, gat, stage):
        def copy(k):
            f = rest_of(flat + k, count)
            send = ag_send.at[stage, 0 if small else k]
            return remote(
                source.at[rest_of(ch + k, 2)], gat.at[a], send, ag_recv.at[stage], f
            )

        return copy

    def gather_wait(gat, stage):
        def take(slots):
            got = gat.at[pl.ds(0, slots)]
            remote(got, got, ag_send.at[stage, 0], ag_recv.at[stage], flat).wait_recv()

        on_reducer(lambda: take(A - 1))
        off_reducer(lambda: take(A))

    def gather_end(source, gat, stage):
        if small:
            sent = gat.at[pl.ds(0, A - 1)]
            remote(sent, sent, ag_send.at[stage, 0], ag_recv.at[stage], flat).wait_send()
        else:
            copy = gather(source, gat, stage)
            on_reducer(lambda: each(1, count, lambda k: copy(k).wait_send()))

    rank = jnp.where(a < M, a, A - 1 - a)
    kept = as_column(kept_ref[...])
    allowed = sel((rank < kept) & (iota((inputs, 128), 1) % M < kept))

    scatter_start(x1, landed1, 0, forward_scale)

    def trade(k):
        p = rest_of(me + k, n)
        return remote(grouped.at[p], came.at[k], trade_send, trade_recv, p * 2 + ch)

    some(1, n, lambda k: trade(k).start())
    came[0] = grouped[me]

    def pointwise(i):
        for u in range(subs):
            b = i * subs + u
            both = mm(kron2_ref[...], f2_ref[b, : inputs * RB, :])
            low = f2_ref[b, inputs * RB :, :]
            pre_ref[b] = both[:rows] + both[rows:] + mm(kron2_ref[:rows, :], low)

    each(0, steps, pointwise)

    def mix():
        s8 = reduced(x1, landed1, 0)
        spec_re, spec_im = spread8(s8)
        w_load.wait()
        re = jnp.zeros((inputs, 128), F32)
        im = jnp.zeros((inputs, 128), F32)
        for c in range(inputs):
            one_re, one_im = spec_re[c : c + 1], spec_im[c : c + 1]
            re = re + (wbuf[0, c] * one_re - wbuf[1, c] * one_im)
            im = im + (wbuf[0, c] * one_im + wbuf[1, c] * one_re)
        keep = allowed * mix_scale
        mixed = compact8(re * keep, im * keep, a)
        for d in range(2):
            send1[d, :8] = s8
            send1[d, 8:10] = mixed[2 * d : 2 * d + 2]
            send1[d, 10:12] = mixed[4 + 2 * d : 6 + 2 * d]
        copy = gather(send1, gat1, 0)
        some(1, count, lambda k: copy(k).start())
        gat1[a] = send1[ch]

    on_reducer(mix)
    if stride > 1:
        off_reducer(lambda: w_load.wait())

    came_all = came.at[pl.ds(1, n - 1)]
    remote(came_all, came_all, trade_send, trade_recv, flat).wait_recv()
    for p in range(n):
        pts[:, p * cap : (p + 1) * cap] = came[p]
    cell = pts[own : own + 1, :].astype(jnp.int32) - 1
    row = cell // width
    fold = jnp.where(cell < 0, -1, row % FOLD)
    code = jnp.where(cell < 0, -1, row // FOLD * width + cell % width).astype(F32)
    for first in range(0, points, 128):
        ids_ref[first : first + 128, :] = jnp.broadcast_to(
            code[:, first : first + 128], (128, 128)
        ).T
    here = fold == iota((FOLD, points), 0)
    half_own = own // 2

    def fill(o):
        value = pts[pl.ds(o, 1), :]
        hi = value.astype(BF16).astype(F32)
        group = o // half_own
        at = pl.multiple_of(lax.rem(o, half_own) * FOLD, FOLD)
        vm_ref[group, pl.ds(at, FOLD), :] = jnp.where(here, hi, 0.0).astype(BF16)
        vm_ref[group, pl.ds(at + half_own * FOLD, FOLD), :] = jnp.where(
            here, value - hi, 0.0
        ).astype(BF16)

    each(0, own, fill)
    span = half_own * FOLD

    def name_columns(q, hot_ref):
        for at in range(0, width, 128):
            names = (iota((points, 128), 1) + (q * width + at)).astype(F32)
            hot_ref[:, at : at + 128] = sel(ids_ref[...] == names).astype(BF16)

    def place(q, hot_ref):
        for group in range(2):
            got = mm(vm_ref[group], hot_ref[...])
            got = (got[:span] + got[span:]).reshape(half_own, FOLD, width)
            cot_ref[
                group * half_own : (group + 1) * half_own,
                pl.ds(pl.multiple_of(q * FOLD, FOLD), FOLD), :,
            ] = got

    def place_pair(i):
        name_columns(2 * i + 1, hot_b)
        place(2 * i, hot_a)
        name_columns(2 * i + 2, hot_a)
        place(2 * i + 1, hot_b)

    name_columns(0, hot_a)
    each(0, height // FOLD // 2, place_pair)

    gather_wait(gat1, 0)
    re = jnp.concatenate((gat1[:, 8, :], gat1[:, 9, :]), axis=1)
    im = jnp.concatenate((gat1[:, 10, :], gat1[:, 11, :]), axis=1)
    bias_shape = (own, own * M)
    bias_at = sel(iota(bias_shape, 1) == iota(bias_shape, 0) * M)
    bias_line = exact(jnp.broadcast_to(bias_ref[...], (8, own)), bias_at)[:1]
    re = re + jnp.where(iota(re.shape, 0) == 0, bias_line, 0.0)
    mode_half(re, im, rows3_ref[...], half_ref)

    def swap(i):
        at = pl.ds(i * subs, subs)
        return remote(
            pre_ref.at[at], other_ref.at[at], swap_send, swap_recv.at[i], me * 2 + 1 - ch
        )

    k0 = math.sqrt(2.0 / math.pi)

    def slopes(i):
        for u in range(GROUP * subs):
            b = i * (GROUP * subs) + u
            first = pl.multiple_of(b * RB, RB)
            half = half_ref[:, pl.ds(first, RB), :].reshape(rows, 6 * M).astype(BF16)
            pre = pre_ref[b] + mm(half, wide3_ref[...])
            cot = cot_ref[:, pl.ds(first, RB), :].reshape(rows, width)
            square = pre * pre
            t = jnp.tanh(k0 * pre * (1.0 + 0.044715 * square))
            rate = 0.5 * (1.0 + t) + 0.5 * k0 * pre * (1.0 - t * t) * (1.0 + 3 * 0.044715 * square)
            slope = cot * rate
            pre_ref[b] = slope
            hi, low = split2(slope)
            sl_ref[b, :rows, :] = hi
            sl_ref[b, rows:, :] = low
            put_tall(tall_ref, first, col_modes(sl_ref[b], cols2_ref[...]), own)
            if u % subs == subs - 1:
                swap(i * GROUP + u // subs).start()

    each(0, steps // GROUP, slopes)
    scatter_start(x2, landed2, 1, mix_scale)

    def point_sums(i):
        fields = jnp.concatenate([f2_ref[i * 2 + u] for u in range(2)], axis=1)
        found = jnp.concatenate([sl_ref[i * 2 + u] for u in range(2)], axis=1)
        acc_ref[...] += mm(fields, found, NT)

    each(0, steps * subs // 2, point_sums)
    total = acc_ref[: inputs * RB, :] + acc_ref[inputs * RB :, :]
    total = total[:, :rows] + total[:, rows:]
    matched = iota(total.shape, 0) % RB == iota(total.shape, 1) % RB
    total = jnp.sum(jnp.where(matched, total, 0.0).reshape(inputs, RB, rows), axis=1)
    into = 128 // own
    group = sel(iota((rows, 128), 0) // RB == iota((rows, 128), 1) % own)
    total = exact(total, group)
    mine = iota(total.shape, 1) // own == iota(total.shape, 0) % into
    gpx[...] = jnp.sum(jnp.where(mine, total, 0.0).reshape(inputs // into, into, 128), axis=1)

    def point_send(k):
        p = rest_of(me + k, n)
        return remote(gpx, gpl.at[k], gp_send, gp_recv, p * 2 + ch)

    some(1, n, lambda k: point_send(k).start())

    def adjoint():
        s8 = reduced(x2, landed2, 1)
        grad_re, grad_im = spread8(s8)
        grad_re = grad_re * allowed
        grad_im = grad_im * allowed
        lines_re, lines_im = [], []
        for c in range(inputs):
            w_re, w_im = wbuf[0, c], wbuf[1, c]
            lines_re.append(jnp.sum(w_re * grad_re + w_im * grad_im, axis=0, keepdims=True))
            lines_im.append(jnp.sum(w_re * grad_im - w_im * grad_re, axis=0, keepdims=True))
        re = jnp.concatenate(lines_re, axis=0) * forward_scale
        im = jnp.concatenate(lines_im, axis=0) * forward_scale
        turned_modes = compact8(re, im, a)
        for d in range(2):
            send2[d, :2] = turned_modes[2 * d : 2 * d + 2]
            send2[d, 2:4] = turned_modes[4 + 2 * d : 6 + 2 * d]
            send2[d, 4:8] = s8[4 * d : 4 * d + 4]
        copy = gather(send2, gat2, 1)
        some(1, count, lambda k: copy(k).start())
        gat2[a] = send2[ch]

    on_reducer(adjoint)

    def store(i):
        at = pl.ds(pl.multiple_of(i * block, block), block)
        return pltpu.make_async_copy(cot_ref.at[:, at, :], partial_ref.at[:, at, :], out_sem)

    def backs(i):
        swap(i).wait_recv()
        for u in range(subs):
            b = i * subs + u
            first = pl.multiple_of(b * RB, RB)
            other_hi, other_low = split2(other_ref[b])
            hi = jnp.concatenate((sl_ref[b, :rows, :], other_hi), axis=0)
            low = jnp.concatenate((sl_ref[b, rows:, :], other_low), axis=0)
            both = mm(kronb_ref[...], hi)
            result = both[:rows] + both[rows:] + mm(kronb_ref[:rows, :], low)
            cot_ref[:, pl.ds(first, RB), :] = result.reshape(own, RB, width)
        store(i).start()

    each(0, steps, backs)

    gp_all = gpl.at[pl.ds(1, n - 1)]
    remote(gp_all, gp_all, gp_send, gp_recv, flat).wait_recv()
    gp_ref[...] = gpx[...] + jnp.sum(gpl[pl.ds(1, n - 1)], axis=0)
    gather_wait(gat2, 1)
    spec_ref[...] = gat1[...]
    back_ref[...] = gat2[...]

    scatter_end(x1, landed1, 0)
    scatter_end(x2, landed2, 1)
    gather_end(send1, gat1, 0)
    gather_end(send2, gat2, 1)
    remote(came_all, came_all, trade_send, trade_recv, flat).wait_send()
    remote(gp_all, gp_all, gp_send, gp_recv, flat).wait_send()
    sent = pre_ref.at[pl.ds(0, steps * subs)]
    remote(sent, sent, swap_send, swap_recv.at[0], flat).wait_send()
    pltpu.make_async_copy(cot_ref, partial_ref, out_sem).wait()


def main_pass(args, constants, scales, cap, n_row, n_col):
    field = args[6]
    n = n_row * n_col
    count = 2 * n
    inputs, height, width = field.shape
    own = inputs // 2
    block = 2 * RB
    steps = height // block
    blocks = height // RB
    rows = own * RB
    kept = own + 8
    points = n * cap
    vmem = pl.BlockSpec(memory_space=pltpu.VMEM)
    hbm = pl.BlockSpec(memory_space=pl.ANY)
    dma = pltpu.SemaphoreType.DMA
    rows2, rows3, cols2, wide3 = constants
    return pl.pallas_call(
        functools.partial(main_kernel, n_row, n_col, scales),
        out_shape=[
            jax.ShapeDtypeStruct((own, height, width), F32),
            jax.ShapeDtypeStruct((A, 12, 128), F32),
            jax.ShapeDtypeStruct((A, 8, 128), F32),
            jax.ShapeDtypeStruct((4, 128), F32),
        ],
        in_specs=[vmem] * 6 + [hbm] * 6,
        out_specs=[hbm, vmem, vmem, vmem],
        scratch_shapes=[
            pltpu.VMEM((rows2.shape[0], height), BF16),
            pltpu.VMEM((height, rows3.shape[1]), BF16),
            pltpu.VMEM((width, cols2.shape[1]), BF16),
            pltpu.VMEM((wide3.shape[0], width), BF16),
            dma((4,)),
            pltpu.VMEM((steps, inputs, block, width), F32),
            dma((steps,)),
            pltpu.VMEM((2, inputs, inputs, 128), F32),
            dma,
            pltpu.VMEM((blocks, 2 * inputs * RB, width), BF16),
            pltpu.VMEM((blocks, rows, width), F32),
            pltpu.VMEM((2 * rows, inputs * RB), BF16),
            pltpu.VMEM((2 * rows, inputs * RB), BF16),
            pltpu.VMEM((height, 2 * own * M), F32),
            pltpu.VMEM((A, 4, 128), F32),
            pltpu.VMEM((count, 4, 128), F32),
            pltpu.VMEM((2, 12, 128), F32),
            pltpu.VMEM((A, 12, 128), F32),
            pltpu.VMEM((A, 4, 128), F32),
            pltpu.VMEM((count, 4, 128), F32),
            pltpu.VMEM((2, 8, 128), F32),
            pltpu.VMEM((A, 8, 128), F32),
            dma((2,)),
            dma((2,)),
            dma((2, count)),
            dma((2,)),
            pltpu.VMEM((n, kept, cap), F32),
            pltpu.VMEM((n, kept, cap), F32),
            dma,
            dma,
            pltpu.VMEM((kept, points), F32),
            pltpu.VMEM((points, 128), F32),
            pltpu.VMEM((2, own * FOLD, points), BF16),
            pltpu.VMEM((points, width), BF16),
            pltpu.VMEM((points, width), BF16),
            pltpu.VMEM((own, height, width), F32),
            pltpu.VMEM((own, height, 6 * M), F32),
            pltpu.VMEM((blocks, 2 * rows, width), BF16),
            pltpu.VMEM((blocks, rows, width), F32),
            dma,
            dma((steps,)),
            pltpu.VMEM((2 * inputs * RB, 2 * rows), F32),
            pltpu.VMEM((4, 128), F32),
            pltpu.VMEM((n, 4, 128), F32),
            dma,
            dma,
            dma,
        ],
        compiler_params=pltpu.CompilerParams(
            collective_id=0, has_side_effects=True, vmem_limit_bytes=58 * MIB
        ),
    )(*args, *constants)


def turn_blocks(x):
    group = iota((8, 128), 1) // M
    line = iota((8, 128), 0)
    out = jnp.where(group == line, x, 0.0)
    for d in range(1, 8):
        y = pltpu.roll(pltpu.roll(x, d * M, 1), 8 - d, 0)
        out = jnp.where((group - line + 8) % 8 == d, y, out)
    return out


def back_kernel(
    scales, partial_ref, spec_ref, back_ref, gp_ref, kept_ref, rows3_hbm, wide3_hbm,
    out_ref, gs_ref, point_ref, bias_ref,
    half_ref, spec_t, grad_t, point_t, rows3_ref, wide3_ref, table_sem,
    held, load_sem, made, out_sem, gs_sem,
):
    grad_scale, norm_points, bias_scale = scales
    steps, own, block, width = held.shape
    rows = own * RB
    height = steps * block
    inputs = 2 * own
    each_c = inputs // steps

    def load(i):
        at = pl.ds(pl.multiple_of(i * block, block), block)
        return pltpu.make_async_copy(partial_ref.at[:, at, :], held.at[i], load_sem.at[i])

    def store(i):
        at = pl.ds(pl.multiple_of(i * block, block), block)
        return pltpu.make_async_copy(held.at[i], out_ref.at[:, at, :], out_sem.at[i])

    def store_gs(i):
        at = pl.ds(i * each_c, each_c)
        return pltpu.make_async_copy(made.at[:, at], gs_ref.at[:, at], gs_sem.at[i])

    def each(low, high, body):
        def go(k, carry):
            body(k)
            return carry

        lax.fori_loop(low, high, go, 0)

    row_at = pl.multiple_of(lax.axis_index("row") * height, 128)
    col_at = pl.multiple_of(lax.axis_index("col") * width, 128)
    loads = [
        pltpu.make_async_copy(rows3_hbm.at[pl.ds(row_at, height), :], rows3_ref, table_sem.at[0]),
        pltpu.make_async_copy(wide3_hbm.at[:, pl.ds(col_at, width)], wide3_ref, table_sem.at[1]),
    ]
    for one in loads:
        one.start()
    each(0, steps, lambda i: load(i).start())
    kept = as_column(kept_ref[...], lax.axis_index("ch") * own, own)
    mode = iota((own, MODES), 1)
    row_mode = mode // M
    rank = jnp.where(row_mode < M, row_mode, A - 1 - row_mode)
    keep = jnp.where((rank < kept) & (mode % M < kept), grad_scale, 0.0)
    biases = jnp.zeros((1, own), F32)
    for part in range(2):
        for octet in range(own // 8):
            j = part * (own // 8) + octet
            for t in range(A // 8):
                lanes = slice(t * 128, (t + 1) * 128)
                lines = slice(octet * 8, octet * 8 + 8)
                got = turn_blocks(back_ref[t * 8 : t * 8 + 8, 4 + j, :])
                if part == 0 and t == 0:
                    shape = (8, own)
                    named = iota(shape, 1) == iota(shape, 0) + octet * 8
                    named = jnp.where(named, got[:, :1] * bias_scale, 0.0)
                    biases = biases + jnp.sum(named, axis=0, keepdims=True)
                grad_t[part, lines, lanes] = got * keep[lines, lanes]
                for side in range(2):
                    at = side * own + octet * 8
                    spec_t[part, at : at + 8, lanes] = turn_blocks(
                        spec_ref[t * 8 : t * 8 + 8, side * 4 + j, :]
                    )

    def spectral(i):
        for u in range(each_c):
            c = i * each_c + u
            spec_re = spec_t[0, pl.ds(c, 1), :]
            spec_im = spec_t[1, pl.ds(c, 1), :]
            made[0, c] = grad_t[0] * spec_re + grad_t[1] * spec_im
            made[1, c] = grad_t[1] * spec_re - grad_t[0] * spec_im
        store_gs(i).start()

    each(0, steps, spectral)
    for one in loads:
        one.wait()
    re = jnp.concatenate((back_ref[:, 0, :], back_ref[:, 1, :]), axis=1)
    im = jnp.concatenate((back_ref[:, 2, :], back_ref[:, 3, :]), axis=1)
    mode_half(re, im, rows3_ref[...], half_ref)

    def fields(i):
        load(i).wait()
        for u in range(block // RB):
            at = slice(u * RB, (u + 1) * RB)
            first = pl.multiple_of(i * block + u * RB, RB)
            half = half_ref[:, pl.ds(first, RB), :].reshape(rows, 6 * M).astype(BF16)
            result = mm(half, wide3_ref[...]).reshape(own, RB, width)
            held[i, :, at, :] = held[i, :, at, :] + result
        store(i).start()

    each(0, steps, fields)
    bias_ref[...] = biases
    gp = gp_ref[...] * norm_points
    into = 128 // own
    for k in range(into):
        for i in range(inputs // into):
            at = i * into + k
            point_t[at : at + 1, :] = gp[i : i + 1, k * own : (k + 1) * own]
    eye = sel(iota((own, own), 0) == iota((own, own), 1))
    point_ref[...] = exact(eye, point_t[...], NT)
    each(0, steps, lambda i: store(i).wait())
    each(0, steps, lambda i: store_gs(i).wait())


def back_pass(partial, spec, back, gp, kept, rows3, wide3, scales):
    own, height, width = partial.shape
    block = 4 * RB
    steps = height // block
    hbm = pl.BlockSpec(memory_space=pl.ANY)
    vmem = pl.BlockSpec(memory_space=pltpu.VMEM)
    dma = pltpu.SemaphoreType.DMA
    return pl.pallas_call(
        functools.partial(back_kernel, scales),
        in_specs=[hbm, vmem, vmem, vmem, vmem, hbm, hbm],
        out_specs=[hbm, hbm, vmem, vmem],
        out_shape=[
            jax.ShapeDtypeStruct((own, height, width), F32),
            jax.ShapeDtypeStruct((2, 2 * own, own, MODES), F32),
            jax.ShapeDtypeStruct((own, 2 * own), F32),
            jax.ShapeDtypeStruct((1, own), F32),
        ],
        scratch_shapes=[
            pltpu.VMEM((own, height, 6 * M), F32),
            pltpu.VMEM((2, 2 * own, MODES), F32),
            pltpu.VMEM((2, own, MODES), F32),
            pltpu.VMEM((2 * own, own), F32),
            pltpu.VMEM((height, rows3.shape[1]), BF16),
            pltpu.VMEM((wide3.shape[0], width), BF16),
            dma((2,)),
            pltpu.VMEM((steps, own, block, width), F32),
            dma((steps,)),
            pltpu.VMEM((2, 2 * own, own, MODES), F32),
            dma((steps,)),
            dma((steps,)),
        ],
        compiler_params=pltpu.CompilerParams(vmem_limit_bytes=58 * MIB),
    )(partial, spec, back, gp, kept, rows3, wide3)


def per_device(
    field, spec_weight, point_weight, bias, kept_modes, residual, trace_dest, trace_cell
):
    n_row = lax.axis_size("row")
    n_col = lax.axis_size("col")
    inputs, height, width = field.shape
    own = inputs // lax.axis_size("ch")
    points = trace_dest.shape[0]
    tiles = n_row * n_col
    points_all = points * tiles
    cap = max(2, 2 * points // tiles)
    forward_scale = 1.0 / math.sqrt(height * n_row * width * n_col)
    mix_scale = 1.0 / math.sqrt(MODES)
    norm_points = 1.0 / math.sqrt(points_all)
    constants = [jnp.asarray(t) for t in tables(height * n_row, width * n_col)]
    kept = kept_modes.reshape(1, inputs)
    args = (
        trace_dest.reshape(1, points), trace_cell.reshape(1, points), residual, kept,
        bias.reshape(1, own), point_weight, field, spec_weight,
    )
    partial, spec, back, gp = main_pass(
        args, constants, (forward_scale, mix_scale), cap, n_row, n_col
    )
    grad_field, grad_spec, grad_point, grad_bias = back_pass(
        partial, spec, back, gp, kept, constants[1], constants[3],
        (math.sqrt(MODES / points_all), norm_points, norm_points / mix_scale),
    )
    return (grad_field, grad_spec, grad_point.T, grad_bias.reshape(own))


def solution(mesh):
    return jax.shard_map(
        per_device,
        mesh=mesh,
        in_specs=(
            P(None, "row", "col"),
            P(),
            P(),
            P("ch"),
            P(),
            P("ch", ("row", "col")),
            P(("row", "col"), None),
            P(("row", "col")),
        ),
        out_specs=(P("ch", "row", "col"), P(None, None, "ch", None), P(None, "ch"), P("ch")),
        check_vma=False,
    )
```

```python
import functools
import math

import jax
import jax.numpy as jnp
import ml_dtypes
import numpy as np
from jax import lax
from jax.experimental import pallas as pl
from jax.experimental.pallas import tpu as pltpu
from jax.sharding import PartitionSpec as P

M = 16
A = 2 * M
MODES = A * M
RB = 8
FOLD = 32
F32 = jnp.float32
BF16 = jnp.bfloat16
FULL_TURN = 6.283185307179586
NN = (((1,), (0,)), ((), ()))
NT = (((1,), (1,)), ((), ()))
MIB = 1 << 20
MESH = pl.DeviceIdType.MESH


def trig(frequency, period):
    phases = frequency[:, None] * np.arange(period)[None, :] % period
    angles = phases.astype(np.float32) * np.float32(FULL_TURN / period)
    angles = angles.astype(np.float64)
    return np.cos(angles).astype(np.float32), np.sin(angles).astype(np.float32)


def np_split(x):
    hi = x.astype(ml_dtypes.bfloat16)
    return hi, (x - hi.astype(np.float32)).astype(ml_dtypes.bfloat16)


@functools.lru_cache(maxsize=None)
def tables(n_rows, n_cols):
    frequency = np.arange(A)
    frequency = np.where(frequency < M, frequency, frequency - A)
    rows = np.concatenate(trig(frequency, n_rows), axis=0)
    cos, sin = trig(np.arange(M), n_cols)
    hi, low = np_split(rows)
    rows2 = np.concatenate((hi, low), axis=0)
    rows3 = np.concatenate((hi.T, low.T, hi.T), axis=1)
    hi, low = np_split(np.concatenate((cos, sin), axis=0))
    gap = np.zeros((n_cols, 128 - 2 * M), ml_dtypes.bfloat16)
    cols2 = np.concatenate((hi.T, gap, low.T, gap), axis=1)
    hi, low = np_split(np.concatenate((cos, -sin), axis=0))
    wide3 = np.concatenate([hi] * 8 + [low] * 4, axis=0)
    return rows2, rows3, cols2, wide3


def split2(x):
    hi = x.astype(BF16)
    return hi, (x - hi.astype(F32)).astype(BF16)


def mm(a, b, dims=NN):
    return lax.dot_general(a, b, dims, preferred_element_type=F32)


def stacked(x, axis):
    hi, low = split2(x)
    return jnp.concatenate((hi.astype(F32), low.astype(F32)), axis=axis).astype(BF16)


def deep_right(x):
    hi = x.astype(BF16).astype(F32)
    return jnp.concatenate((hi, hi, x - hi), axis=0).astype(BF16)


def exact(a, b, dims=NN):
    return lax.dot_general(
        a, b, dims, precision=lax.Precision.HIGHEST, preferred_element_type=F32
    )


def iota(shape, axis):
    return lax.broadcasted_iota(jnp.int32, shape, axis)


def sel(mask):
    return mask.astype(F32)


def pack(dest, vals, out_ref, tiles, cap):
    n = dest.shape[1]
    named = dest == iota((tiles, n), 0)
    before = iota((n, n), 0) < iota((n, n), 1)
    earlier = mm(sel(named).astype(BF16), sel(before).astype(BF16))
    rank = jnp.sum(jnp.where(named, earlier, 0.0), axis=0, keepdims=True)
    position = dest * cap + rank.astype(jnp.int32)
    rows = vals.shape[0]
    hi = vals.astype(BF16)
    left = vals - hi.astype(F32)
    mid = left.astype(BF16)
    low = (left - mid.astype(F32)).astype(BF16)
    parts = jnp.concatenate((hi.astype(F32), mid.astype(F32), low.astype(F32)), axis=0).astype(BF16)
    step = 512
    for first in range(0, tiles * cap, step):
        place = sel(position == iota((step, n), 0) + first).astype(BF16)
        got = mm(parts, place, NT)
        got = got[:rows] + got[rows : 2 * rows] + got[2 * rows : 3 * rows]
        for at in range(0, step, cap):
            out_ref[(first + at) // cap] = got[:, at : at + cap]


def mode_lines(rows2, tall_ref, x_ref, scale):
    height = tall_ref.shape[0] * RB
    for o in range(tall_ref.shape[1] // RB):
        tall = tall_ref[:, o * RB : (o + 1) * RB, :].reshape(height, 2 * M)
        hi, low = split2(tall)
        both = mm(rows2, hi)
        grid = both[: 2 * A] + both[2 * A :] + mm(rows2[: 2 * A], low)
        re = (grid[:A, :M] - grid[A:, M:]) * scale
        im = (grid[A:, :M] + grid[:A, M:]) * (-scale)
        octet, at = o // 8, o % 8 * M
        x_ref[:, octet, at : at + M] = re
        x_ref[:, 2 + octet, at : at + M] = im


def part_of(x, size):
    if size & (size - 1) == 0:
        return lax.shift_right_logical(x, size.bit_length() - 1)
    return lax.div(x, size)


def rest_of(x, size):
    if size & (size - 1) == 0:
        return x & (size - 1)
    return lax.rem(x, size)


def as_column(line, first=0, count=None):
    width = line.shape[1]
    shape = (count or width, width)
    picked = jnp.where(iota(shape, 1) == iota(shape, 0) + first, line.astype(F32), 0.0)
    return jnp.sum(picked, axis=1, keepdims=True).astype(jnp.int32)


def same_place():
    return sel(iota((128, 128), 0) % M == iota((128, 128), 1) % M)


def spread8(s8):
    z = jnp.broadcast_to(s8[:, None, :], (8, 8, 128)).reshape(64, 128)
    z = jnp.where(iota((64, 128), 1) // M == iota((64, 128), 0) % 8, z, 0.0)
    z = exact(z, same_place())
    re = jnp.concatenate((z[0:16], z[32:48]), axis=0)
    im = jnp.concatenate((z[16:32], z[48:64]), axis=0)
    return re, im


def compact8(re, im, a):
    group = iota(re.shape, 1) // M
    mine = group == rest_of(a, 8)
    pair = jnp.concatenate((jnp.where(mine, re, 0.0), jnp.where(mine, im, 0.0)), axis=0)
    pair = exact(pair, same_place())
    count = re.shape[0]
    want = iota(re.shape, 0) % 4 * 2
    y = jnp.where(group == want, pair[:count], jnp.where(group == want + 1, pair[count:], 0.0))
    fours = sel(iota((8, count), 0) == iota((8, count), 1) // 4)
    return exact(fours, y)


def mode_half(lines, rows3, half_ref):
    for q, x in enumerate(lines):
        lane = iota(x.shape, 1)
        low_half = lane % (2 * M) < M
        y = jnp.where(low_half, -pltpu.roll(x, 128 - M, 1), pltpu.roll(x, M, 1))
        half = mm(rows3, deep_right(jnp.concatenate((x, y), axis=0)))
        own = iota(half.shape, 1) // (2 * M)
        for k in range(4):
            half_ref[q * 4 + k] = jnp.where(own == k, half, 0.0)


def from_half(half, wide3):
    hi, low = split2(half)
    return mm(jnp.concatenate((hi, low), axis=1), wide3[:256]) + mm(hi, wide3[256:])


def col_modes(parts, cols2):
    half = parts.shape[0] // 2
    got = mm(parts, cols2)
    return got[:half, : 2 * M] + got[:half, 128 : 128 + 2 * M] + got[half:, : 2 * M]


def main_kernel(
    n_row, n_col, scales,
    dest_ref, cell_ref, res_ref, kept_ref, bias_ref, point_ref, field_ref, w_ref,
    rows2_hbm, rows3_hbm, cols2_hbm, wide3_hbm,
    partial_ref, spec_ref, back_ref, gp_ref,
    rows2_ref, rows3_ref, cols2_ref, wide3_ref, table_sem,
    fbuf, load_sem, wbuf, w_sem, f2_ref, pre_ref, kron2_ref, kronb_ref, tall_ref,
    x1, landed1, send1, gat1, x2, landed2, send2, gat2, rs_send, rs_recv, ag_send, ag_recv,
    grouped, came, trade_send, trade_recv, pts, ids_ref, vm_ref, hot_a, hot_b, cot_ref, half_ref,
    sl_ref, other_ref, swap_send, swap_recv, acc_ref, gpx, gpl, gp_send, gp_recv, out_sem,
):
    forward_scale, mix_scale = scales
    n = n_row * n_col
    count = 2 * n
    stride = count // A
    ch = lax.axis_index("ch")
    me = lax.axis_index("row") * n_col + lax.axis_index("col")
    flat = me * 2 + ch
    a = part_of(flat, stride)
    is_reducer = rest_of(flat, stride) == 0
    small = stride == 1
    steps, inputs, block, width = fbuf.shape
    own = inputs // 2
    rows = own * RB
    height = steps * block
    subs = block // RB
    points = pts.shape[1]

    def device_of(f):
        f = jnp.int32(f)
        p = part_of(f, 2)
        return (part_of(p, n_col), rest_of(p, n_col), rest_of(f, 2))

    def remote(src, dst, send, recv, f):
        return pltpu.make_async_remote_copy(
            src_ref=src, dst_ref=dst, send_sem=send, recv_sem=recv,
            device_id=device_of(f), device_id_type=MESH,
        )

    def some(low, high, body):
        if small:
            for k in range(low, high):
                body(k)
        else:
            each(low, high, body)

    def each(low, high, body):
        def go(k, carry):
            body(k)
            return carry

        lax.fori_loop(low, high, go, 0)

    def on_reducer(body):
        if stride == 1:
            body()
        else:
            pl.when(is_reducer)(body)

    def off_reducer(body):
        if stride > 1:
            pl.when(jnp.logical_not(is_reducer))(body)

    row_at = pl.multiple_of(lax.axis_index("row") * height, 128)
    col_at = pl.multiple_of(lax.axis_index("col") * width, 128)
    table_loads = [
        pltpu.make_async_copy(src, dst, table_sem.at[i])
        for i, (src, dst) in enumerate((
            (rows2_hbm.at[:, pl.ds(row_at, height)], rows2_ref),
            (rows3_hbm.at[pl.ds(row_at, height), :], rows3_ref),
            (cols2_hbm.at[pl.ds(col_at, width), :], cols2_ref),
            (wide3_hbm.at[:, pl.ds(col_at, width)], wide3_ref),
        ))
    ]

    def load(i):
        return pltpu.make_async_copy(
            field_ref.at[:, pl.ds(pl.multiple_of(i * block, block), block), :],
            fbuf.at[i], load_sem.at[i],
        )

    w_load = pltpu.make_async_copy(
        w_ref.at[:, :, :, pl.ds(pl.multiple_of(part_of(a, 8) * 128, 128), 128)], wbuf, w_sem
    )
    for one in table_loads:
        one.start()
    each(0, steps, lambda i: load(i).start())
    w_load.start()

    barrier = pltpu.get_barrier_semaphore()
    some(1, count, lambda k: pl.semaphore_signal(
        barrier, inc=1, device_id=device_of(rest_of(flat + k, count)), device_id_type=MESH
    ))

    shape = (rows, inputs)
    pick = sel(iota(shape, 1) == ch * own + iota(shape, 0) // RB)
    wide_shape = (inputs, inputs * RB)
    spread = sel(iota(wide_shape, 0) == iota(wide_shape, 1) // RB)
    turned = sel(iota(wide_shape, 0) == (iota(wide_shape, 1) // RB + ch * own) % inputs)
    kron_shape = (rows, inputs * RB)
    same = iota(kron_shape, 0) % RB == iota(kron_shape, 1) % RB
    forward_point = exact(exact(pick, point_ref[...], NT), spread)
    kron2_ref[...] = stacked(jnp.where(same, forward_point, 0.0), 0)
    backward_point = exact(exact(pick, point_ref[...]), turned)
    kronb_ref[...] = stacked(jnp.where(same, backward_point, 0.0), 0)
    acc_ref[...] = jnp.zeros_like(acc_ref)
    cells = (cell_ref[...] + 1).astype(F32)
    vals = jnp.concatenate(
        (res_ref[...], jnp.broadcast_to(cells, (8, cells.shape[1]))), axis=0
    )
    cap = grouped.shape[2]
    pack(dest_ref[...], vals, grouped, n, cap)
    pl.semaphore_wait(barrier, count - 1)

    def trade(k):
        p = rest_of(me + k, n)
        return remote(grouped.at[p], came.at[k], trade_send, trade_recv, p * 2 + ch)

    some(1, n, lambda k: trade(k).start())
    came[0] = grouped[me]


    for one in table_loads:
        one.wait()

    def front(i):
        load(i).wait()
        for u in range(subs):
            b = i * subs + u
            hi, low = split2(fbuf[i, :, u * RB : (u + 1) * RB, :].reshape(inputs * RB, width))
            f2_ref[b, : inputs * RB, :] = hi
            f2_ref[b, inputs * RB :, :] = low

    def front_modes(i):
        at = pl.multiple_of(ch * rows, rows)
        for u in range(subs):
            b = i * subs + u
            mine = jnp.concatenate(
                (f2_ref[b, pl.ds(at, rows), :], f2_ref[b, pl.ds(at + inputs * RB, rows), :]), axis=0
            )
            tall_ref[b] = col_modes(mine, cols2_ref[...])

    def front_next(i):
        front(i)
        front_modes(i - 1)

    front(0)
    each(1, steps, front_next)
    front_modes(steps - 1)

    def scatter(x, landed, stage):
        def copy(k):
            to = rest_of(a + k, A)
            target = to * stride
            slot = count - k if small else rest_of(flat - target + count, count)
            return remote(
                x.at[to], landed.at[slot], rs_send.at[stage], rs_recv.at[stage], target
            )

        return copy

    def scatter_start(x, landed, stage, scale):
        mode_lines(rows2_ref[...], tall_ref, x, scale)
        copy = scatter(x, landed, stage)
        some(1, A, lambda k: copy(k).start())
        off_reducer(lambda: copy(0).start())

    def scatter_end(x, landed, stage):
        def take(slots):
            sent = x.at[pl.ds(0, slots)]
            remote(sent, sent, rs_send.at[stage], rs_recv.at[stage], flat).wait_send()

        on_reducer(lambda: take(A - 1))
        off_reducer(lambda: take(A))

    def reduced(x, landed, stage):
        got = landed.at[pl.ds(1, count - 1)]
        remote(got, got, rs_send.at[stage], rs_recv.at[stage], flat).wait_recv()
        pairs = landed[pl.ds(2, count - 2)].reshape(n - 1, 2, 4, 128)
        pairs = jnp.sum(pairs, axis=0)
        mine = x[a] + pairs[0]
        theirs = landed[1] + pairs[1]
        first = jnp.where(ch == 0, mine, theirs)
        second = jnp.where(ch == 0, theirs, mine)
        return jnp.concatenate((first, second), axis=0)

    def gather(source, gat, stage):
        def copy(k):
            f = rest_of(flat + k, count)
            send = ag_send.at[stage, 0 if small else k]
            return remote(
                source.at[rest_of(ch + k, 2)], gat.at[a], send, ag_recv.at[stage], f
            )

        return copy

    def gather_wait(gat, stage):
        def take(slots):
            got = gat.at[pl.ds(0, slots)]
            remote(got, got, ag_send.at[stage, 0], ag_recv.at[stage], flat).wait_recv()

        on_reducer(lambda: take(A - 1))
        off_reducer(lambda: take(A))

    def gather_end(source, gat, stage):
        if small:
            sent = gat.at[pl.ds(0, A - 1)]
            remote(sent, sent, ag_send.at[stage, 0], ag_recv.at[stage], flat).wait_send()
        else:
            copy = gather(source, gat, stage)
            on_reducer(lambda: each(1, count, lambda k: copy(k).wait_send()))

    rank = jnp.where(a < M, a, A - 1 - a)
    kept = as_column(kept_ref[...])
    allowed = sel((rank < kept) & (iota((inputs, 128), 1) % M < kept))

    scatter_start(x1, landed1, 0, forward_scale)

    def pointwise(i):
        for u in range(subs):
            b = i * subs + u
            both = mm(kron2_ref[...], f2_ref[b, : inputs * RB, :])
            low = f2_ref[b, inputs * RB :, :]
            pre_ref[b] = both[:rows] + both[rows:] + mm(kron2_ref[:rows, :], low)

    each(0, steps, pointwise)

    came_all = came.at[pl.ds(1, n - 1)]
    remote(came_all, came_all, trade_send, trade_recv, flat).wait_recv()
    for p in range(n):
        pts[:, p * cap : (p + 1) * cap] = came[p]
    cell = pts[own : own + 1, :].astype(jnp.int32) - 1
    row = cell // width
    fold = jnp.where(cell < 0, -1, row % FOLD)
    code = jnp.where(cell < 0, -1, row // FOLD * width + cell % width).astype(F32)
    for first in range(0, points, 128):
        ids_ref[first : first + 128, :] = jnp.broadcast_to(
            code[:, first : first + 128], (128, 128)
        ).T
    here = fold == iota((FOLD, points), 0)
    half_own = own // 2

    def fill(o):
        value = pts[pl.ds(o, 1), :]
        hi = value.astype(BF16).astype(F32)
        group = o // half_own
        at = pl.multiple_of(lax.rem(o, half_own) * FOLD, FOLD)
        vm_ref[group, pl.ds(at, FOLD), :] = jnp.where(here, hi, 0.0).astype(BF16)
        vm_ref[group, pl.ds(at + half_own * FOLD, FOLD), :] = jnp.where(
            here, value - hi, 0.0
        ).astype(BF16)

    each(0, own, fill)

    span = half_own * FOLD

    def name_columns(q, hot_ref):
        for at in range(0, width, 128):
            names = (iota((points, 128), 1) + (q * width + at)).astype(F32)
            hot_ref[:, at : at + 128] = sel(ids_ref[...] == names).astype(BF16)

    name_columns(0, hot_a)

    def mix():
        s8 = reduced(x1, landed1, 0)
        spec_re, spec_im = spread8(s8)
        w_load.wait()
        re = jnp.zeros((inputs, 128), F32)
        im = jnp.zeros((inputs, 128), F32)
        for c in range(inputs):
            one_re, one_im = spec_re[c : c + 1], spec_im[c : c + 1]
            re = re + (wbuf[0, c] * one_re - wbuf[1, c] * one_im)
            im = im + (wbuf[0, c] * one_im + wbuf[1, c] * one_re)
        keep = allowed * mix_scale
        mixed = compact8(re * keep, im * keep, a)
        for d in range(2):
            send1[d, :8] = s8
            send1[d, 8:12] = mixed[4 * d : 4 * d + 4]
        copy = gather(send1, gat1, 0)
        some(1, count, lambda k: copy(k).start())
        gat1[a] = send1[ch]

    on_reducer(mix)
    if stride > 1:
        off_reducer(lambda: w_load.wait())

    def place(q, hot_ref):
        for group in range(2):
            got = mm(vm_ref[group], hot_ref[...])
            got = (got[:span] + got[span:]).reshape(half_own, FOLD, width)
            cot_ref[
                group * half_own : (group + 1) * half_own,
                pl.ds(pl.multiple_of(q * FOLD, FOLD), FOLD), :,
            ] = got

    def place_pair(i):
        name_columns(2 * i + 1, hot_b)
        place(2 * i, hot_a)
        name_columns(2 * i + 2, hot_a)
        place(2 * i + 1, hot_b)

    each(0, height // FOLD // 2, place_pair)

    gather_wait(gat1, 0)
    bias_shape = (own, own * 2 * M)
    bias_at = sel(iota(bias_shape, 1) == iota(bias_shape, 0) * (2 * M))
    bias_line = exact(jnp.broadcast_to(bias_ref[...], (8, own)), bias_at)[:1]
    first_mode = iota((A, 128), 0) == 0
    mode_half(
        [
            gat1[:, 8 + q, :]
            + jnp.where(first_mode, bias_line[:, q * 128 : (q + 1) * 128], 0.0)
            for q in range(4)
        ],
        rows3_ref[...], half_ref,
    )

    def swap(i):
        at = pl.ds(i * subs, subs)
        return remote(
            pre_ref.at[at], other_ref.at[at], swap_send, swap_recv.at[i], me * 2 + 1 - ch
        )

    k0 = math.sqrt(2.0 / math.pi)

    def slopes(i):
        for u in range(subs):
            b = i * subs + u
            first = pl.multiple_of(b * RB, RB)
            half = half_ref[:, pl.ds(first, RB), :].reshape(rows, 128)
            pre = pre_ref[b] + from_half(half, wide3_ref)
            cot = cot_ref[:, pl.ds(first, RB), :].reshape(rows, width)
            square = pre * pre
            t = jnp.tanh(k0 * pre * (1.0 + 0.044715 * square))
            rate = 0.5 * (1.0 + t) + 0.5 * k0 * pre * (1.0 - t * t) * (1.0 + 3 * 0.044715 * square)
            slope = cot * rate
            pre_ref[b] = slope
            hi, low = split2(slope)
            sl_ref[b, :rows, :] = hi
            sl_ref[b, rows:, :] = low
            if u % subs == subs - 1:
                swap(i).start()

    def slope_modes(i):
        for u in range(subs):
            b = i * subs + u
            tall_ref[b] = col_modes(sl_ref[b], cols2_ref[...])

    def slopes_next(i):
        slope_modes(i - 1)
        slopes(i)

    slopes(0)
    each(1, steps, slopes_next)
    slope_modes(steps - 1)
    scatter_start(x2, landed2, 1, mix_scale)

    def point_sums(i):
        fields = jnp.concatenate([f2_ref[i * 2 + u] for u in range(2)], axis=1)
        found = jnp.concatenate([sl_ref[i * 2 + u] for u in range(2)], axis=1)
        acc_ref[...] += mm(fields, found, NT)

    each(0, steps * subs // 2, point_sums)
    total = acc_ref[: inputs * RB, :] + acc_ref[inputs * RB :, :]
    total = total[:, :rows] + total[:, rows:]
    matched = iota(total.shape, 0) % RB == iota(total.shape, 1) % RB
    total = jnp.sum(jnp.where(matched, total, 0.0).reshape(inputs, RB, rows), axis=1)
    into = 128 // own
    group = sel(iota((rows, 128), 0) // RB == iota((rows, 128), 1) % own)
    total = exact(total, group)
    mine = iota(total.shape, 1) // own == iota(total.shape, 0) % into
    gpx[...] = jnp.sum(jnp.where(mine, total, 0.0).reshape(inputs // into, into, 128), axis=1)

    def point_send(k):
        p = rest_of(me + k, n)
        return remote(gpx, gpl.at[k], gp_send, gp_recv, p * 2 + ch)

    some(1, n, lambda k: point_send(k).start())

    def adjoint():
        s8 = reduced(x2, landed2, 1)
        grad_re, grad_im = spread8(s8)
        grad_re = grad_re * allowed
        grad_im = grad_im * allowed
        lines_re, lines_im = [], []
        for c in range(inputs):
            w_re, w_im = wbuf[0, c], wbuf[1, c]
            lines_re.append(jnp.sum(w_re * grad_re + w_im * grad_im, axis=0, keepdims=True))
            lines_im.append(jnp.sum(w_re * grad_im - w_im * grad_re, axis=0, keepdims=True))
        re = jnp.concatenate(lines_re, axis=0) * forward_scale
        im = jnp.concatenate(lines_im, axis=0) * forward_scale
        turned_modes = compact8(re, im, a)
        for d in range(2):
            send2[d, :4] = turned_modes[4 * d : 4 * d + 4]
            send2[d, 4:8] = s8[4 * d : 4 * d + 4]
        copy = gather(send2, gat2, 1)
        some(1, count, lambda k: copy(k).start())
        gat2[a] = send2[ch]

    on_reducer(adjoint)

    def store(i):
        at = pl.ds(pl.multiple_of(i * block, block), block)
        return pltpu.make_async_copy(cot_ref.at[:, at, :], partial_ref.at[:, at, :], out_sem)

    def backs(i):
        swap(i).wait_recv()
        for u in range(subs):
            b = i * subs + u
            first = pl.multiple_of(b * RB, RB)
            other_hi, other_low = split2(other_ref[b])
            hi = jnp.concatenate((sl_ref[b, :rows, :], other_hi), axis=0)
            low = jnp.concatenate((sl_ref[b, rows:, :], other_low), axis=0)
            both = mm(kronb_ref[...], hi)
            result = both[:rows] + both[rows:] + mm(kronb_ref[:rows, :], low)
            cot_ref[:, pl.ds(first, RB), :] = result.reshape(own, RB, width)
        store(i).start()

    each(0, steps, backs)

    gp_all = gpl.at[pl.ds(1, n - 1)]
    remote(gp_all, gp_all, gp_send, gp_recv, flat).wait_recv()
    gp_ref[...] = gpx[...] + jnp.sum(gpl[pl.ds(1, n - 1)], axis=0)
    gather_wait(gat2, 1)
    spec_ref[...] = gat1[...]
    back_ref[...] = gat2[...]

    scatter_end(x1, landed1, 0)
    scatter_end(x2, landed2, 1)
    gather_end(send1, gat1, 0)
    gather_end(send2, gat2, 1)
    remote(came_all, came_all, trade_send, trade_recv, flat).wait_send()
    remote(gp_all, gp_all, gp_send, gp_recv, flat).wait_send()
    sent = pre_ref.at[pl.ds(0, steps * subs)]
    remote(sent, sent, swap_send, swap_recv.at[0], flat).wait_send()
    pltpu.make_async_copy(cot_ref, partial_ref, out_sem).wait()


def main_pass(args, constants, scales, cap, n_row, n_col):
    field = args[6]
    n = n_row * n_col
    count = 2 * n
    inputs, height, width = field.shape
    own = inputs // 2
    block = 2 * RB
    steps = height // block
    blocks = height // RB
    rows = own * RB
    kept = own + 8
    points = n * cap
    vmem = pl.BlockSpec(memory_space=pltpu.VMEM)
    hbm = pl.BlockSpec(memory_space=pl.ANY)
    dma = pltpu.SemaphoreType.DMA
    rows2, rows3, cols2, wide3 = constants
    return pl.pallas_call(
        functools.partial(main_kernel, n_row, n_col, scales),
        out_shape=[
            jax.ShapeDtypeStruct((own, height, width), F32),
            jax.ShapeDtypeStruct((A, 12, 128), F32),
            jax.ShapeDtypeStruct((A, 8, 128), F32),
            jax.ShapeDtypeStruct((4, 128), F32),
        ],
        in_specs=[vmem] * 6 + [hbm] * 6,
        out_specs=[hbm, vmem, vmem, vmem],
        scratch_shapes=[
            pltpu.VMEM((rows2.shape[0], height), BF16),
            pltpu.VMEM((height, rows3.shape[1]), BF16),
            pltpu.VMEM((width, cols2.shape[1]), BF16),
            pltpu.VMEM((wide3.shape[0], width), BF16),
            dma((4,)),
            pltpu.VMEM((steps, inputs, block, width), F32),
            dma((steps,)),
            pltpu.VMEM((2, inputs, inputs, 128), F32),
            dma,
            pltpu.VMEM((blocks, 2 * inputs * RB, width), BF16),
            pltpu.VMEM((blocks, rows, width), F32),
            pltpu.VMEM((2 * rows, inputs * RB), BF16),
            pltpu.VMEM((2 * rows, inputs * RB), BF16),
            pltpu.VMEM((blocks, rows, 2 * M), F32),
            pltpu.VMEM((A, 4, 128), F32),
            pltpu.VMEM((count, 4, 128), F32),
            pltpu.VMEM((2, 12, 128), F32),
            pltpu.VMEM((A, 12, 128), F32),
            pltpu.VMEM((A, 4, 128), F32),
            pltpu.VMEM((count, 4, 128), F32),
            pltpu.VMEM((2, 8, 128), F32),
            pltpu.VMEM((A, 8, 128), F32),
            dma((2,)),
            dma((2,)),
            dma((2, count)),
            dma((2,)),
            pltpu.VMEM((n, kept, cap), F32),
            pltpu.VMEM((n, kept, cap), F32),
            dma,
            dma,
            pltpu.VMEM((kept, points), F32),
            pltpu.VMEM((points, 128), F32),
            pltpu.VMEM((2, own * FOLD, points), BF16),
            pltpu.VMEM((points, width), BF16),
            pltpu.VMEM((points, width), BF16),
            pltpu.VMEM((own, height, width), F32),
            pltpu.VMEM((own, height, 128), F32),
            pltpu.VMEM((blocks, 2 * rows, width), BF16),
            pltpu.VMEM((blocks, rows, width), F32),
            dma,
            dma((steps,)),
            pltpu.VMEM((2 * inputs * RB, 2 * rows), F32),
            pltpu.VMEM((4, 128), F32),
            pltpu.VMEM((n, 4, 128), F32),
            dma,
            dma,
            dma,
        ],
        compiler_params=pltpu.CompilerParams(
            collective_id=0, has_side_effects=True, vmem_limit_bytes=58 * MIB
        ),
    )(*args, *constants)


def turn_blocks(x):
    group = iota((8, 128), 1) // M
    line = iota((8, 128), 0)
    out = jnp.where(group == line, x, 0.0)
    for d in range(1, 8):
        y = pltpu.roll(pltpu.roll(x, d * M, 1), 8 - d, 0)
        out = jnp.where((group - line + 8) % 8 == d, y, out)
    return out


def back_kernel(
    scales, partial_ref, spec_ref, back_ref, gp_ref, kept_ref, rows3_hbm, wide3_hbm,
    out_ref, gs_ref, point_ref, bias_ref,
    half_ref, spec_t, grad_t, point_t, rows3_ref, wide3_ref, table_sem,
    held, load_sem, made, out_sem, gs_sem,
):
    grad_scale, norm_points, bias_scale = scales
    steps, own, block, width = held.shape
    rows = own * RB
    height = steps * block
    inputs = 2 * own
    each_c = inputs // steps

    def load(i):
        at = pl.ds(pl.multiple_of(i * block, block), block)
        return pltpu.make_async_copy(partial_ref.at[:, at, :], held.at[i], load_sem.at[i])

    def store(i):
        at = pl.ds(pl.multiple_of(i * block, block), block)
        return pltpu.make_async_copy(held.at[i], out_ref.at[:, at, :], out_sem.at[i])

    def store_gs(i):
        at = pl.ds(i * each_c, each_c)
        return pltpu.make_async_copy(made.at[:, at], gs_ref.at[:, at], gs_sem.at[i])

    def each(low, high, body):
        def go(k, carry):
            body(k)
            return carry

        lax.fori_loop(low, high, go, 0)

    row_at = pl.multiple_of(lax.axis_index("row") * height, 128)
    col_at = pl.multiple_of(lax.axis_index("col") * width, 128)
    loads = [
        pltpu.make_async_copy(rows3_hbm.at[pl.ds(row_at, height), :], rows3_ref, table_sem.at[0]),
        pltpu.make_async_copy(wide3_hbm.at[:, pl.ds(col_at, width)], wide3_ref, table_sem.at[1]),
    ]
    for one in loads:
        one.start()
    each(0, steps, lambda i: load(i).start())
    kept = as_column(kept_ref[...], lax.axis_index("ch") * own, own)
    mode = iota((own, MODES), 1)
    row_mode = mode // M
    rank = jnp.where(row_mode < M, row_mode, A - 1 - row_mode)
    keep = jnp.where((rank < kept) & (mode % M < kept), grad_scale, 0.0)
    biases = jnp.zeros((1, own), F32)
    for part in range(2):
        for octet in range(own // 8):
            j = part * (own // 8) + octet
            for t in range(A // 8):
                lanes = slice(t * 128, (t + 1) * 128)
                lines = slice(octet * 8, octet * 8 + 8)
                got = turn_blocks(back_ref[t * 8 : t * 8 + 8, 4 + j, :])
                if part == 0 and t == 0:
                    shape = (8, own)
                    named = iota(shape, 1) == iota(shape, 0) + octet * 8
                    named = jnp.where(named, got[:, :1] * bias_scale, 0.0)
                    biases = biases + jnp.sum(named, axis=0, keepdims=True)
                grad_t[part, lines, lanes] = got * keep[lines, lanes]
                for side in range(2):
                    at = side * own + octet * 8
                    spec_t[part, at : at + 8, lanes] = turn_blocks(
                        spec_ref[t * 8 : t * 8 + 8, side * 4 + j, :]
                    )

    def spectral(i):
        for u in range(each_c):
            c = i * each_c + u
            spec_re = spec_t[0, pl.ds(c, 1), :]
            spec_im = spec_t[1, pl.ds(c, 1), :]
            made[0, c] = grad_t[0] * spec_re + grad_t[1] * spec_im
            made[1, c] = grad_t[1] * spec_re - grad_t[0] * spec_im
        store_gs(i).start()

    each(0, steps, spectral)
    for one in loads:
        one.wait()
    mode_half([back_ref[:, q, :] for q in range(4)], rows3_ref[...], half_ref)

    def fields(i):
        load(i).wait()
        for u in range(block // RB):
            at = slice(u * RB, (u + 1) * RB)
            first = pl.multiple_of(i * block + u * RB, RB)
            half = half_ref[:, pl.ds(first, RB), :].reshape(rows, 128)
            result = from_half(half, wide3_ref).reshape(own, RB, width)
            held[i, :, at, :] = held[i, :, at, :] + result
        store(i).start()

    each(0, steps, fields)
    bias_ref[...] = biases
    gp = gp_ref[...] * norm_points
    into = 128 // own
    for k in range(into):
        for i in range(inputs // into):
            at = i * into + k
            point_t[at : at + 1, :] = gp[i : i + 1, k * own : (k + 1) * own]
    eye = sel(iota((own, own), 0) == iota((own, own), 1))
    point_ref[...] = exact(eye, point_t[...], NT)
    each(0, steps, lambda i: store(i).wait())
    each(0, steps, lambda i: store_gs(i).wait())


def back_pass(partial, spec, back, gp, kept, rows3, wide3, scales):
    own, height, width = partial.shape
    block = 4 * RB
    steps = height // block
    hbm = pl.BlockSpec(memory_space=pl.ANY)
    vmem = pl.BlockSpec(memory_space=pltpu.VMEM)
    dma = pltpu.SemaphoreType.DMA
    return pl.pallas_call(
        functools.partial(back_kernel, scales),
        in_specs=[hbm, vmem, vmem, vmem, vmem, hbm, hbm],
        out_specs=[hbm, hbm, vmem, vmem],
        out_shape=[
            jax.ShapeDtypeStruct((own, height, width), F32),
            jax.ShapeDtypeStruct((2, 2 * own, own, MODES), F32),
            jax.ShapeDtypeStruct((own, 2 * own), F32),
            jax.ShapeDtypeStruct((1, own), F32),
        ],
        scratch_shapes=[
            pltpu.VMEM((own, height, 128), F32),
            pltpu.VMEM((2, 2 * own, MODES), F32),
            pltpu.VMEM((2, own, MODES), F32),
            pltpu.VMEM((2 * own, own), F32),
            pltpu.VMEM((height, rows3.shape[1]), BF16),
            pltpu.VMEM((wide3.shape[0], width), BF16),
            dma((2,)),
            pltpu.VMEM((steps, own, block, width), F32),
            dma((steps,)),
            pltpu.VMEM((2, 2 * own, own, MODES), F32),
            dma((steps,)),
            dma((steps,)),
        ],
        compiler_params=pltpu.CompilerParams(vmem_limit_bytes=58 * MIB),
    )(partial, spec, back, gp, kept, rows3, wide3)


def per_device(
    field, spec_weight, point_weight, bias, kept_modes, residual, trace_dest, trace_cell
):
    n_row = lax.axis_size("row")
    n_col = lax.axis_size("col")
    inputs, height, width = field.shape
    own = inputs // lax.axis_size("ch")
    points = trace_dest.shape[0]
    tiles = n_row * n_col
    points_all = points * tiles
    cap = max(2, 2 * points // tiles)
    forward_scale = 1.0 / math.sqrt(height * n_row * width * n_col)
    mix_scale = 1.0 / math.sqrt(MODES)
    norm_points = 1.0 / math.sqrt(points_all)
    constants = [jnp.asarray(t) for t in tables(height * n_row, width * n_col)]
    kept = kept_modes.reshape(1, inputs)
    args = (
        trace_dest.reshape(1, points), trace_cell.reshape(1, points), residual, kept,
        bias.reshape(1, own), point_weight, field, spec_weight,
    )
    partial, spec, back, gp = main_pass(
        args, constants, (forward_scale, mix_scale), cap, n_row, n_col
    )
    grad_field, grad_spec, grad_point, grad_bias = back_pass(
        partial, spec, back, gp, kept, constants[1], constants[3],
        (math.sqrt(MODES / points_all), norm_points, norm_points / mix_scale),
    )
    return (grad_field, grad_spec, grad_point.T, grad_bias.reshape(own))


def solution(mesh):
    return jax.shard_map(
        per_device,
        mesh=mesh,
        in_specs=(
            P(None, "row", "col"),
            P(),
            P(),
            P("ch"),
            P(),
            P("ch", ("row", "col")),
            P(("row", "col"), None),
            P(("row", "col")),
        ),
        out_specs=(P("ch", "row", "col"), P(None, None, "ch", None), P(None, "ch"), P("ch")),
        check_vma=False,
    )
```

```python
import functools
import math

import jax
import jax.numpy as jnp
import ml_dtypes
import numpy as np
from jax import lax
from jax.experimental import pallas as pl
from jax.experimental.pallas import tpu as pltpu
from jax.sharding import PartitionSpec as P

M = 16
A = 2 * M
MODES = A * M
RB = 8
FOLD = 32
F32 = jnp.float32
BF16 = jnp.bfloat16
FULL_TURN = 6.283185307179586
NN = (((1,), (0,)), ((), ()))
NT = (((1,), (1,)), ((), ()))
MIB = 1 << 20
MESH = pl.DeviceIdType.MESH


def trig(frequency, period):
    phases = frequency[:, None] * np.arange(period)[None, :] % period
    angles = phases.astype(np.float32) * np.float32(FULL_TURN / period)
    angles = angles.astype(np.float64)
    return np.cos(angles).astype(np.float32), np.sin(angles).astype(np.float32)


def np_split(x):
    hi = x.astype(ml_dtypes.bfloat16)
    return hi, (x - hi.astype(np.float32)).astype(ml_dtypes.bfloat16)


@functools.lru_cache(maxsize=None)
def tables(n_rows, n_cols):
    frequency = np.arange(A)
    frequency = np.where(frequency < M, frequency, frequency - A)
    rows = np.concatenate(trig(frequency, n_rows), axis=0)
    cos, sin = trig(np.arange(M), n_cols)
    hi, low = np_split(rows)
    rows2 = np.concatenate((hi, low), axis=0)
    rows3 = np.concatenate((hi.T, low.T, hi.T), axis=1)
    hi, low = np_split(np.concatenate((cos, sin), axis=0))
    gap = np.zeros((n_cols, 128 - 2 * M), ml_dtypes.bfloat16)
    cols2 = np.concatenate((hi.T, gap, low.T, gap), axis=1)
    hi, low = np_split(np.concatenate((cos, -sin), axis=0))
    wide3 = np.concatenate([hi] * 8 + [low] * 4, axis=0)
    return rows2, rows3, cols2, wide3


def split2(x):
    hi = x.astype(BF16)
    return hi, (x - hi.astype(F32)).astype(BF16)


def mm(a, b, dims=NN):
    return lax.dot_general(a, b, dims, preferred_element_type=F32)


def stacked(x, axis):
    hi, low = split2(x)
    return jnp.concatenate((hi.astype(F32), low.astype(F32)), axis=axis).astype(BF16)


def deep_right(x):
    hi = x.astype(BF16).astype(F32)
    return jnp.concatenate((hi, hi, x - hi), axis=0).astype(BF16)


def exact(a, b, dims=NN):
    return lax.dot_general(
        a, b, dims, precision=lax.Precision.HIGHEST, preferred_element_type=F32
    )


def iota(shape, axis):
    return lax.broadcasted_iota(jnp.int32, shape, axis)


def sel(mask):
    return mask.astype(F32)


def pack(dest, vals, out_ref, tiles, cap):
    n = dest.shape[1]
    named = dest == iota((tiles, n), 0)
    before = iota((n, n), 0) < iota((n, n), 1)
    earlier = mm(sel(named).astype(BF16), sel(before).astype(BF16))
    rank = jnp.sum(jnp.where(named, earlier, 0.0), axis=0, keepdims=True)
    position = dest * cap + rank.astype(jnp.int32)
    rows = vals.shape[0]
    hi = vals.astype(BF16)
    left = vals - hi.astype(F32)
    mid = left.astype(BF16)
    low = (left - mid.astype(F32)).astype(BF16)
    parts = jnp.concatenate((hi.astype(F32), mid.astype(F32), low.astype(F32)), axis=0).astype(BF16)
    step = 512
    for first in range(0, tiles * cap, step):
        place = sel(position == iota((step, n), 0) + first).astype(BF16)
        got = mm(parts, place, NT)
        got = got[:rows] + got[rows : 2 * rows] + got[2 * rows : 3 * rows]
        for at in range(0, step, cap):
            out_ref[(first + at) // cap] = got[:, at : at + cap]


def mode_lines(rows2, tall_ref, x_ref, scale):
    height = tall_ref.shape[0] * RB
    for o in range(tall_ref.shape[1] // RB):
        tall = tall_ref[:, o * RB : (o + 1) * RB, :].reshape(height, 2 * M)
        hi, low = split2(tall)
        both = mm(rows2, hi)
        grid = both[: 2 * A] + both[2 * A :] + mm(rows2[: 2 * A], low)
        re = (grid[:A, :M] - grid[A:, M:]) * scale
        im = (grid[A:, :M] + grid[:A, M:]) * (-scale)
        octet, at = o // 8, o % 8 * M
        x_ref[:, octet, at : at + M] = re
        x_ref[:, 2 + octet, at : at + M] = im


def part_of(x, size):
    if size & (size - 1) == 0:
        return lax.shift_right_logical(x, size.bit_length() - 1)
    return lax.div(x, size)


def rest_of(x, size):
    if size & (size - 1) == 0:
        return x & (size - 1)
    return lax.rem(x, size)


def as_column(line, first=0, count=None):
    width = line.shape[1]
    shape = (count or width, width)
    picked = jnp.where(iota(shape, 1) == iota(shape, 0) + first, line.astype(F32), 0.0)
    return jnp.sum(picked, axis=1, keepdims=True).astype(jnp.int32)


def same_place():
    return sel(iota((128, 128), 0) % M == iota((128, 128), 1) % M)


def spread8(s8):
    z = jnp.broadcast_to(s8[:, None, :], (8, 8, 128)).reshape(64, 128)
    z = jnp.where(iota((64, 128), 1) // M == iota((64, 128), 0) % 8, z, 0.0)
    z = exact(z, same_place())
    re = jnp.concatenate((z[0:16], z[32:48]), axis=0)
    im = jnp.concatenate((z[16:32], z[48:64]), axis=0)
    return re, im


def compact8(re, im, a):
    group = iota(re.shape, 1) // M
    mine = group == rest_of(a, 8)
    pair = jnp.concatenate((jnp.where(mine, re, 0.0), jnp.where(mine, im, 0.0)), axis=0)
    pair = exact(pair, same_place())
    count = re.shape[0]
    want = iota(re.shape, 0) % 4 * 2
    y = jnp.where(group == want, pair[:count], jnp.where(group == want + 1, pair[count:], 0.0))
    fours = sel(iota((8, count), 0) == iota((8, count), 1) // 4)
    return exact(fours, y)


def mode_half(lines, rows3, half_ref):
    for q, x in enumerate(lines):
        lane = iota(x.shape, 1)
        low_half = lane % (2 * M) < M
        y = jnp.where(low_half, -pltpu.roll(x, 128 - M, 1), pltpu.roll(x, M, 1))
        half = mm(rows3, deep_right(jnp.concatenate((x, y), axis=0)))
        own = iota(half.shape, 1) // (2 * M)
        for k in range(4):
            half_ref[q * 4 + k] = jnp.where(own == k, half, 0.0)


def from_half(half, wide3):
    hi, low = split2(half)
    return mm(jnp.concatenate((hi, low), axis=1), wide3[:256]) + mm(hi, wide3[256:])


def col_modes(parts, cols2):
    half = parts.shape[0] // 2
    got = mm(parts, cols2)
    return got[:half, : 2 * M] + got[:half, 128 : 128 + 2 * M] + got[half:, : 2 * M]


def main_kernel(
    n_row, n_col, scales,
    dest_ref, cell_ref, res_ref, kept_ref, bias_ref, point_ref, field_ref, w_ref,
    rows2_hbm, rows3_hbm, cols2_hbm, wide3_hbm,
    partial_ref, spec_ref, back_ref, gp_ref,
    rows2_ref, rows3_ref, cols2_ref, wide3_ref, table_sem,
    fbuf, load_sem, wbuf, w_sem, f2_ref, pre_ref, kron2_ref, kronb_ref, tall_ref,
    x1, landed1, send1, gat1, x2, landed2, send2, gat2, rs_send, rs_recv, ag_send, ag_recv,
    grouped, came, trade_send, trade_recv, pts, ids_ref, vm_ref, hot_a, hot_b, cot_ref, half_ref,
    sl_ref, other_ref, swap_send, swap_recv, acc_ref, gpx, gpl, gp_send, gp_recv, out_sem,
):
    forward_scale, mix_scale = scales
    n = n_row * n_col
    count = 2 * n
    stride = count // A
    ch = lax.axis_index("ch")
    me = lax.axis_index("row") * n_col + lax.axis_index("col")
    flat = me * 2 + ch
    a = part_of(flat, stride)
    is_reducer = rest_of(flat, stride) == 0
    small = stride == 1
    steps, inputs, block, width = fbuf.shape
    own = inputs // 2
    rows = own * RB
    height = steps * block
    subs = block // RB
    points = pts.shape[1]

    def device_of(f):
        f = jnp.int32(f)
        p = part_of(f, 2)
        return (part_of(p, n_col), rest_of(p, n_col), rest_of(f, 2))

    def remote(src, dst, send, recv, f):
        return pltpu.make_async_remote_copy(
            src_ref=src, dst_ref=dst, send_sem=send, recv_sem=recv,
            device_id=device_of(f), device_id_type=MESH,
        )

    def some(low, high, body):
        if small:
            for k in range(low, high):
                body(k)
        else:
            each(low, high, body)

    def each(low, high, body):
        def go(k, carry):
            body(k)
            return carry

        lax.fori_loop(low, high, go, 0)

    def pairs(low, high, body):
        def both(i):
            body(low + 2 * i)
            body(low + 2 * i + 1)

        each(0, (high - low) // 2, both)
        if (high - low) % 2:
            body(high - 1)

    def on_reducer(body):
        if stride == 1:
            body()
        else:
            pl.when(is_reducer)(body)

    def off_reducer(body):
        if stride > 1:
            pl.when(jnp.logical_not(is_reducer))(body)

    row_at = pl.multiple_of(lax.axis_index("row") * height, 128)
    col_at = pl.multiple_of(lax.axis_index("col") * width, 128)
    table_loads = [
        pltpu.make_async_copy(src, dst, table_sem.at[i])
        for i, (src, dst) in enumerate((
            (rows2_hbm.at[:, pl.ds(row_at, height)], rows2_ref),
            (rows3_hbm.at[pl.ds(row_at, height), :], rows3_ref),
            (cols2_hbm.at[pl.ds(col_at, width), :], cols2_ref),
            (wide3_hbm.at[:, pl.ds(col_at, width)], wide3_ref),
        ))
    ]

    def load(i):
        return pltpu.make_async_copy(
            field_ref.at[:, pl.ds(pl.multiple_of(i * block, block), block), :],
            fbuf.at[i], load_sem.at[i],
        )

    w_load = pltpu.make_async_copy(
        w_ref.at[:, :, :, pl.ds(pl.multiple_of(part_of(a, 8) * 128, 128), 128)], wbuf, w_sem
    )
    for one in table_loads:
        one.start()
    each(0, steps, lambda i: load(i).start())
    w_load.start()

    barrier = pltpu.get_barrier_semaphore()
    some(1, count, lambda k: pl.semaphore_signal(
        barrier, inc=1, device_id=device_of(rest_of(flat + k, count)), device_id_type=MESH
    ))

    shape = (rows, inputs)
    pick = sel(iota(shape, 1) == ch * own + iota(shape, 0) // RB)
    wide_shape = (inputs, inputs * RB)
    spread = sel(iota(wide_shape, 0) == iota(wide_shape, 1) // RB)
    turned = sel(iota(wide_shape, 0) == (iota(wide_shape, 1) // RB + ch * own) % inputs)
    kron_shape = (rows, inputs * RB)
    same = iota(kron_shape, 0) % RB == iota(kron_shape, 1) % RB
    forward_point = exact(exact(pick, point_ref[...], NT), spread)
    kron2_ref[...] = stacked(jnp.where(same, forward_point, 0.0), 0)
    backward_point = exact(exact(pick, point_ref[...]), turned)
    kronb_ref[...] = stacked(jnp.where(same, backward_point, 0.0), 0)
    acc_ref[...] = jnp.zeros_like(acc_ref)
    cells = (cell_ref[...] + 1).astype(F32)
    vals = jnp.concatenate(
        (res_ref[...], jnp.broadcast_to(cells, (8, cells.shape[1]))), axis=0
    )
    cap = grouped.shape[2]
    pack(dest_ref[...], vals, grouped, n, cap)
    pl.semaphore_wait(barrier, count - 1)

    def trade(k):
        p = rest_of(me + k, n)
        return remote(grouped.at[p], came.at[k], trade_send, trade_recv, p * 2 + ch)

    some(1, n, lambda k: trade(k).start())
    came[0] = grouped[me]


    for one in table_loads:
        one.wait()

    def front(i):
        load(i).wait()
        for u in range(subs):
            b = i * subs + u
            hi, low = split2(fbuf[i, :, u * RB : (u + 1) * RB, :].reshape(inputs * RB, width))
            f2_ref[b, : inputs * RB, :] = hi
            f2_ref[b, inputs * RB :, :] = low

    def front_modes(i):
        at = pl.multiple_of(ch * rows, rows)
        for u in range(subs):
            b = i * subs + u
            mine = jnp.concatenate(
                (f2_ref[b, pl.ds(at, rows), :], f2_ref[b, pl.ds(at + inputs * RB, rows), :]), axis=0
            )
            tall_ref[b] = col_modes(mine, cols2_ref[...])

    def front_next(i):
        front(i)
        front_modes(i - 1)

    front(0)
    pairs(1, steps, front_next)
    front_modes(steps - 1)

    def scatter(x, landed, stage):
        def copy(k):
            to = rest_of(a + k, A)
            target = to * stride
            slot = count - k if small else rest_of(flat - target + count, count)
            return remote(
                x.at[to], landed.at[slot], rs_send.at[stage], rs_recv.at[stage], target
            )

        return copy

    def scatter_start(x, landed, stage, scale):
        mode_lines(rows2_ref[...], tall_ref, x, scale)
        copy = scatter(x, landed, stage)
        some(1, A, lambda k: copy(k).start())
        off_reducer(lambda: copy(0).start())

    def scatter_end(x, landed, stage):
        def take(slots):
            sent = x.at[pl.ds(0, slots)]
            remote(sent, sent, rs_send.at[stage], rs_recv.at[stage], flat).wait_send()

        on_reducer(lambda: take(A - 1))
        off_reducer(lambda: take(A))

    def reduced(x, landed, stage):
        got = landed.at[pl.ds(1, count - 1)]
        remote(got, got, rs_send.at[stage], rs_recv.at[stage], flat).wait_recv()
        pairs = landed[pl.ds(2, count - 2)].reshape(n - 1, 2, 4, 128)
        pairs = jnp.sum(pairs, axis=0)
        mine = x[a] + pairs[0]
        theirs = landed[1] + pairs[1]
        first = jnp.where(ch == 0, mine, theirs)
        second = jnp.where(ch == 0, theirs, mine)
        return jnp.concatenate((first, second), axis=0)

    def gather(source, gat, stage):
        def copy(k):
            f = rest_of(flat + k, count)
            send = ag_send.at[stage, 0 if small else k]
            return remote(
                source.at[rest_of(ch + k, 2)], gat.at[a], send, ag_recv.at[stage], f
            )

        return copy

    def gather_wait(gat, stage):
        def take(slots):
            got = gat.at[pl.ds(0, slots)]
            remote(got, got, ag_send.at[stage, 0], ag_recv.at[stage], flat).wait_recv()

        on_reducer(lambda: take(A - 1))
        off_reducer(lambda: take(A))

    def gather_end(source, gat, stage):
        if small:
            sent = gat.at[pl.ds(0, A - 1)]
            remote(sent, sent, ag_send.at[stage, 0], ag_recv.at[stage], flat).wait_send()
        else:
            copy = gather(source, gat, stage)
            on_reducer(lambda: each(1, count, lambda k: copy(k).wait_send()))

    rank = jnp.where(a < M, a, A - 1 - a)
    kept = as_column(kept_ref[...])
    allowed = sel((rank < kept) & (iota((inputs, 128), 1) % M < kept))

    scatter_start(x1, landed1, 0, forward_scale)

    def pointwise(i):
        for u in range(subs):
            b = i * subs + u
            both = mm(kron2_ref[...], f2_ref[b, : inputs * RB, :])
            low = f2_ref[b, inputs * RB :, :]
            pre_ref[b] = both[:rows] + both[rows:] + mm(kron2_ref[:rows, :], low)

    pairs(0, steps, pointwise)

    came_all = came.at[pl.ds(1, n - 1)]
    remote(came_all, came_all, trade_send, trade_recv, flat).wait_recv()
    for p in range(n):
        pts[:, p * cap : (p + 1) * cap] = came[p]
    cell = pts[own : own + 1, :].astype(jnp.int32) - 1
    row = cell // width
    fold = jnp.where(cell < 0, -1, row % FOLD)
    code = jnp.where(cell < 0, -1, row // FOLD * width + cell % width).astype(F32)
    for first in range(0, points, 128):
        ids_ref[first : first + 128, :] = jnp.broadcast_to(
            code[:, first : first + 128], (128, 128)
        ).T
    here = fold == iota((FOLD, points), 0)
    half_own = own // 2

    def fill(o):
        value = pts[pl.ds(o, 1), :]
        hi = value.astype(BF16).astype(F32)
        group = o // half_own
        at = pl.multiple_of(lax.rem(o, half_own) * FOLD, FOLD)
        vm_ref[group, pl.ds(at, FOLD), :] = jnp.where(here, hi, 0.0).astype(BF16)
        vm_ref[group, pl.ds(at + half_own * FOLD, FOLD), :] = jnp.where(
            here, value - hi, 0.0
        ).astype(BF16)

    each(0, own, fill)

    span = half_own * FOLD

    def name_columns(q, hot_ref):
        for at in range(0, width, 128):
            names = (iota((points, 128), 1) + (q * width + at)).astype(F32)
            hot_ref[:, at : at + 128] = sel(ids_ref[...] == names).astype(BF16)

    name_columns(0, hot_a)

    def mix():
        s8 = reduced(x1, landed1, 0)
        spec_re, spec_im = spread8(s8)
        w_load.wait()
        re = jnp.zeros((inputs, 128), F32)
        im = jnp.zeros((inputs, 128), F32)
        for c in range(inputs):
            one_re, one_im = spec_re[c : c + 1], spec_im[c : c + 1]
            re = re + (wbuf[0, c] * one_re - wbuf[1, c] * one_im)
            im = im + (wbuf[0, c] * one_im + wbuf[1, c] * one_re)
        keep = allowed * mix_scale
        mixed = compact8(re * keep, im * keep, a)
        for d in range(2):
            send1[d, :8] = s8
            send1[d, 8:12] = mixed[4 * d : 4 * d + 4]
        copy = gather(send1, gat1, 0)
        some(1, count, lambda k: copy(k).start())
        gat1[a] = send1[ch]

    on_reducer(mix)
    if stride > 1:
        off_reducer(lambda: w_load.wait())

    def place(q, hot_ref):
        for group in range(2):
            got = mm(vm_ref[group], hot_ref[...])
            got = (got[:span] + got[span:]).reshape(half_own, FOLD, width)
            cot_ref[
                group * half_own : (group + 1) * half_own,
                pl.ds(pl.multiple_of(q * FOLD, FOLD), FOLD), :,
            ] = got

    def place_pair(i):
        name_columns(2 * i + 1, hot_b)
        place(2 * i, hot_a)
        name_columns(2 * i + 2, hot_a)
        place(2 * i + 1, hot_b)

    each(0, height // FOLD // 2, place_pair)

    gather_wait(gat1, 0)
    bias_shape = (own, own * 2 * M)
    bias_at = sel(iota(bias_shape, 1) == iota(bias_shape, 0) * (2 * M))
    bias_line = exact(jnp.broadcast_to(bias_ref[...], (8, own)), bias_at)[:1]
    first_mode = iota((A, 128), 0) == 0
    mode_half(
        [
            gat1[:, 8 + q, :]
            + jnp.where(first_mode, bias_line[:, q * 128 : (q + 1) * 128], 0.0)
            for q in range(4)
        ],
        rows3_ref[...], half_ref,
    )

    def swap(i):
        at = pl.ds(i * subs, subs)
        return remote(
            pre_ref.at[at], other_ref.at[at], swap_send, swap_recv.at[i], me * 2 + 1 - ch
        )

    k0 = math.sqrt(2.0 / math.pi)

    def slopes(i):
        for u in range(subs):
            b = i * subs + u
            first = pl.multiple_of(b * RB, RB)
            half = half_ref[:, pl.ds(first, RB), :].reshape(rows, 128)
            pre = pre_ref[b] + from_half(half, wide3_ref)
            cot = cot_ref[:, pl.ds(first, RB), :].reshape(rows, width)
            square = pre * pre
            t = jnp.tanh(k0 * pre * (1.0 + 0.044715 * square))
            rate = 0.5 * (1.0 + t) + 0.5 * k0 * pre * (1.0 - t * t) * (1.0 + 3 * 0.044715 * square)
            slope = cot * rate
            pre_ref[b] = slope
            hi, low = split2(slope)
            sl_ref[b, :rows, :] = hi
            sl_ref[b, rows:, :] = low
            if u % subs == subs - 1:
                swap(i).start()

    def slope_modes(i):
        for u in range(subs):
            b = i * subs + u
            tall_ref[b] = col_modes(sl_ref[b], cols2_ref[...])

    def slopes_next(i):
        slope_modes(i - 1)
        slopes(i)

    slopes(0)
    pairs(1, steps, slopes_next)
    slope_modes(steps - 1)
    scatter_start(x2, landed2, 1, mix_scale)

    def point_sums(i):
        fields = jnp.concatenate([f2_ref[i * 2 + u] for u in range(2)], axis=1)
        found = jnp.concatenate([sl_ref[i * 2 + u] for u in range(2)], axis=1)
        acc_ref[...] += mm(fields, found, NT)

    each(0, steps * subs // 2, point_sums)
    total = acc_ref[: inputs * RB, :] + acc_ref[inputs * RB :, :]
    total = total[:, :rows] + total[:, rows:]
    matched = iota(total.shape, 0) % RB == iota(total.shape, 1) % RB
    total = jnp.sum(jnp.where(matched, total, 0.0).reshape(inputs, RB, rows), axis=1)
    into = 128 // own
    group = sel(iota((rows, 128), 0) // RB == iota((rows, 128), 1) % own)
    total = exact(total, group)
    mine = iota(total.shape, 1) // own == iota(total.shape, 0) % into
    gpx[...] = jnp.sum(jnp.where(mine, total, 0.0).reshape(inputs // into, into, 128), axis=1)

    def point_send(k):
        p = rest_of(me + k, n)
        return remote(gpx, gpl.at[k], gp_send, gp_recv, p * 2 + ch)

    some(1, n, lambda k: point_send(k).start())

    def adjoint():
        s8 = reduced(x2, landed2, 1)
        grad_re, grad_im = spread8(s8)
        grad_re = grad_re * allowed
        grad_im = grad_im * allowed
        lines_re, lines_im = [], []
        for c in range(inputs):
            w_re, w_im = wbuf[0, c], wbuf[1, c]
            lines_re.append(jnp.sum(w_re * grad_re + w_im * grad_im, axis=0, keepdims=True))
            lines_im.append(jnp.sum(w_re * grad_im - w_im * grad_re, axis=0, keepdims=True))
        re = jnp.concatenate(lines_re, axis=0) * forward_scale
        im = jnp.concatenate(lines_im, axis=0) * forward_scale
        turned_modes = compact8(re, im, a)
        for d in range(2):
            send2[d, :4] = turned_modes[4 * d : 4 * d + 4]
            send2[d, 4:8] = s8[4 * d : 4 * d + 4]
        copy = gather(send2, gat2, 1)
        some(1, count, lambda k: copy(k).start())
        gat2[a] = send2[ch]

    on_reducer(adjoint)

    def store(i):
        at = pl.ds(pl.multiple_of(i * block, block), block)
        return pltpu.make_async_copy(cot_ref.at[:, at, :], partial_ref.at[:, at, :], out_sem)

    def backs(i):
        swap(i).wait_recv()
        for u in range(subs):
            b = i * subs + u
            first = pl.multiple_of(b * RB, RB)
            other_hi, other_low = split2(other_ref[b])
            hi = jnp.concatenate((sl_ref[b, :rows, :], other_hi), axis=0)
            low = jnp.concatenate((sl_ref[b, rows:, :], other_low), axis=0)
            both = mm(kronb_ref[...], hi)
            result = both[:rows] + both[rows:] + mm(kronb_ref[:rows, :], low)
            cot_ref[:, pl.ds(first, RB), :] = result.reshape(own, RB, width)
        store(i).start()

    pairs(0, steps, backs)

    gp_all = gpl.at[pl.ds(1, n - 1)]
    remote(gp_all, gp_all, gp_send, gp_recv, flat).wait_recv()
    gp_ref[...] = gpx[...] + jnp.sum(gpl[pl.ds(1, n - 1)], axis=0)
    gather_wait(gat2, 1)
    spec_ref[...] = gat1[...]
    back_ref[...] = gat2[...]

    scatter_end(x1, landed1, 0)
    scatter_end(x2, landed2, 1)
    gather_end(send1, gat1, 0)
    gather_end(send2, gat2, 1)
    remote(came_all, came_all, trade_send, trade_recv, flat).wait_send()
    remote(gp_all, gp_all, gp_send, gp_recv, flat).wait_send()
    sent = pre_ref.at[pl.ds(0, steps * subs)]
    remote(sent, sent, swap_send, swap_recv.at[0], flat).wait_send()
    pltpu.make_async_copy(cot_ref, partial_ref, out_sem).wait()


def main_pass(args, constants, scales, cap, n_row, n_col):
    field = args[6]
    n = n_row * n_col
    count = 2 * n
    inputs, height, width = field.shape
    own = inputs // 2
    block = 2 * RB
    steps = height // block
    blocks = height // RB
    rows = own * RB
    kept = own + 8
    points = n * cap
    vmem = pl.BlockSpec(memory_space=pltpu.VMEM)
    hbm = pl.BlockSpec(memory_space=pl.ANY)
    dma = pltpu.SemaphoreType.DMA
    rows2, rows3, cols2, wide3 = constants
    return pl.pallas_call(
        functools.partial(main_kernel, n_row, n_col, scales),
        out_shape=[
            jax.ShapeDtypeStruct((own, height, width), F32),
            jax.ShapeDtypeStruct((A, 12, 128), F32),
            jax.ShapeDtypeStruct((A, 8, 128), F32),
            jax.ShapeDtypeStruct((4, 128), F32),
        ],
        in_specs=[vmem] * 6 + [hbm] * 6,
        out_specs=[hbm, vmem, vmem, vmem],
        scratch_shapes=[
            pltpu.VMEM((rows2.shape[0], height), BF16),
            pltpu.VMEM((height, rows3.shape[1]), BF16),
            pltpu.VMEM((width, cols2.shape[1]), BF16),
            pltpu.VMEM((wide3.shape[0], width), BF16),
            dma((4,)),
            pltpu.VMEM((steps, inputs, block, width), F32),
            dma((steps,)),
            pltpu.VMEM((2, inputs, inputs, 128), F32),
            dma,
            pltpu.VMEM((blocks, 2 * inputs * RB, width), BF16),
            pltpu.VMEM((blocks, rows, width), F32),
            pltpu.VMEM((2 * rows, inputs * RB), BF16),
            pltpu.VMEM((2 * rows, inputs * RB), BF16),
            pltpu.VMEM((blocks, rows, 2 * M), F32),
            pltpu.VMEM((A, 4, 128), F32),
            pltpu.VMEM((count, 4, 128), F32),
            pltpu.VMEM((2, 12, 128), F32),
            pltpu.VMEM((A, 12, 128), F32),
            pltpu.VMEM((A, 4, 128), F32),
            pltpu.VMEM((count, 4, 128), F32),
            pltpu.VMEM((2, 8, 128), F32),
            pltpu.VMEM((A, 8, 128), F32),
            dma((2,)),
            dma((2,)),
            dma((2, count)),
            dma((2,)),
            pltpu.VMEM((n, kept, cap), F32),
            pltpu.VMEM((n, kept, cap), F32),
            dma,
            dma,
            pltpu.VMEM((kept, points), F32),
            pltpu.VMEM((points, 128), F32),
            pltpu.VMEM((2, own * FOLD, points), BF16),
            pltpu.VMEM((points, width), BF16),
            pltpu.VMEM((points, width), BF16),
            pltpu.VMEM((own, height, width), F32),
            pltpu.VMEM((own, height, 128), F32),
            pltpu.VMEM((blocks, 2 * rows, width), BF16),
            pltpu.VMEM((blocks, rows, width), F32),
            dma,
            dma((steps,)),
            pltpu.VMEM((2 * inputs * RB, 2 * rows), F32),
            pltpu.VMEM((4, 128), F32),
            pltpu.VMEM((n, 4, 128), F32),
            dma,
            dma,
            dma,
        ],
        compiler_params=pltpu.CompilerParams(
            collective_id=0, has_side_effects=True, vmem_limit_bytes=58 * MIB
        ),
    )(*args, *constants)


def turn_blocks(x):
    group = iota((8, 128), 1) // M
    line = iota((8, 128), 0)
    out = jnp.where(group == line, x, 0.0)
    for d in range(1, 8):
        y = pltpu.roll(pltpu.roll(x, d * M, 1), 8 - d, 0)
        out = jnp.where((group - line + 8) % 8 == d, y, out)
    return out


def back_kernel(
    scales, partial_ref, spec_ref, back_ref, gp_ref, kept_ref, rows3_hbm, wide3_hbm,
    out_ref, gs_ref, point_ref, bias_ref,
    half_ref, spec_t, grad_t, point_t, rows3_ref, wide3_ref, table_sem,
    held, load_sem, made, out_sem, gs_sem,
):
    grad_scale, norm_points, bias_scale = scales
    steps, own, block, width = held.shape
    rows = own * RB
    height = steps * block
    inputs = 2 * own
    each_c = inputs // steps

    def load(i):
        at = pl.ds(pl.multiple_of(i * block, block), block)
        return pltpu.make_async_copy(partial_ref.at[:, at, :], held.at[i], load_sem.at[i])

    def store(i):
        at = pl.ds(pl.multiple_of(i * block, block), block)
        return pltpu.make_async_copy(held.at[i], out_ref.at[:, at, :], out_sem.at[i])

    def store_gs(i):
        at = pl.ds(i * each_c, each_c)
        return pltpu.make_async_copy(made.at[:, at], gs_ref.at[:, at], gs_sem.at[i])

    def each(low, high, body):
        def go(k, carry):
            body(k)
            return carry

        lax.fori_loop(low, high, go, 0)

    row_at = pl.multiple_of(lax.axis_index("row") * height, 128)
    col_at = pl.multiple_of(lax.axis_index("col") * width, 128)
    loads = [
        pltpu.make_async_copy(rows3_hbm.at[pl.ds(row_at, height), :], rows3_ref, table_sem.at[0]),
        pltpu.make_async_copy(wide3_hbm.at[:, pl.ds(col_at, width)], wide3_ref, table_sem.at[1]),
    ]
    for one in loads:
        one.start()
    each(0, steps, lambda i: load(i).start())
    for one in loads:
        one.wait()
    mode_half([back_ref[:, q, :] for q in range(4)], rows3_ref[...], half_ref)

    def fields(i):
        load(i).wait()
        for u in range(block // RB):
            at = slice(u * RB, (u + 1) * RB)
            first = pl.multiple_of(i * block + u * RB, RB)
            half = half_ref[:, pl.ds(first, RB), :].reshape(rows, 128)
            result = from_half(half, wide3_ref).reshape(own, RB, width)
            held[i, :, at, :] = held[i, :, at, :] + result
        store(i).start()

    each(0, steps, fields)
    kept = as_column(kept_ref[...], lax.axis_index("ch") * own, own)
    mode = iota((own, MODES), 1)
    row_mode = mode // M
    rank = jnp.where(row_mode < M, row_mode, A - 1 - row_mode)
    keep = jnp.where((rank < kept) & (mode % M < kept), grad_scale, 0.0)
    biases = jnp.zeros((1, own), F32)
    for part in range(2):
        for octet in range(own // 8):
            j = part * (own // 8) + octet
            for t in range(A // 8):
                lanes = slice(t * 128, (t + 1) * 128)
                lines = slice(octet * 8, octet * 8 + 8)
                got = turn_blocks(back_ref[t * 8 : t * 8 + 8, 4 + j, :])
                if part == 0 and t == 0:
                    shape = (8, own)
                    named = iota(shape, 1) == iota(shape, 0) + octet * 8
                    named = jnp.where(named, got[:, :1] * bias_scale, 0.0)
                    biases = biases + jnp.sum(named, axis=0, keepdims=True)
                grad_t[part, lines, lanes] = got * keep[lines, lanes]
                for side in range(2):
                    at = side * own + octet * 8
                    spec_t[part, at : at + 8, lanes] = turn_blocks(
                        spec_ref[t * 8 : t * 8 + 8, side * 4 + j, :]
                    )

    def spectral(i):
        for u in range(each_c):
            c = i * each_c + u
            spec_re = spec_t[0, pl.ds(c, 1), :]
            spec_im = spec_t[1, pl.ds(c, 1), :]
            made[0, c] = grad_t[0] * spec_re + grad_t[1] * spec_im
            made[1, c] = grad_t[1] * spec_re - grad_t[0] * spec_im
        store_gs(i).start()

    each(0, steps, spectral)
    bias_ref[...] = biases
    gp = gp_ref[...] * norm_points
    into = 128 // own
    for k in range(into):
        for i in range(inputs // into):
            at = i * into + k
            point_t[at : at + 1, :] = gp[i : i + 1, k * own : (k + 1) * own]
    eye = sel(iota((own, own), 0) == iota((own, own), 1))
    point_ref[...] = exact(eye, point_t[...], NT)
    each(0, steps, lambda i: store(i).wait())
    each(0, steps, lambda i: store_gs(i).wait())


def back_pass(partial, spec, back, gp, kept, rows3, wide3, scales):
    own, height, width = partial.shape
    block = 4 * RB
    steps = height // block
    hbm = pl.BlockSpec(memory_space=pl.ANY)
    vmem = pl.BlockSpec(memory_space=pltpu.VMEM)
    dma = pltpu.SemaphoreType.DMA
    return pl.pallas_call(
        functools.partial(back_kernel, scales),
        in_specs=[hbm, vmem, vmem, vmem, vmem, hbm, hbm],
        out_specs=[hbm, hbm, vmem, vmem],
        out_shape=[
            jax.ShapeDtypeStruct((own, height, width), F32),
            jax.ShapeDtypeStruct((2, 2 * own, own, MODES), F32),
            jax.ShapeDtypeStruct((own, 2 * own), F32),
            jax.ShapeDtypeStruct((1, own), F32),
        ],
        scratch_shapes=[
            pltpu.VMEM((own, height, 128), F32),
            pltpu.VMEM((2, 2 * own, MODES), F32),
            pltpu.VMEM((2, own, MODES), F32),
            pltpu.VMEM((2 * own, own), F32),
            pltpu.VMEM((height, rows3.shape[1]), BF16),
            pltpu.VMEM((wide3.shape[0], width), BF16),
            dma((2,)),
            pltpu.VMEM((steps, own, block, width), F32),
            dma((steps,)),
            pltpu.VMEM((2, 2 * own, own, MODES), F32),
            dma((steps,)),
            dma((steps,)),
        ],
        compiler_params=pltpu.CompilerParams(vmem_limit_bytes=58 * MIB),
    )(partial, spec, back, gp, kept, rows3, wide3)


def per_device(
    field, spec_weight, point_weight, bias, kept_modes, residual, trace_dest, trace_cell
):
    n_row = lax.axis_size("row")
    n_col = lax.axis_size("col")
    inputs, height, width = field.shape
    own = inputs // lax.axis_size("ch")
    points = trace_dest.shape[0]
    tiles = n_row * n_col
    points_all = points * tiles
    cap = max(2, 2 * points // tiles)
    forward_scale = 1.0 / math.sqrt(height * n_row * width * n_col)
    mix_scale = 1.0 / math.sqrt(MODES)
    norm_points = 1.0 / math.sqrt(points_all)
    constants = [jnp.asarray(t) for t in tables(height * n_row, width * n_col)]
    kept = kept_modes.reshape(1, inputs)
    args = (
        trace_dest.reshape(1, points), trace_cell.reshape(1, points), residual, kept,
        bias.reshape(1, own), point_weight, field, spec_weight,
    )
    partial, spec, back, gp = main_pass(
        args, constants, (forward_scale, mix_scale), cap, n_row, n_col
    )
    grad_field, grad_spec, grad_point, grad_bias = back_pass(
        partial, spec, back, gp, kept, constants[1], constants[3],
        (math.sqrt(MODES / points_all), norm_points, norm_points / mix_scale),
    )
    return (grad_field, grad_spec, grad_point.T, grad_bias.reshape(own))


def solution(mesh):
    return jax.shard_map(
        per_device,
        mesh=mesh,
        in_specs=(
            P(None, "row", "col"),
            P(),
            P(),
            P("ch"),
            P(),
            P("ch", ("row", "col")),
            P(("row", "col"), None),
            P(("row", "col")),
        ),
        out_specs=(P("ch", "row", "col"), P(None, None, "ch", None), P(None, "ch"), P("ch")),
        check_vma=False,
    )
```

```python
import functools
import math

import jax
import jax.numpy as jnp
import ml_dtypes
import numpy as np
from jax import lax
from jax.experimental import pallas as pl
from jax.experimental.pallas import tpu as pltpu
from jax.sharding import PartitionSpec as P

M = 16
A = 2 * M
MODES = A * M
RB = 8
FOLD = 32
F32 = jnp.float32
BF16 = jnp.bfloat16
FULL_TURN = 6.283185307179586
NN = (((1,), (0,)), ((), ()))
NT = (((1,), (1,)), ((), ()))
MIB = 1 << 20
MESH = pl.DeviceIdType.MESH


def trig(frequency, period):
    phases = frequency[:, None] * np.arange(period)[None, :] % period
    angles = phases.astype(np.float32) * np.float32(FULL_TURN / period)
    angles = angles.astype(np.float64)
    return np.cos(angles).astype(np.float32), np.sin(angles).astype(np.float32)


def np_split(x):
    hi = x.astype(ml_dtypes.bfloat16)
    return hi, (x - hi.astype(np.float32)).astype(ml_dtypes.bfloat16)


@functools.lru_cache(maxsize=None)
def tables(n_rows, n_cols):
    frequency = np.arange(A)
    frequency = np.where(frequency < M, frequency, frequency - A)
    rows = np.concatenate(trig(frequency, n_rows), axis=0)
    cos, sin = trig(np.arange(M), n_cols)
    hi, low = np_split(rows)
    rows2 = np.concatenate((hi, low), axis=0)
    rows3 = np.concatenate((hi.T, low.T, hi.T), axis=1)
    hi, low = np_split(np.concatenate((cos, sin), axis=0))
    gap = np.zeros((n_cols, 128 - 2 * M), ml_dtypes.bfloat16)
    cols2 = np.concatenate((hi.T, gap, low.T, gap), axis=1)
    hi, low = np_split(np.concatenate((cos, -sin), axis=0))
    wide3 = np.concatenate([hi] * 8 + [low] * 4, axis=0)
    return rows2, rows3, cols2, wide3


def split2(x):
    hi = x.astype(BF16)
    return hi, (x - hi.astype(F32)).astype(BF16)


def mm(a, b, dims=NN):
    return lax.dot_general(a, b, dims, preferred_element_type=F32)


def stacked(x, axis):
    hi, low = split2(x)
    return jnp.concatenate((hi.astype(F32), low.astype(F32)), axis=axis).astype(BF16)


def deep_right(x):
    hi = x.astype(BF16).astype(F32)
    return jnp.concatenate((hi, hi, x - hi), axis=0).astype(BF16)


def exact(a, b, dims=NN):
    return lax.dot_general(
        a, b, dims, precision=lax.Precision.HIGHEST, preferred_element_type=F32
    )


def iota(shape, axis):
    return lax.broadcasted_iota(jnp.int32, shape, axis)


def sel(mask):
    return mask.astype(F32)


def pack(dest, vals, out_ref, tiles, cap):
    n = dest.shape[1]
    named = dest == iota((tiles, n), 0)
    before = iota((n, n), 0) < iota((n, n), 1)
    earlier = mm(sel(named).astype(BF16), sel(before).astype(BF16))
    rank = jnp.sum(jnp.where(named, earlier, 0.0), axis=0, keepdims=True)
    position = dest * cap + rank.astype(jnp.int32)
    rows = vals.shape[0]
    hi = vals.astype(BF16)
    left = vals - hi.astype(F32)
    mid = left.astype(BF16)
    low = (left - mid.astype(F32)).astype(BF16)
    parts = jnp.concatenate((hi.astype(F32), mid.astype(F32), low.astype(F32)), axis=0).astype(BF16)
    step = 512
    for first in range(0, tiles * cap, step):
        place = sel(position == iota((step, n), 0) + first).astype(BF16)
        got = mm(parts, place, NT)
        got = got[:rows] + got[rows : 2 * rows] + got[2 * rows : 3 * rows]
        for at in range(0, step, cap):
            out_ref[(first + at) // cap] = got[:, at : at + cap]


def mode_lines(rows2, tall_ref, x_ref, scale):
    height = tall_ref.shape[0] * RB
    for o in range(tall_ref.shape[1] // RB):
        tall = tall_ref[:, o * RB : (o + 1) * RB, :].reshape(height, 2 * M)
        hi, low = split2(tall)
        both = mm(rows2, hi)
        grid = both[: 2 * A] + both[2 * A :] + mm(rows2[: 2 * A], low)
        re = (grid[:A, :M] - grid[A:, M:]) * scale
        im = (grid[A:, :M] + grid[:A, M:]) * (-scale)
        octet, at = o // 8, o % 8 * M
        x_ref[:, octet, at : at + M] = re
        x_ref[:, 2 + octet, at : at + M] = im


def part_of(x, size):
    if size & (size - 1) == 0:
        return lax.shift_right_logical(x, size.bit_length() - 1)
    return lax.div(x, size)


def rest_of(x, size):
    if size & (size - 1) == 0:
        return x & (size - 1)
    return lax.rem(x, size)


def as_column(line, first=0, count=None):
    width = line.shape[1]
    shape = (count or width, width)
    picked = jnp.where(iota(shape, 1) == iota(shape, 0) + first, line.astype(F32), 0.0)
    return jnp.sum(picked, axis=1, keepdims=True).astype(jnp.int32)


def same_place():
    return sel(iota((128, 128), 0) % M == iota((128, 128), 1) % M)


def spread8(s8):
    z = jnp.broadcast_to(s8[:, None, :], (8, 8, 128)).reshape(64, 128)
    z = jnp.where(iota((64, 128), 1) // M == iota((64, 128), 0) % 8, z, 0.0)
    z = exact(z, same_place())
    re = jnp.concatenate((z[0:16], z[32:48]), axis=0)
    im = jnp.concatenate((z[16:32], z[48:64]), axis=0)
    return re, im


def compact8(re, im, a):
    group = iota(re.shape, 1) // M
    mine = group == rest_of(a, 8)
    pair = jnp.concatenate((jnp.where(mine, re, 0.0), jnp.where(mine, im, 0.0)), axis=0)
    pair = exact(pair, same_place())
    count = re.shape[0]
    want = iota(re.shape, 0) % 4 * 2
    y = jnp.where(group == want, pair[:count], jnp.where(group == want + 1, pair[count:], 0.0))
    fours = sel(iota((8, count), 0) == iota((8, count), 1) // 4)
    return exact(fours, y)


def mode_half(lines, rows3, half_ref):
    for q, x in enumerate(lines):
        lane = iota(x.shape, 1)
        low_half = lane % (2 * M) < M
        y = jnp.where(low_half, -pltpu.roll(x, 128 - M, 1), pltpu.roll(x, M, 1))
        half = mm(rows3, deep_right(jnp.concatenate((x, y), axis=0)))
        own = iota(half.shape, 1) // (2 * M)
        for k in range(4):
            half_ref[q * 4 + k] = jnp.where(own == k, half, 0.0)


def from_half(half, wide3):
    hi, low = split2(half)
    return mm(jnp.concatenate((hi, low), axis=1), wide3[:256]) + mm(hi, wide3[256:])


def col_modes(parts, cols2):
    half = parts.shape[0] // 2
    got = mm(parts, cols2)
    return got[:half, : 2 * M] + got[:half, 128 : 128 + 2 * M] + got[half:, : 2 * M]


def main_kernel(
    n_row, n_col, scales,
    dest_ref, cell_ref, res_ref, kept_ref, bias_ref, point_ref, field_ref, w_ref,
    rows2_hbm, rows3_hbm, cols2_hbm, wide3_hbm,
    partial_ref, spec_ref, back_ref, gp_ref,
    rows2_ref, rows3_ref, cols2_ref, wide3_ref, table_sem,
    fbuf, load_sem, wbuf, w_sem, f2_ref, pre_ref, kron2_ref, kronb_ref, tall_ref,
    x1, landed1, send1, gat1, x2, landed2, send2, gat2, rs_send, rs_recv, ag_send, ag_recv,
    grouped, came, trade_send, trade_recv, pts, ids_ref, vm_ref, hot_a, hot_b, cot_ref, half_ref,
    sl_ref, other_ref, swap_send, swap_recv, acc_ref, gpx, gpl, gp_send, gp_recv, out_sem,
):
    forward_scale, mix_scale = scales
    n = n_row * n_col
    count = 2 * n
    stride = count // A
    ch = lax.axis_index("ch")
    me = lax.axis_index("row") * n_col + lax.axis_index("col")
    flat = me * 2 + ch
    a = part_of(flat, stride)
    is_reducer = rest_of(flat, stride) == 0
    small = stride == 1
    steps, inputs, block, width = fbuf.shape
    own = inputs // 2
    rows = own * RB
    height = steps * block
    subs = block // RB
    points = pts.shape[1]

    def device_of(f):
        f = jnp.int32(f)
        p = part_of(f, 2)
        return (part_of(p, n_col), rest_of(p, n_col), rest_of(f, 2))

    def remote(src, dst, send, recv, f):
        return pltpu.make_async_remote_copy(
            src_ref=src, dst_ref=dst, send_sem=send, recv_sem=recv,
            device_id=device_of(f), device_id_type=MESH,
        )

    def some(low, high, body):
        if small:
            for k in range(low, high):
                body(k)
        else:
            each(low, high, body)

    def each(low, high, body):
        def go(k, carry):
            body(k)
            return carry

        lax.fori_loop(low, high, go, 0)

    def pairs(low, high, body):
        def both(i):
            body(low + 2 * i)
            body(low + 2 * i + 1)

        each(0, (high - low) // 2, both)
        if (high - low) % 2:
            body(high - 1)

    def on_reducer(body):
        if stride == 1:
            body()
        else:
            pl.when(is_reducer)(body)

    def off_reducer(body):
        if stride > 1:
            pl.when(jnp.logical_not(is_reducer))(body)

    row_at = pl.multiple_of(lax.axis_index("row") * height, 128)
    col_at = pl.multiple_of(lax.axis_index("col") * width, 128)
    table_loads = [
        pltpu.make_async_copy(src, dst, table_sem.at[i])
        for i, (src, dst) in enumerate((
            (rows2_hbm.at[:, pl.ds(row_at, height)], rows2_ref),
            (rows3_hbm.at[pl.ds(row_at, height), :], rows3_ref),
            (cols2_hbm.at[pl.ds(col_at, width), :], cols2_ref),
            (wide3_hbm.at[:, pl.ds(col_at, width)], wide3_ref),
        ))
    ]

    def load(i):
        return pltpu.make_async_copy(
            field_ref.at[:, pl.ds(pl.multiple_of(i * block, block), block), :],
            fbuf.at[i], load_sem.at[i],
        )

    w_load = pltpu.make_async_copy(
        w_ref.at[:, :, :, pl.ds(pl.multiple_of(part_of(a, 8) * 128, 128), 128)], wbuf, w_sem
    )
    for one in table_loads:
        one.start()
    each(0, steps, lambda i: load(i).start())
    w_load.start()

    barrier = pltpu.get_barrier_semaphore()
    some(1, count, lambda k: pl.semaphore_signal(
        barrier, inc=1, device_id=device_of(rest_of(flat + k, count)), device_id_type=MESH
    ))

    shape = (rows, inputs)
    pick = sel(iota(shape, 1) == ch * own + iota(shape, 0) // RB)
    wide_shape = (inputs, inputs * RB)
    spread = sel(iota(wide_shape, 0) == iota(wide_shape, 1) // RB)
    turned = sel(iota(wide_shape, 0) == (iota(wide_shape, 1) // RB + ch * own) % inputs)
    kron_shape = (rows, inputs * RB)
    same = iota(kron_shape, 0) % RB == iota(kron_shape, 1) % RB
    forward_point = exact(exact(pick, point_ref[...], NT), spread)
    kron2_ref[...] = stacked(jnp.where(same, forward_point, 0.0), 0)
    backward_point = exact(exact(pick, point_ref[...]), turned)
    kronb_ref[...] = stacked(jnp.where(same, backward_point, 0.0), 0)
    acc_ref[...] = jnp.zeros_like(acc_ref)
    cells = (cell_ref[...] + 1).astype(F32)
    vals = jnp.concatenate(
        (res_ref[...], jnp.broadcast_to(cells, (8, cells.shape[1]))), axis=0
    )
    cap = grouped.shape[2]
    pack(dest_ref[...], vals, grouped, n, cap)
    pl.semaphore_wait(barrier, count - 1)

    def trade(k):
        p = rest_of(me + k, n)
        return remote(grouped.at[p], came.at[k], trade_send, trade_recv, p * 2 + ch)

    some(1, n, lambda k: trade(k).start())
    came[0] = grouped[me]


    for one in table_loads:
        one.wait()

    def front(i):
        load(i).wait()
        for u in range(subs):
            b = i * subs + u
            hi, low = split2(fbuf[i, :, u * RB : (u + 1) * RB, :].reshape(inputs * RB, width))
            f2_ref[b, : inputs * RB, :] = hi
            f2_ref[b, inputs * RB :, :] = low

    def front_modes(i):
        at = pl.multiple_of(ch * rows, rows)
        for u in range(subs):
            b = i * subs + u
            mine = jnp.concatenate(
                (f2_ref[b, pl.ds(at, rows), :], f2_ref[b, pl.ds(at + inputs * RB, rows), :]), axis=0
            )
            tall_ref[b] = col_modes(mine, cols2_ref[...])

    def front_next(i):
        front(i)
        front_modes(i - 1)

    front(0)
    for i in range(1, steps):
        front_next(i)
    front_modes(steps - 1)

    def scatter(x, landed, stage):
        def copy(k):
            to = rest_of(a + k, A)
            target = to * stride
            slot = count - k if small else rest_of(flat - target + count, count)
            return remote(
                x.at[to], landed.at[slot], rs_send.at[stage], rs_recv.at[stage], target
            )

        return copy

    def scatter_start(x, landed, stage, scale):
        mode_lines(rows2_ref[...], tall_ref, x, scale)
        copy = scatter(x, landed, stage)
        some(1, A, lambda k: copy(k).start())
        off_reducer(lambda: copy(0).start())

    def scatter_end(x, landed, stage):
        def take(slots):
            sent = x.at[pl.ds(0, slots)]
            remote(sent, sent, rs_send.at[stage], rs_recv.at[stage], flat).wait_send()

        on_reducer(lambda: take(A - 1))
        off_reducer(lambda: take(A))

    def reduced(x, landed, stage):
        got = landed.at[pl.ds(1, count - 1)]
        remote(got, got, rs_send.at[stage], rs_recv.at[stage], flat).wait_recv()
        pairs = landed[pl.ds(2, count - 2)].reshape(n - 1, 2, 4, 128)
        pairs = jnp.sum(pairs, axis=0)
        mine = x[a] + pairs[0]
        theirs = landed[1] + pairs[1]
        first = jnp.where(ch == 0, mine, theirs)
        second = jnp.where(ch == 0, theirs, mine)
        return jnp.concatenate((first, second), axis=0)

    def gather(source, gat, stage):
        def copy(k):
            f = rest_of(flat + k, count)
            send = ag_send.at[stage, 0 if small else k]
            return remote(
                source.at[rest_of(ch + k, 2)], gat.at[a], send, ag_recv.at[stage], f
            )

        return copy

    def gather_wait(gat, stage):
        def take(slots):
            got = gat.at[pl.ds(0, slots)]
            remote(got, got, ag_send.at[stage, 0], ag_recv.at[stage], flat).wait_recv()

        on_reducer(lambda: take(A - 1))
        off_reducer(lambda: take(A))

    def gather_end(source, gat, stage):
        if small:
            sent = gat.at[pl.ds(0, A - 1)]
            remote(sent, sent, ag_send.at[stage, 0], ag_recv.at[stage], flat).wait_send()
        else:
            copy = gather(source, gat, stage)
            on_reducer(lambda: each(1, count, lambda k: copy(k).wait_send()))

    rank = jnp.where(a < M, a, A - 1 - a)
    kept = as_column(kept_ref[...])
    allowed = sel((rank < kept) & (iota((inputs, 128), 1) % M < kept))

    scatter_start(x1, landed1, 0, forward_scale)

    def pointwise(i):
        for u in range(subs):
            b = i * subs + u
            both = mm(kron2_ref[...], f2_ref[b, : inputs * RB, :])
            low = f2_ref[b, inputs * RB :, :]
            pre_ref[b] = both[:rows] + both[rows:] + mm(kron2_ref[:rows, :], low)

    for i in range(steps):
        pointwise(i)

    came_all = came.at[pl.ds(1, n - 1)]
    remote(came_all, came_all, trade_send, trade_recv, flat).wait_recv()
    for p in range(n):
        pts[:, p * cap : (p + 1) * cap] = came[p]
    cell = pts[own : own + 1, :].astype(jnp.int32) - 1
    row = cell // width
    fold = jnp.where(cell < 0, -1, row % FOLD)
    code = jnp.where(cell < 0, -1, row // FOLD * width + cell % width).astype(F32)
    for first in range(0, points, 128):
        ids_ref[first : first + 128, :] = jnp.broadcast_to(
            code[:, first : first + 128], (128, 128)
        ).T
    here = fold == iota((FOLD, points), 0)
    half_own = own // 2

    def fill(o):
        value = pts[pl.ds(o, 1), :]
        hi = value.astype(BF16).astype(F32)
        group = o // half_own
        at = pl.multiple_of(lax.rem(o, half_own) * FOLD, FOLD)
        vm_ref[group, pl.ds(at, FOLD), :] = jnp.where(here, hi, 0.0).astype(BF16)
        vm_ref[group, pl.ds(at + half_own * FOLD, FOLD), :] = jnp.where(
            here, value - hi, 0.0
        ).astype(BF16)

    each(0, own, fill)

    span = half_own * FOLD

    def name_columns(q, hot_ref):
        for at in range(0, width, 128):
            names = (iota((points, 128), 1) + (q * width + at)).astype(F32)
            hot_ref[:, at : at + 128] = sel(ids_ref[...] == names).astype(BF16)

    name_columns(0, hot_a)

    def mix():
        s8 = reduced(x1, landed1, 0)
        spec_re, spec_im = spread8(s8)
        w_load.wait()
        re = jnp.zeros((inputs, 128), F32)
        im = jnp.zeros((inputs, 128), F32)
        for c in range(inputs):
            one_re, one_im = spec_re[c : c + 1], spec_im[c : c + 1]
            re = re + (wbuf[0, c] * one_re - wbuf[1, c] * one_im)
            im = im + (wbuf[0, c] * one_im + wbuf[1, c] * one_re)
        keep = allowed * mix_scale
        mixed = compact8(re * keep, im * keep, a)
        for d in range(2):
            send1[d, :8] = s8
            send1[d, 8:12] = mixed[4 * d : 4 * d + 4]
        copy = gather(send1, gat1, 0)
        some(1, count, lambda k: copy(k).start())
        gat1[a] = send1[ch]

    on_reducer(mix)
    if stride > 1:
        off_reducer(lambda: w_load.wait())

    def place(q, hot_ref):
        for group in range(2):
            got = mm(vm_ref[group], hot_ref[...])
            got = (got[:span] + got[span:]).reshape(half_own, FOLD, width)
            cot_ref[
                group * half_own : (group + 1) * half_own,
                pl.ds(pl.multiple_of(q * FOLD, FOLD), FOLD), :,
            ] = got

    def place_pair(i):
        name_columns(2 * i + 1, hot_b)
        place(2 * i, hot_a)
        name_columns(2 * i + 2, hot_a)
        place(2 * i + 1, hot_b)

    each(0, height // FOLD // 2, place_pair)

    gather_wait(gat1, 0)
    bias_shape = (own, own * 2 * M)
    bias_at = sel(iota(bias_shape, 1) == iota(bias_shape, 0) * (2 * M))
    bias_line = exact(jnp.broadcast_to(bias_ref[...], (8, own)), bias_at)[:1]
    first_mode = iota((A, 128), 0) == 0
    mode_half(
        [
            gat1[:, 8 + q, :]
            + jnp.where(first_mode, bias_line[:, q * 128 : (q + 1) * 128], 0.0)
            for q in range(4)
        ],
        rows3_ref[...], half_ref,
    )

    def swap(i):
        at = pl.ds(i * subs, subs)
        return remote(
            pre_ref.at[at], other_ref.at[at], swap_send, swap_recv.at[i], me * 2 + 1 - ch
        )

    k0 = math.sqrt(2.0 / math.pi)

    def slopes(i):
        for u in range(subs):
            b = i * subs + u
            first = pl.multiple_of(b * RB, RB)
            half = half_ref[:, pl.ds(first, RB), :].reshape(rows, 128)
            pre = pre_ref[b] + from_half(half, wide3_ref)
            cot = cot_ref[:, pl.ds(first, RB), :].reshape(rows, width)
            square = pre * pre
            t = jnp.tanh(k0 * pre * (1.0 + 0.044715 * square))
            rate = 0.5 * (1.0 + t) + 0.5 * k0 * pre * (1.0 - t * t) * (1.0 + 3 * 0.044715 * square)
            slope = cot * rate
            pre_ref[b] = slope
            hi, low = split2(slope)
            sl_ref[b, :rows, :] = hi
            sl_ref[b, rows:, :] = low
            if u % subs == subs - 1:
                swap(i).start()

    def slope_modes(i):
        for u in range(subs):
            b = i * subs + u
            tall_ref[b] = col_modes(sl_ref[b], cols2_ref[...])

    def slopes_next(i):
        slope_modes(i - 1)
        slopes(i)

    slopes(0)
    pairs(1, steps, slopes_next)
    slope_modes(steps - 1)
    scatter_start(x2, landed2, 1, mix_scale)

    def point_sums(i):
        fields = jnp.concatenate([f2_ref[i * 2 + u] for u in range(2)], axis=1)
        found = jnp.concatenate([sl_ref[i * 2 + u] for u in range(2)], axis=1)
        acc_ref[...] += mm(fields, found, NT)

    each(0, steps * subs // 2, point_sums)
    total = acc_ref[: inputs * RB, :] + acc_ref[inputs * RB :, :]
    total = total[:, :rows] + total[:, rows:]
    matched = iota(total.shape, 0) % RB == iota(total.shape, 1) % RB
    total = jnp.sum(jnp.where(matched, total, 0.0).reshape(inputs, RB, rows), axis=1)
    into = 128 // own
    group = sel(iota((rows, 128), 0) // RB == iota((rows, 128), 1) % own)
    total = exact(total, group)
    mine = iota(total.shape, 1) // own == iota(total.shape, 0) % into
    gpx[...] = jnp.sum(jnp.where(mine, total, 0.0).reshape(inputs // into, into, 128), axis=1)

    def point_send(k):
        p = rest_of(me + k, n)
        return remote(gpx, gpl.at[k], gp_send, gp_recv, p * 2 + ch)

    some(1, n, lambda k: point_send(k).start())

    def adjoint():
        s8 = reduced(x2, landed2, 1)
        grad_re, grad_im = spread8(s8)
        grad_re = grad_re * allowed
        grad_im = grad_im * allowed
        lines_re, lines_im = [], []
        for c in range(inputs):
            w_re, w_im = wbuf[0, c], wbuf[1, c]
            lines_re.append(jnp.sum(w_re * grad_re + w_im * grad_im, axis=0, keepdims=True))
            lines_im.append(jnp.sum(w_re * grad_im - w_im * grad_re, axis=0, keepdims=True))
        re = jnp.concatenate(lines_re, axis=0) * forward_scale
        im = jnp.concatenate(lines_im, axis=0) * forward_scale
        turned_modes = compact8(re, im, a)
        for d in range(2):
            send2[d, :4] = turned_modes[4 * d : 4 * d + 4]
            send2[d, 4:8] = s8[4 * d : 4 * d + 4]
        copy = gather(send2, gat2, 1)
        some(1, count, lambda k: copy(k).start())
        gat2[a] = send2[ch]

    on_reducer(adjoint)

    def store(i):
        at = pl.ds(pl.multiple_of(i * block, block), block)
        return pltpu.make_async_copy(cot_ref.at[:, at, :], partial_ref.at[:, at, :], out_sem)

    def backs(i):
        swap(i).wait_recv()
        for u in range(subs):
            b = i * subs + u
            first = pl.multiple_of(b * RB, RB)
            other_hi, other_low = split2(other_ref[b])
            hi = jnp.concatenate((sl_ref[b, :rows, :], other_hi), axis=0)
            low = jnp.concatenate((sl_ref[b, rows:, :], other_low), axis=0)
            both = mm(kronb_ref[...], hi)
            result = both[:rows] + both[rows:] + mm(kronb_ref[:rows, :], low)
            cot_ref[:, pl.ds(first, RB), :] = result.reshape(own, RB, width)
        store(i).start()

    pairs(0, steps, backs)

    gp_all = gpl.at[pl.ds(1, n - 1)]
    remote(gp_all, gp_all, gp_send, gp_recv, flat).wait_recv()
    gp_ref[...] = gpx[...] + jnp.sum(gpl[pl.ds(1, n - 1)], axis=0)
    gather_wait(gat2, 1)
    spec_ref[...] = gat1[...]
    back_ref[...] = gat2[...]

    scatter_end(x1, landed1, 0)
    scatter_end(x2, landed2, 1)
    gather_end(send1, gat1, 0)
    gather_end(send2, gat2, 1)
    remote(came_all, came_all, trade_send, trade_recv, flat).wait_send()
    remote(gp_all, gp_all, gp_send, gp_recv, flat).wait_send()
    sent = pre_ref.at[pl.ds(0, steps * subs)]
    remote(sent, sent, swap_send, swap_recv.at[0], flat).wait_send()
    pltpu.make_async_copy(cot_ref, partial_ref, out_sem).wait()


def main_pass(args, constants, scales, cap, n_row, n_col):
    field = args[6]
    n = n_row * n_col
    count = 2 * n
    inputs, height, width = field.shape
    own = inputs // 2
    block = 2 * RB
    steps = height // block
    blocks = height // RB
    rows = own * RB
    kept = own + 8
    points = n * cap
    vmem = pl.BlockSpec(memory_space=pltpu.VMEM)
    hbm = pl.BlockSpec(memory_space=pl.ANY)
    dma = pltpu.SemaphoreType.DMA
    rows2, rows3, cols2, wide3 = constants
    return pl.pallas_call(
        functools.partial(main_kernel, n_row, n_col, scales),
        out_shape=[
            jax.ShapeDtypeStruct((own, height, width), F32),
            jax.ShapeDtypeStruct((A, 12, 128), F32),
            jax.ShapeDtypeStruct((A, 8, 128), F32),
            jax.ShapeDtypeStruct((4, 128), F32),
        ],
        in_specs=[vmem] * 6 + [hbm] * 6,
        out_specs=[hbm, vmem, vmem, vmem],
        scratch_shapes=[
            pltpu.VMEM((rows2.shape[0], height), BF16),
            pltpu.VMEM((height, rows3.shape[1]), BF16),
            pltpu.VMEM((width, cols2.shape[1]), BF16),
            pltpu.VMEM((wide3.shape[0], width), BF16),
            dma((4,)),
            pltpu.VMEM((steps, inputs, block, width), F32),
            dma((steps,)),
            pltpu.VMEM((2, inputs, inputs, 128), F32),
            dma,
            pltpu.VMEM((blocks, 2 * inputs * RB, width), BF16),
            pltpu.VMEM((blocks, rows, width), F32),
            pltpu.VMEM((2 * rows, inputs * RB), BF16),
            pltpu.VMEM((2 * rows, inputs * RB), BF16),
            pltpu.VMEM((blocks, rows, 2 * M), F32),
            pltpu.VMEM((A, 4, 128), F32),
            pltpu.VMEM((count, 4, 128), F32),
            pltpu.VMEM((2, 12, 128), F32),
            pltpu.VMEM((A, 12, 128), F32),
            pltpu.VMEM((A, 4, 128), F32),
            pltpu.VMEM((count, 4, 128), F32),
            pltpu.VMEM((2, 8, 128), F32),
            pltpu.VMEM((A, 8, 128), F32),
            dma((2,)),
            dma((2,)),
            dma((2, count)),
            dma((2,)),
            pltpu.VMEM((n, kept, cap), F32),
            pltpu.VMEM((n, kept, cap), F32),
            dma,
            dma,
            pltpu.VMEM((kept, points), F32),
            pltpu.VMEM((points, 128), F32),
            pltpu.VMEM((2, own * FOLD, points), BF16),
            pltpu.VMEM((points, width), BF16),
            pltpu.VMEM((points, width), BF16),
            pltpu.VMEM((own, height, width), F32),
            pltpu.VMEM((own, height, 128), F32),
            pltpu.VMEM((blocks, 2 * rows, width), BF16),
            pltpu.VMEM((blocks, rows, width), F32),
            dma,
            dma((steps,)),
            pltpu.VMEM((2 * inputs * RB, 2 * rows), F32),
            pltpu.VMEM((4, 128), F32),
            pltpu.VMEM((n, 4, 128), F32),
            dma,
            dma,
            dma,
        ],
        compiler_params=pltpu.CompilerParams(
            collective_id=0, has_side_effects=True, vmem_limit_bytes=58 * MIB
        ),
    )(*args, *constants)


def turn_blocks(x):
    group = iota((8, 128), 1) // M
    line = iota((8, 128), 0)
    out = jnp.where(group == line, x, 0.0)
    for d in range(1, 8):
        y = pltpu.roll(pltpu.roll(x, d * M, 1), 8 - d, 0)
        out = jnp.where((group - line + 8) % 8 == d, y, out)
    return out


def back_kernel(
    scales, partial_ref, spec_ref, back_ref, gp_ref, kept_ref, rows3_hbm, wide3_hbm,
    out_ref, gs_ref, point_ref, bias_ref,
    half_ref, spec_t, grad_t, point_t, rows3_ref, wide3_ref, table_sem,
    held, load_sem, made, out_sem, gs_sem,
):
    grad_scale, norm_points, bias_scale = scales
    steps, own, block, width = held.shape
    rows = own * RB
    height = steps * block
    inputs = 2 * own
    each_c = inputs // steps

    def load(i):
        at = pl.ds(pl.multiple_of(i * block, block), block)
        return pltpu.make_async_copy(partial_ref.at[:, at, :], held.at[i], load_sem.at[i])

    def store(i):
        at = pl.ds(pl.multiple_of(i * block, block), block)
        return pltpu.make_async_copy(held.at[i], out_ref.at[:, at, :], out_sem.at[i])

    def store_gs(i):
        at = pl.ds(i * each_c, each_c)
        return pltpu.make_async_copy(made.at[:, at], gs_ref.at[:, at], gs_sem.at[i])

    def each(low, high, body):
        def go(k, carry):
            body(k)
            return carry

        lax.fori_loop(low, high, go, 0)

    row_at = pl.multiple_of(lax.axis_index("row") * height, 128)
    col_at = pl.multiple_of(lax.axis_index("col") * width, 128)
    loads = [
        pltpu.make_async_copy(rows3_hbm.at[pl.ds(row_at, height), :], rows3_ref, table_sem.at[0]),
        pltpu.make_async_copy(wide3_hbm.at[:, pl.ds(col_at, width)], wide3_ref, table_sem.at[1]),
    ]
    for one in loads:
        one.start()
    each(0, steps, lambda i: load(i).start())
    for one in loads:
        one.wait()
    mode_half([back_ref[:, q, :] for q in range(4)], rows3_ref[...], half_ref)

    def fields(i):
        load(i).wait()
        for u in range(block // RB):
            at = slice(u * RB, (u + 1) * RB)
            first = pl.multiple_of(i * block + u * RB, RB)
            half = half_ref[:, pl.ds(first, RB), :].reshape(rows, 128)
            result = from_half(half, wide3_ref).reshape(own, RB, width)
            held[i, :, at, :] = held[i, :, at, :] + result
        store(i).start()

    each(0, steps, fields)
    kept = as_column(kept_ref[...], lax.axis_index("ch") * own, own)
    mode = iota((own, MODES), 1)
    row_mode = mode // M
    rank = jnp.where(row_mode < M, row_mode, A - 1 - row_mode)
    keep = jnp.where((rank < kept) & (mode % M < kept), grad_scale, 0.0)
    biases = jnp.zeros((1, own), F32)
    for part in range(2):
        for octet in range(own // 8):
            j = part * (own // 8) + octet
            for t in range(A // 8):
                lanes = slice(t * 128, (t + 1) * 128)
                lines = slice(octet * 8, octet * 8 + 8)
                got = turn_blocks(back_ref[t * 8 : t * 8 + 8, 4 + j, :])
                if part == 0 and t == 0:
                    shape = (8, own)
                    named = iota(shape, 1) == iota(shape, 0) + octet * 8
                    named = jnp.where(named, got[:, :1] * bias_scale, 0.0)
                    biases = biases + jnp.sum(named, axis=0, keepdims=True)
                grad_t[part, lines, lanes] = got * keep[lines, lanes]
                for side in range(2):
                    at = side * own + octet * 8
                    spec_t[part, at : at + 8, lanes] = turn_blocks(
                        spec_ref[t * 8 : t * 8 + 8, side * 4 + j, :]
                    )

    def spectral(i):
        for u in range(each_c):
            c = i * each_c + u
            spec_re = spec_t[0, pl.ds(c, 1), :]
            spec_im = spec_t[1, pl.ds(c, 1), :]
            made[0, c] = grad_t[0] * spec_re + grad_t[1] * spec_im
            made[1, c] = grad_t[1] * spec_re - grad_t[0] * spec_im
        store_gs(i).start()

    each(0, steps, spectral)
    bias_ref[...] = biases
    gp = gp_ref[...] * norm_points
    into = 128 // own
    for k in range(into):
        for i in range(inputs // into):
            at = i * into + k
            point_t[at : at + 1, :] = gp[i : i + 1, k * own : (k + 1) * own]
    eye = sel(iota((own, own), 0) == iota((own, own), 1))
    point_ref[...] = exact(eye, point_t[...], NT)
    each(0, steps, lambda i: store(i).wait())
    each(0, steps, lambda i: store_gs(i).wait())


def back_pass(partial, spec, back, gp, kept, rows3, wide3, scales):
    own, height, width = partial.shape
    block = 4 * RB
    steps = height // block
    hbm = pl.BlockSpec(memory_space=pl.ANY)
    vmem = pl.BlockSpec(memory_space=pltpu.VMEM)
    dma = pltpu.SemaphoreType.DMA
    return pl.pallas_call(
        functools.partial(back_kernel, scales),
        in_specs=[hbm, vmem, vmem, vmem, vmem, hbm, hbm],
        out_specs=[hbm, hbm, vmem, vmem],
        out_shape=[
            jax.ShapeDtypeStruct((own, height, width), F32),
            jax.ShapeDtypeStruct((2, 2 * own, own, MODES), F32),
            jax.ShapeDtypeStruct((own, 2 * own), F32),
            jax.ShapeDtypeStruct((1, own), F32),
        ],
        scratch_shapes=[
            pltpu.VMEM((own, height, 128), F32),
            pltpu.VMEM((2, 2 * own, MODES), F32),
            pltpu.VMEM((2, own, MODES), F32),
            pltpu.VMEM((2 * own, own), F32),
            pltpu.VMEM((height, rows3.shape[1]), BF16),
            pltpu.VMEM((wide3.shape[0], width), BF16),
            dma((2,)),
            pltpu.VMEM((steps, own, block, width), F32),
            dma((steps,)),
            pltpu.VMEM((2, 2 * own, own, MODES), F32),
            dma((steps,)),
            dma((steps,)),
        ],
        compiler_params=pltpu.CompilerParams(vmem_limit_bytes=58 * MIB),
    )(partial, spec, back, gp, kept, rows3, wide3)


def per_device(
    field, spec_weight, point_weight, bias, kept_modes, residual, trace_dest, trace_cell
):
    n_row = lax.axis_size("row")
    n_col = lax.axis_size("col")
    inputs, height, width = field.shape
    own = inputs // lax.axis_size("ch")
    points = trace_dest.shape[0]
    tiles = n_row * n_col
    points_all = points * tiles
    cap = max(2, 2 * points // tiles)
    forward_scale = 1.0 / math.sqrt(height * n_row * width * n_col)
    mix_scale = 1.0 / math.sqrt(MODES)
    norm_points = 1.0 / math.sqrt(points_all)
    constants = [jnp.asarray(t) for t in tables(height * n_row, width * n_col)]
    kept = kept_modes.reshape(1, inputs)
    args = (
        trace_dest.reshape(1, points), trace_cell.reshape(1, points), residual, kept,
        bias.reshape(1, own), point_weight, field, spec_weight,
    )
    partial, spec, back, gp = main_pass(
        args, constants, (forward_scale, mix_scale), cap, n_row, n_col
    )
    grad_field, grad_spec, grad_point, grad_bias = back_pass(
        partial, spec, back, gp, kept, constants[1], constants[3],
        (math.sqrt(MODES / points_all), norm_points, norm_points / mix_scale),
    )
    return (grad_field, grad_spec, grad_point.T, grad_bias.reshape(own))


def solution(mesh):
    return jax.shard_map(
        per_device,
        mesh=mesh,
        in_specs=(
            P(None, "row", "col"),
            P(),
            P(),
            P("ch"),
            P(),
            P("ch", ("row", "col")),
            P(("row", "col"), None),
            P(("row", "col")),
        ),
        out_specs=(P("ch", "row", "col"), P(None, None, "ch", None), P(None, "ch"), P("ch")),
        check_vma=False,
    )
```
